128 devices in a mesh: row: 16 (over x, y_lo, core), col: 8 (over y_hi, z).
Axes of the slice: x: 4, y: 4 (y_hi: 2, y_lo: 2; y = y_hi * 2 + y_lo), z: 4, core: 2. Of those that a mesh axis runs over, the one named last changes fastest.
Arguments:
- vision_tokens: bfloat16 [2048, 8192], P(('row', 'col')), may hold values from -6 to 6
- image_counts: int32 [64], replicated, may hold values from 1 to 32, 1024 in all
- image_owner: int32 [128], replicated, may hold values from 0 to 127, each once
- gate_weight: bfloat16 [8192, 14336], P('row', 'col'), may hold values from -0.0625 to 0.0625
- up_weight: bfloat16 [8192, 14336], P('row', 'col'), may hold values from -0.0625 to 0.0625
- down_weight: bfloat16 [14336, 8192], P('col', 'row'), may hold values from -0.046875 to 0.046875
- out_grad: bfloat16 [1024, 8192], P('col', 'row'), may hold values from -0.19921875 to 0.19921875
Outputs:
- layer_out: bfloat16 [1024, 8192], P('col', 'row')
- grad_gate: float32 [8192, 14336], P('row', 'col')
- grad_up: float32 [8192, 14336], P('row', 'col')
- grad_down: float32 [14336, 8192], P('col', 'row')
The draws below stay inside these ranges and needn't reach their ends.
Inputs may be any that keep to these rules, and one draw needn't show every extreme that they name: `image_counts`: every image has 1 to 32 tokens, together 1024; some image has exactly 32. `image_owner`: each encoder device, numbered row index * 8 + col index, appears once; so every device holds at most 16 tokens, and one holds exactly 16.
All inputs are finite; a program needn't handle non-finite values.
Results may differ from the reference program's by a relative error of at most 0.0049.
Values may be sent and summed in bfloat16 or wider, within the bound.
A program may use at most 128 MiB of HBM per device.

```python
import math
import jax
import jax.numpy as jnp
import numpy as np

D = 8192
FF = 14336
IMG_TOK = 16
ENCODERS = 128
IMAGES = 64
TOKENS = 1024
MOST = 32


def levels(key, shape, split, low, top_value):
    loudness, own = 1.0, jax.random.fold_in(key, 6)
    for dim, shards_of in split:
        draws = jnp.exp(jax.random.uniform(jax.random.fold_in(own, dim), (shards_of,), jnp.float32, low / len(split), top_value / len(split)))
        loudness = loudness * jnp.repeat(draws, shape[dim] // shards_of).reshape([-1 if axis == dim else 1 for axis in range(len(shape))])
    return loudness


def split_up(amount, total, most, skew):
    weights = [(1 << 20) // math.isqrt(grade ** skew) + 1 for grade in range(2, amount + 1)]
    rest, holding = total - most - (amount - 1), [1] * (amount - 1)
    while rest > 0:
        free = [i for i in range(amount - 1) if holding[i] < most]
        pool, left = sum([weights[i] for i in free]), rest
        for i in free:
            more = min(most - holding[i], max(1, left * weights[i] // pool), rest)
            holding[i] = holding[i] + more
            rest = rest - more
    return np.array([most] + holding)


def ragged(own_key, number_of, total, reach, lean):
    if number_of == 2:
        one = jax.random.randint(own_key, (), max(1, total - reach), min(reach, total - 1) + 1)
        return jnp.stack([one, total - one])
    tallies = jnp.asarray(split_up(number_of, total, reach, lean), jnp.int32)
    twos = (number_of - 1) // 2
    giver, taker = tallies[1:1 + 2 * twos:2], tallies[2:2 + 2 * twos:2]
    slack = jnp.minimum(giver - 1, reach - taker)
    passed = jax.random.randint(jax.random.fold_in(own_key, 1), (twos,), 0, 1 << 20) % (slack + 1)
    tallies = tallies.at[1:1 + 2 * twos:2].set(giver - passed).at[2:2 + 2 * twos:2].set(taker + passed)
    return tallies[jax.random.permutation(jax.random.fold_in(own_key, 2), number_of)]


def bell_draw(own_key, shape, scale, bound, cuts=(), kind=jnp.bfloat16):
    array = jax.random.normal(own_key, shape, jnp.float32) * scale
    if len(cuts) > 0:
        array = levels(own_key, shape, cuts, -0.22, 0.18) * array
    return jnp.clip(array, min=-bound, max=bound).astype(kind)


def setup_inputs(seed: int = 0) -> dict:
    splits = jax.random.split(jax.random.key(seed), 8)
    return {
        "vision_tokens": bell_draw(splits[0], (ENCODERS * IMG_TOK, D), 1.0, 6.0, ((0, 128),)),
        "image_counts": ragged(splits[1], IMAGES, TOKENS, MOST, 1).astype(jnp.int32),
        "image_owner": jax.random.permutation(splits[2], ENCODERS).astype(jnp.int32),
        "gate_weight": bell_draw(splits[3], (D, FF), D ** -0.5, 0.0625, ((0, 16), (1, 8))),
        "up_weight": bell_draw(splits[4], (D, FF), D ** -0.5, 0.0625, ((0, 16), (1, 8))),
        "down_weight": bell_draw(splits[5], (FF, D), FF ** -0.5, 0.046875, ((0, 8), (1, 16))),
        "out_grad": bell_draw(splits[6], (TOKENS, D), 0.03, 0.19921875, ((0, 8), (1, 16))),
    }


def token_place(image_counts, image_owner, total):
    position = jnp.arange(total, dtype=jnp.int32)
    ends = jnp.cumsum(image_counts).astype(jnp.int32)
    starts = (ends - image_counts).astype(jnp.int32)
    member = ((position[:, None] >= starts[None, :]) & (position[:, None] < ends[None, :])).astype(jnp.int32)
    count = jnp.sum(member * image_counts[None, :], axis=1).astype(jnp.int32)
    begin = jnp.sum(member * starts[None, :], axis=1).astype(jnp.int32)
    owner_first = jnp.sum(member * image_owner[0::2][None, :], axis=1).astype(jnp.int32)
    owner_second = jnp.sum(member * image_owner[1::2][None, :], axis=1).astype(jnp.int32)
    first = (count + 1) // 2
    within = position - begin
    second = (within >= first).astype(jnp.int32)
    slot = (within - second * first).astype(jnp.int32)
    owner = jnp.where(second > 0, owner_second, owner_first).astype(jnp.int32)
    return owner, slot


def pair_grads(gate, up, hidden_grad):
    sigma = jax.nn.sigmoid(gate)
    gate_grad = hidden_grad * up * sigma * (1.0 + gate * (1.0 - sigma))
    up_grad = hidden_grad * gate * sigma
    return jnp.concatenate((gate_grad, up_grad), axis=1).astype(jnp.bfloat16)


def reference(vision_tokens, image_counts, image_owner, gate_weight, up_weight, down_weight, out_grad):
    owner, slot = token_place(image_counts, image_owner, TOKENS)
    token_rows = (owner * IMG_TOK + slot).astype(jnp.int32)
    inputs = jnp.take(vision_tokens, token_rows, axis=0)
    gate_up = jnp.dot(inputs, jnp.concatenate((gate_weight, up_weight), axis=1), preferred_element_type=jnp.float32)
    gate = gate_up[:, :FF]
    up = gate_up[:, FF:]
    hidden = (gate * jax.nn.sigmoid(gate) * up).astype(jnp.bfloat16)
    layer_out = jnp.dot(hidden, down_weight, preferred_element_type=jnp.float32).astype(jnp.bfloat16)
    hidden_grad = jnp.dot(out_grad, down_weight.T, preferred_element_type=jnp.float32)
    pre_grads = pair_grads(gate, up, hidden_grad)
    grad_down = jnp.dot(hidden.T, out_grad, preferred_element_type=jnp.float32)
    both = jnp.dot(inputs.T, pre_grads, preferred_element_type=jnp.float32)
    return layer_out, both[:, :FF], both[:, FF:], grad_down
```

```python
import functools
import jax
import jax.numpy as jnp
from jax import lax
from jax.experimental import pallas as pl
from jax.experimental.pallas import tpu as pltpu
from jax.sharding import PartitionSpec as P

BF = jnp.bfloat16
F32 = jnp.float32
MESH = pl.DeviceIdType.MESH

CHUNKS = 8
HALF = 896
XW = 512
YW = HALF - XW

XD, XR, X2, XY, YY, YD, YR, Y2 = range(8)
AXY, AXP, AXM, AXF, AYP, AYM, AYF, AYY, CORE, Z1, Z2, Z3, YH = range(8, 21)
KINDS = 21


def token_place(image_counts, image_owner, total):
    position = jnp.arange(total, dtype=jnp.int32)
    ends = jnp.cumsum(image_counts)
    starts = ends - image_counts
    member = ((position[:, None] >= starts[None, :]) & (position[:, None] < ends[None, :])).astype(
        jnp.int32
    )
    count = jnp.sum(member * image_counts[None, :], axis=1)
    begin = jnp.sum(member * starts[None, :], axis=1)
    owner_first = jnp.sum(member * image_owner[0::2][None, :], axis=1)
    owner_second = jnp.sum(member * image_owner[1::2][None, :], axis=1)
    first = (count + 1) // 2
    within = position - begin
    second = (within >= first).astype(jnp.int32)
    slot = within - second * first
    owner = jnp.where(second > 0, owner_second, owner_first)
    return (owner, slot)


def rem(a, n):
    return lax.rem(a, n)


def main_kernel(
    x_ref, c_ref, wg_ref, wu_ref, wd_ref, wdo_ref,
    out_ref, o_ref,
    act, px, py,
    sxd, sxr, sx2, sxy, syy, syd, syr, sy2,
    rxd, rxr, rx2, rxy, ryy, ryd, ryr, ry2,
    lo, zs, rz, rh,
    ssem, rsem, osem,
):
    row = lax.axis_index("row")
    col = lax.axis_index("col")
    x, y, k = row // 4, rem(row // 2, 2), rem(row, 2)
    yh, z = col // 4, rem(col, 4)
    yo, ko, ho = 1 - y, 1 - k, 1 - yh

    def at_row(xx, yy, kk):
        return {"row": xx * 4 + yy * 2 + kk}

    def at_col(hh, zz):
        return {"col": hh * 4 + zz}

    far = rem(x + 2, 4)
    y_dev = at_row(x, yo, k)
    core_dev = at_row(x, y, ko)
    partners = [
        core_dev, y_dev, at_row(rem(x + 1, 4), y, k), at_row(rem(x + 3, 4), y, k),
        at_col(yh, rem(z + 1, 4)), at_col(yh, rem(z + 2, 4)), at_col(yh, rem(z + 3, 4)),
        at_col(ho, z),
    ]
    barrier = pltpu.get_barrier_semaphore()
    for dev in partners:
        pl.semaphore_signal(barrier, inc=1, device_id=dev, device_id_type=MESH)
    pl.semaphore_wait(barrier, len(partners))

    cx = pl.ds(pl.multiple_of(k * HALF, 128), XW)
    cy = pl.ds(pl.multiple_of(k * HALF + XW, 128), YW)
    cc = pl.ds(pl.multiple_of(k * HALF, 128), HALF)
    cp = pl.ds(pl.multiple_of(ko * HALF, 128), HALF)

    def copy(kind, t, src, dst, dev):
        return pltpu.make_async_remote_copy(
            src_ref=src, dst_ref=dst, send_sem=ssem.at[kind, t], recv_sem=rsem.at[kind, t],
            device_id=dev, device_id_type=MESH,
        )

    def sides(t):
        s = 1 - 2 * rem(t, 2)
        return rem(x + s + 4, 4), rem(x - s + 4, 4)

    def sends(t):
        ahead, back = sides(t)
        to_ahead, to_back = at_row(ahead, y, k), at_row(back, y, k)
        c = functools.partial
        return {
            XD: c(copy, XD, t, sxd.at[t], rxd.at[t], to_ahead),
            XR: c(copy, XR, t, sxr.at[t], rxr.at[t], to_back),
            X2: c(copy, X2, t, sx2.at[t], rx2.at[t], to_back),
            XY: c(copy, XY, t, sxy.at[t], rxy.at[t], y_dev),
            YY: c(copy, YY, t, syy.at[t], ryy.at[t], y_dev),
            YD: c(copy, YD, t, syd.at[t], ryd.at[t], to_ahead),
            YR: c(copy, YR, t, syr.at[t], ryr.at[t], to_back),
            Y2: c(copy, Y2, t, sy2.at[t], ry2.at[t], to_back),
            AXY: lambda: both(AXY, t, act.at[t, x, y, :, :, cx], y_dev),
            AXP: lambda: both(AXP, t, act.at[t, x, :, :, :, cx], to_ahead),
            AXM: lambda: both(AXM, t, act.at[t, x, :, :, :, cx], to_back),
            AXF: lambda: both(AXF, t, act.at[t, back, :, :, :, cx], to_ahead),
            AYP: lambda: both(AYP, t, act.at[t, x, y, :, :, cy], to_ahead),
            AYM: lambda: both(AYM, t, act.at[t, x, y, :, :, cy], to_back),
            AYF: lambda: both(AYF, t, act.at[t, back, y, :, :, cy], to_ahead),
            AYY: lambda: both(AYY, t, act.at[t, :, y, :, :, cy], y_dev),
            CORE: lambda: both(CORE, t, act.at[t, :, :, :, :, cc], core_dev),
            Z1: lambda: copy(Z1, t, lo.at[t, :, rem(z + 1, 4)], rz.at[t, 0], at_col(yh, rem(z + 1, 4))),
            Z2: lambda: copy(Z2, t, lo.at[t, :, rem(z + 2, 4)], rz.at[t, 1], at_col(yh, rem(z + 2, 4))),
            Z3: lambda: copy(Z3, t, lo.at[t, :, rem(z + 3, 4)], rz.at[t, 2], at_col(yh, rem(z + 3, 4))),
            YH: lambda: copy(YH, t, zs.at[t, ho], rh.at[t], at_col(ho, z)),
        }

    def both(kind, t, ref, dev):
        return copy(kind, t, ref, ref, dev)

    def landed(kind, t):
        ahead, back = sides(t)
        place = {
            XD: lambda: rxd.at[t], XR: lambda: rxr.at[t], X2: lambda: rx2.at[t], XY: lambda: rxy.at[t],
            YY: lambda: ryy.at[t], YD: lambda: ryd.at[t], YR: lambda: ryr.at[t], Y2: lambda: ry2.at[t],
            AXY: lambda: act.at[t, x, yo, :, :, cx],
            AXP: lambda: act.at[t, back, :, :, :, cx],
            AXM: lambda: act.at[t, ahead, :, :, :, cx],
            AXF: lambda: act.at[t, far, :, :, :, cx],
            AYP: lambda: act.at[t, back, y, :, :, cy],
            AYM: lambda: act.at[t, ahead, y, :, :, cy],
            AYF: lambda: act.at[t, far, y, :, :, cy],
            AYY: lambda: act.at[t, :, yo, :, :, cy],
            CORE: lambda: act.at[t, :, :, :, :, cp],
            Z1: lambda: rz.at[t, 0], Z2: lambda: rz.at[t, 1], Z3: lambda: rz.at[t, 2],
            YH: lambda: rh.at[t],
        }[kind]()
        return copy(kind, t, place, place, y_dev)

    def start(t, *kinds):
        table = sends(t)
        for kind in kinds:
            table[kind]().start()

    def arrive(t, *kinds):
        for kind in kinds:
            landed(kind, t).wait_recv()

    def s0(t):
        b = rem(t, 4)
        ahead, _ = sides(t)
        x_t = x_ref[pl.ds(pl.multiple_of(t * 128, 128), 128), :]
        c_t = c_ref[:, pl.ds(pl.multiple_of(t * 16, 16), 16), :].reshape(128, 1024)
        for m in range(3):
            if m == 0:
                g = jnp.dot(x_t, wg_ref[...], preferred_element_type=F32)
            elif m == 1:
                g = jnp.dot(x_t, wu_ref[...], preferred_element_type=F32)
            else:
                g = lax.dot_general(c_t, wd_ref[...], (((1,), (1,)), ((), ())), preferred_element_type=F32)
            px[b, :, m] = g[:, :XW].reshape(4, 32, XW)
            gy = g[:, XW:].reshape(4, 2, 16, YW)
            for yy in range(2):
                py[b, yy, :, m] = gy[:, yy]
        sxd[t] = px[b, ahead].astype(BF)
        sxr[t] = px[b, far].astype(BF)
        start(t, XD, XR)
        syy[t] = py[b, yo].astype(BF)
        start(t, YY)

    def s1(t):
        b = rem(t, 4)
        ahead, back = sides(t)
        arrive(t, XR)
        sx2[t] = (px[b, back] + rxr[t].astype(F32)).astype(BF)
        start(t, X2)
        arrive(t, YY)
        py[b, y] = py[b, y] + ryy[t].astype(F32)
        syd[t] = py[b, y, ahead].astype(BF)
        syr[t] = py[b, y, far].astype(BF)
        start(t, YD, YR)

    def s2(t):
        b = rem(t, 4)
        _, back = sides(t)
        arrive(t, XD, X2)
        px[b, x] = px[b, x] + rxd[t].astype(F32) + rx2[t].astype(F32)
        sxy[t] = px[b, x, :, pl.ds(pl.multiple_of(yo * 16, 16), 16), :].astype(BF)
        start(t, XY)
        arrive(t, YR)
        sy2[t] = (py[b, y, back] + ryr[t].astype(F32)).astype(BF)
        start(t, Y2)

    def activate(t, full, cols):
        gate, up, hg = full[0], full[1], full[2]
        sigma = jax.nn.sigmoid(gate)
        act[t, x, y, 0, :, cols] = (gate * sigma * up).astype(BF)
        act[t, x, y, 1, :, cols] = (hg * up * sigma * (1.0 + gate * (1.0 - sigma))).astype(BF)
        act[t, x, y, 2, :, cols] = (hg * gate * sigma).astype(BF)

    def s3(t):
        b = rem(t, 4)
        arrive(t, XY)
        activate(t, px[b, x, :, pl.ds(pl.multiple_of(y * 16, 16), 16), :] + rxy[t].astype(F32), cx)
        start(t, AXY)
        arrive(t, YD, Y2)
        activate(t, py[b, y, x] + ryd[t].astype(F32) + ry2[t].astype(F32), cy)
        start(t, AYP, AYM)

    def s4(t):
        arrive(t, AXY)
        start(t, AXP, AXM)
        arrive(t, AYP)
        start(t, AYF)
        arrive(t, AYM)

    def s5(t):
        arrive(t, AXP)
        start(t, AXF)
        arrive(t, AXM)
        arrive(t, AYF)
        start(t, AYY)

    def s6(t):
        arrive(t, AXF, AYY)
        start(t, CORE)

    def s7(t):
        arrive(t, CORE)
        pltpu.make_async_copy(act.at[t], o_ref.at[t], osem.at[t]).start()
        hidden = act[t, :, :, 0].reshape(128, 2 * HALF)
        part = jnp.dot(hidden, wdo_ref[...], preferred_element_type=F32)
        lo[t] = part.reshape(2, 4, 16, 512)
        start(t, Z1, Z2, Z3)

    def s8(t):
        arrive(t, Z1, Z2, Z3)
        zs[t] = lo[t, :, z] + rz[t, 0] + rz[t, 1] + rz[t, 2]
        start(t, YH)

    def s9(t):
        arrive(t, YH)
        out_ref[pl.ds(pl.multiple_of(t * 16, 16), 16), :] = (zs[t, yh] + rh[t]).astype(BF)

    stages = [s0, s1, s2, s3, s4, s5, s6, s7, s8, s9]

    def step(n, carry):
        for lag, stage in enumerate(stages):
            t = n - lag

            @pl.when((t >= 0) & (t < CHUNKS))
            def _():
                stage(t)

        return carry

    lax.fori_loop(0, CHUNKS + len(stages) - 1, step, 0)

    def finish(t, carry):
        table = sends(t)
        for kind in range(KINDS):
            table[kind]().wait_send()
        pltpu.make_async_copy(act.at[t], o_ref.at[t], osem.at[t]).wait()
        return carry

    lax.fori_loop(0, CHUNKS, finish, 0)


def main_call(x, c, wg, wu, wd, wdo):
    n = CHUNKS
    vm = lambda *s: pltpu.VMEM(s, BF)
    vf = lambda *s: pltpu.VMEM(s, F32)
    xb, xq, yb = (n, 3, 32, XW), (n, 3, 16, XW), (n, 3, 16, YW)
    moves = [vm(*xb), vm(*xb), vm(*xb), vm(*xq), vm(n, 4, 3, 16, YW), vm(*yb), vm(*yb), vm(*yb)]
    return pl.pallas_call(
        main_kernel,
        out_shape=(
            jax.ShapeDtypeStruct((128, 512), BF),
            jax.ShapeDtypeStruct((n, 4, 2, 3, 16, 2 * HALF), BF),
        ),
        in_specs=[pl.BlockSpec(memory_space=pltpu.VMEM)] * 6,
        out_specs=(pl.BlockSpec(memory_space=pltpu.VMEM), pl.BlockSpec(memory_space=pl.ANY)),
        scratch_shapes=[
            vm(n, 4, 2, 3, 16, 2 * HALF), vf(4, 4, 3, 32, XW), vf(4, 2, 4, 3, 16, YW),
            *moves, *moves,
            vf(n, 2, 4, 16, 512), vf(n, 2, 16, 512), vf(n, 3, 2, 16, 512), vf(n, 16, 512),
            pltpu.SemaphoreType.DMA((KINDS, n)), pltpu.SemaphoreType.DMA((KINDS, n)),
            pltpu.SemaphoreType.DMA((n,)),
        ],
        compiler_params=pltpu.CompilerParams(
            collective_id=0, has_side_effects=True, vmem_limit_bytes=58 << 20
        ),
        cost_estimate=pl.CostEstimate(flops=8 * 10**9, bytes_accessed=30 * 10**6, transcendentals=0),
        name="row_sums",
    )(x, c, wg, wu, wd, wdo)


def grads_kernel(x_ref, c_ref, h_ref, gg_ref, ug_ref, gate_ref, up_ref, down_ref, xt, cs):
    @pl.when(pl.program_id(0) == 0)
    def _():
        xt[...] = x_ref[...].T
        for t in range(CHUNKS):
            cs[pl.ds(t * 128, 128), :] = c_ref[:, t].reshape(128, 512)

    width = h_ref.shape[-1]
    gate_ref[...] = jnp.dot(xt[...], gg_ref[...].reshape(1024, width), preferred_element_type=F32)
    up_ref[...] = jnp.dot(xt[...], ug_ref[...].reshape(1024, width), preferred_element_type=F32)
    down_ref[...] = lax.dot_general(
        h_ref[...].reshape(1024, width), cs[...], (((0,), (0,)), ((), ())), preferred_element_type=F32
    )


def grads_call(x, c, o):
    width = 256
    n = CHUNKS
    part = lambda m: pl.BlockSpec((n, 4, 2, 1, 16, width), lambda j: (0, 0, 0, m, 0, j))
    return pl.pallas_call(
        grads_kernel,
        grid=(1792 // width,),
        out_shape=(
            jax.ShapeDtypeStruct((512, 1792), F32),
            jax.ShapeDtypeStruct((512, 1792), F32),
            jax.ShapeDtypeStruct((1792, 512), F32),
        ),
        in_specs=[
            pl.BlockSpec((1024, 512), lambda j: (0, 0)),
            pl.BlockSpec((8, n, 16, 512), lambda j: (0, 0, 0, 0)),
            part(0), part(1), part(2),
        ],
        out_specs=(
            pl.BlockSpec((512, width), lambda j: (0, j)),
            pl.BlockSpec((512, width), lambda j: (0, j)),
            pl.BlockSpec((width, 512), lambda j: (j, 0)),
        ),
        scratch_shapes=[pltpu.VMEM((512, 1024), BF), pltpu.VMEM((1024, 512), BF)],
        compiler_params=pltpu.CompilerParams(vmem_limit_bytes=40 << 20),
        cost_estimate=pl.CostEstimate(flops=6 * 10**9, bytes_accessed=24 * 10**6, transcendentals=0),
        name="weight_grads",
    )(x, c, o, o, o)


def local(vision_tokens, image_counts, image_owner, gate_weight, up_weight, down_weight, out_grad):
    slots = vision_tokens.shape[0]
    row_count = lax.axis_size("row")
    col_count = lax.axis_size("col")
    token_total = out_grad.shape[0] * col_count
    owner, slot = token_place(image_counts, image_owner, token_total)
    owner_row = owner // col_count
    owner_col = owner % col_count
    core = lax.axis_index("row") % 2
    swap = [(i, i ^ 1) for i in range(row_count)]

    def other(a):
        return lax.ppermute(a, "row", swap)

    def halves(w, axis):
        mine = lax.dynamic_slice_in_dim(w, core * HALF, HALF, axis)
        theirs = lax.dynamic_slice_in_dim(w, (1 - core) * HALF, HALF, axis)
        return jnp.concatenate((mine, other(theirs)), axis=1 - axis)

    wg, wu, wd = halves(gate_weight, 1), halves(up_weight, 1), halves(down_weight, 0)
    received = lax.all_to_all(vision_tokens, "row", split_axis=1, concat_axis=0, tiled=True)
    pooled, cotangent = (
        lax.all_gather(received, "col", axis=0, tiled=True),
        lax.all_gather(out_grad, "col", axis=0, tiled=True),
    )
    pool_index = owner_col * (row_count * slots) + owner_row * slots + slot
    pool_index = pool_index.reshape(8, CHUNKS, 16).transpose(1, 0, 2).reshape(token_total)
    inputs = jnp.take(pooled, pool_index, axis=0)
    x2 = jnp.concatenate((inputs, other(inputs)), axis=1)
    c2 = jnp.concatenate((cotangent, other(cotangent)), axis=1).reshape(8, 128, 1024)
    layer_out, o = main_call(x2, c2, wg, wu, wd, down_weight)
    grad_gate, grad_up, grad_down = grads_call(inputs, cotangent.reshape(8, CHUNKS, 16, 512), o)
    return (layer_out, grad_gate, grad_up, grad_down)


def solution(mesh):
    in_specs = (
        P(("row", "col"), None),
        P(),
        P(),
        P("row", "col"),
        P("row", "col"),
        P("col", "row"),
        P("col", "row"),
    )
    out_specs = (P("col", "row"), P("row", "col"), P("row", "col"), P("col", "row"))
    return jax.shard_map(local, mesh=mesh, in_specs=in_specs, out_specs=out_specs, check_vma=False)
```

```python
import functools
import jax
import jax.numpy as jnp
from jax import lax
from jax.experimental import pallas as pl
from jax.experimental.pallas import tpu as pltpu
from jax.sharding import PartitionSpec as P

BF = jnp.bfloat16
F32 = jnp.float32
MESH = pl.DeviceIdType.MESH

CHUNKS = 8
HALF = 896
XW = 512
YW = HALF - XW

XD, XR, X2, XY, YY, YD, YR, Y2 = range(8)
HG = 8
AXY, AXP, AXM, AXF, AYP, AYM, AYF, AYY, CORE, XIN, CIN, LOZ = range(16, 28)
KINDS = 28
CP, CM, CY, CF1, CF2, DP, DM, DF1, DF2 = range(9)
VY, VP, VM, WP, WM, VF1, VF2, VH, WF1, WF2 = range(9, 19)
WG, WU, WD, LOY = range(19, 23)
ONCE = 23
FIRST = 7
VR = 12

def token_place(image_counts, image_owner, total):
    position = jnp.arange(total, dtype=jnp.int32)
    ends = jnp.cumsum(image_counts)
    starts = ends - image_counts
    member = ((position[:, None] >= starts[None, :]) & (position[:, None] < ends[None, :])).astype(
        jnp.int32
    )
    count = jnp.sum(member * image_counts[None, :], axis=1)
    begin = jnp.sum(member * starts[None, :], axis=1)
    owner_first = jnp.sum(member * image_owner[0::2][None, :], axis=1)
    owner_second = jnp.sum(member * image_owner[1::2][None, :], axis=1)
    first = (count + 1) // 2
    within = position - begin
    second = (within >= first).astype(jnp.int32)
    slot = within - second * first
    owner = jnp.where(second > 0, owner_second, owner_first)
    return (owner, slot)


def rem(a, n):
    return lax.rem(a, n)


class RowSum:
    def __init__(self, base, refs):
        self.base = base
        (self.px, self.py, self.sxd, self.sxr, self.sx2, self.sxy, self.syy, self.syd, self.syr,
         self.sy2, self.rxd, self.rxr, self.rx2, self.rxy, self.ryy, self.ryd, self.ryr, self.ry2) = refs


def main_kernel(
    v_ref, pos_ref, og_ref, gate_hbm, up_hbm, down_hbm,
    out_ref, o_ref, xo_ref, co_ref,
    act, pool, xin, c2, wg, wu, wd, wdo,
    hfx, hfy, lo, rz, zs, rh,
    *rest,
):
    gu, hg = RowSum(0, rest[:18]), RowSum(HG, rest[18:36])
    ssem, rsem, ssem1, rsem1, sa, ra, osem, lsem = rest[36:]
    row = lax.axis_index("row")
    col = lax.axis_index("col")
    x, y, k = row // 4, rem(row // 2, 2), rem(row, 2)
    yh, z = col // 4, rem(col, 4)
    yo, ko, ho = 1 - y, 1 - k, 1 - yh
    far = rem(x + 2, 4)
    zp, zm, zf = rem(z + 1, 4), rem(z + 3, 4), rem(z + 2, 4)

    def at_row(xx, yy, kk):
        return {"row": xx * 4 + yy * 2 + kk}

    def at_col(hh, zz):
        return {"col": hh * 4 + zz}

    y_dev, core_dev = at_row(x, yo, k), at_row(x, y, ko)
    up_dev, down_dev, hi_dev = at_col(yh, zp), at_col(yh, zm), at_col(ho, z)
    barrier = pltpu.get_barrier_semaphore()

    def greet(i, carry):
        pl.semaphore_signal(barrier, inc=1, device_id={"row": rem(row + i, 16)}, device_id_type=MESH)
        return carry

    lax.fori_loop(1, 16, greet, 0)
    for dev in (up_dev, down_dev, at_col(yh, zf), hi_dev):
        pl.semaphore_signal(barrier, inc=1, device_id=dev, device_id_type=MESH)

    mine = pl.ds(pl.multiple_of(k * HALF, 128), HALF)
    theirs = pl.ds(pl.multiple_of(ko * HALF, 128), HALF)
    here = [
        pltpu.make_async_copy(down_hbm.at[mine, :], wd.at[:, 0:512], lsem.at[0]),
        pltpu.make_async_copy(gate_hbm.at[:, mine], wg.at[0:512, :], lsem.at[1]),
        pltpu.make_async_copy(up_hbm.at[:, mine], wu.at[0:512, :], lsem.at[2]),
        pltpu.make_async_copy(down_hbm, wdo, lsem.at[3]),
    ]
    here[0].start()
    c2[col, :, 0:512] = og_ref[...]
    pool[yh, z, row] = v_ref[:, pl.ds(pl.multiple_of(row * 512, 512), 512)]
    pl.semaphore_wait(barrier, 19)

    cx = pl.ds(pl.multiple_of(k * HALF, 128), XW)
    cy = pl.ds(pl.multiple_of(k * HALF + XW, 128), YW)

    def copy(kind, t, src, dst, dev):
        return pltpu.make_async_remote_copy(
            src_ref=src, dst_ref=dst, send_sem=ssem.at[kind, t], recv_sem=rsem.at[kind, t],
            device_id=dev, device_id_type=MESH,
        )

    def once(kind, src, dst, dev):
        return pltpu.make_async_remote_copy(
            src_ref=src, dst_ref=dst, send_sem=ssem1.at[kind], recv_sem=rsem1.at[kind],
            device_id=dev, device_id_type=MESH,
        )

    def same(ref):
        return ref, ref

    def cblk(hh, zz, lo_=0, n=128):
        return c2.at[hh * 4 + zz, lo_:lo_ + n, 0:512]

    single = {
        WD: lambda: (down_hbm.at[theirs, :], wd.at[:, 512:1024], core_dev, wd.at[:, 512:1024]),
        WG: lambda: (gate_hbm.at[:, theirs], wg.at[512:1024, :], core_dev, wg.at[512:1024, :]),
        WU: lambda: (up_hbm.at[:, theirs], wu.at[512:1024, :], core_dev, wu.at[512:1024, :]),
        CP: lambda: (*same(cblk(yh, z)), up_dev, cblk(yh, zm)),
        CM: lambda: (*same(cblk(yh, z)), down_dev, cblk(yh, zp)),
        CY: lambda: (*same(cblk(yh, z)), hi_dev, cblk(ho, z)),
        CF1: lambda: (*same(cblk(yh, zm, 0, 64)), up_dev, cblk(yh, zf, 0, 64)),
        CF2: lambda: (*same(cblk(yh, zp, 64, 64)), down_dev, cblk(yh, zf, 64, 64)),
        DP: lambda: (*same(cblk(ho, z)), up_dev, cblk(ho, zm)),
        DM: lambda: (*same(cblk(ho, z)), down_dev, cblk(ho, zp)),
        DF1: lambda: (*same(cblk(ho, zm, 0, 64)), up_dev, cblk(ho, zf, 0, 64)),
        DF2: lambda: (*same(cblk(ho, zp, 64, 64)), down_dev, cblk(ho, zf, 64, 64)),
        VY: lambda: (*same(pool.at[yh, z, 0:VR]), hi_dev, pool.at[ho, z, 0:VR]),
        VP: lambda: (*same(pool.at[yh, z, VR:16]), up_dev, pool.at[yh, zm, VR:16]),
        VM: lambda: (*same(pool.at[yh, z, VR:16]), down_dev, pool.at[yh, zp, VR:16]),
        VF1: lambda: (*same(pool.at[yh, zm, VR:VR + 2]), up_dev, pool.at[yh, zf, VR:VR + 2]),
        VF2: lambda: (*same(pool.at[yh, zp, VR + 2:16]), down_dev, pool.at[yh, zf, VR + 2:16]),
        VH: lambda: (*same(pool.at[yh, :, VR:16]), hi_dev, pool.at[ho, :, VR:16]),
        WP: lambda: (*same(pool.at[:, z, 0:VR]), up_dev, pool.at[:, zm, 0:VR]),
        WM: lambda: (*same(pool.at[:, z, 0:VR]), down_dev, pool.at[:, zp, 0:VR]),
        WF1: lambda: (*same(pool.at[:, zm, 0:VR // 2]), up_dev, pool.at[:, zf, 0:VR // 2]),
        WF2: lambda: (*same(pool.at[:, zp, VR // 2:VR]), down_dev, pool.at[:, zf, VR // 2:VR]),
        LOY: lambda: (zs, rh, hi_dev, rh),
    }

    def start1(*kinds):
        for kind in kinds:
            src, dst, dev, _ = single[kind]()
            once(kind, src, dst, dev).start()

    def arrive1(*kinds):
        for kind in kinds:
            place = single[kind]()[3]
            once(kind, place, place, y_dev).wait_recv()

    def sides(t):
        s = 1 - 2 * rem(t, 2)
        return rem(x + s + 4, 4), rem(x - s + 4, 4)

    def tok(t):
        return rem(yh + 1 + t // 4, 2) * 4 + rem(z + 1 + rem(t, 4), 4)

    def tokh(u):
        w = rem(u, 4)
        return rem(yh + u // 4, 2) * 4 + rem(z + w + (w // 2) * (5 - 2 * w), 4)

    def table(kind, t):
        ahead, back = sides(t)
        to_ahead, to_back = at_row(ahead, y, k), at_row(back, y, k)
        if kind < 16:
            r = gu if kind < HG else hg
            src, dst, dev = {
                XD: lambda: (r.sxd, r.rxd, to_ahead), XR: lambda: (r.sxr, r.rxr, to_back),
                X2: lambda: (r.sx2, r.rx2, to_back), XY: lambda: (r.sxy, r.rxy, y_dev),
                YY: lambda: (r.syy, r.ryy, y_dev), YD: lambda: (r.syd, r.ryd, to_ahead),
                YR: lambda: (r.syr, r.ryr, to_back), Y2: lambda: (r.sy2, r.ry2, to_back),
            }[kind % HG]()
            return src.at[t], dst.at[t], dev, dst.at[t]
        if kind == CIN:
            c = tokh(t)
            return c2.at[c, :, 0:512], c2.at[c, :, 512:1024], core_dev, c2.at[c, :, 512:1024]
        c = tok(t)
        return {
            AXY: lambda: (*same(act.at[c, x, y, :, :, cx]), y_dev, act.at[c, x, yo, :, :, cx]),
            AXP: lambda: (*same(act.at[c, x, :, :, :, cx]), to_ahead, act.at[c, back, :, :, :, cx]),
            AXM: lambda: (*same(act.at[c, x, :, :, :, cx]), to_back, act.at[c, ahead, :, :, :, cx]),
            AXF: lambda: (*same(act.at[c, back, :, :, :, cx]), to_ahead, act.at[c, far, :, :, :, cx]),
            AYP: lambda: (*same(act.at[c, x, y, :, :, cy]), to_ahead, act.at[c, back, y, :, :, cy]),
            AYM: lambda: (*same(act.at[c, x, y, :, :, cy]), to_back, act.at[c, ahead, y, :, :, cy]),
            AYF: lambda: (*same(act.at[c, back, y, :, :, cy]), to_ahead, act.at[c, far, y, :, :, cy]),
            AYY: lambda: (*same(act.at[c, :, y, :, :, cy]), y_dev, act.at[c, :, yo, :, :, cy]),
            CORE: lambda: (*same(act.at[c, :, :, :, :, mine]), core_dev, act.at[c, :, :, :, :, theirs]),
            XIN: lambda: (xin.at[c, :, 0:512], xin.at[c, :, 512:1024], core_dev, xin.at[c, :, 512:1024]),
            LOZ: lambda: (lo.at[t], rz.at[t], at_col(yh, rem(c, 4)), rz.at[t]),
        }[kind]()

    def start(t, *kinds):
        for kind in kinds:
            src, dst, dev, _ = table(kind, t)
            copy(kind, t, src, dst, dev).start()

    def arrive(t, *kinds):
        for kind in kinds:
            place = table(kind, t)[3]
            copy(kind, t, place, place, y_dev).wait_recv()

    def r0(r, t, parts):
        b = rem(t, 4)
        ahead, _ = sides(t)
        for m, g in enumerate(parts):
            r.px[b, :, m] = g[:, :XW].reshape(4, 32, XW)
            gy = g[:, XW:].reshape(4, 2, 16, YW)
            for yy in range(2):
                r.py[b, yy, :, m] = gy[:, yy]
        r.sxd[t] = r.px[b, ahead].astype(BF)
        r.sxr[t] = r.px[b, far].astype(BF)
        start(t, r.base + XD, r.base + XR)
        r.syy[t] = r.py[b, yo].astype(BF)
        start(t, r.base + YY)

    def r1(r, t):
        b = rem(t, 4)
        ahead, back = sides(t)
        arrive(t, r.base + XR)
        r.sx2[t] = (r.px[b, back] + r.rxr[t].astype(F32)).astype(BF)
        start(t, r.base + X2)
        arrive(t, r.base + YY)
        r.py[b, y] = r.py[b, y] + r.ryy[t].astype(F32)
        r.syd[t] = r.py[b, y, ahead].astype(BF)
        r.syr[t] = r.py[b, y, far].astype(BF)
        start(t, r.base + YD, r.base + YR)

    def r2(r, t):
        b = rem(t, 4)
        _, back = sides(t)
        arrive(t, r.base + XD, r.base + X2)
        r.px[b, x] = r.px[b, x] + r.rxd[t].astype(F32) + r.rx2[t].astype(F32)
        r.sxy[t] = r.px[b, x, :, pl.ds(pl.multiple_of(yo * 16, 16), 16), :].astype(BF)
        start(t, r.base + XY)
        arrive(t, r.base + YR)
        r.sy2[t] = (r.py[b, y, back] + r.ryr[t].astype(F32)).astype(BF)
        start(t, r.base + Y2)

    def r3x(r, t):
        b = rem(t, 4)
        arrive(t, r.base + XY)
        return r.px[b, x, :, pl.ds(pl.multiple_of(y * 16, 16), 16), :] + r.rxy[t].astype(F32)

    def r3y(r, t):
        b = rem(t, 4)
        arrive(t, r.base + YD, r.base + Y2)
        return r.py[b, y, x] + r.ryd[t].astype(F32) + r.ry2[t].astype(F32)

    def hx(u):
        start(u, CIN)

    def h0(u):
        arrive(u, CIN)
        r0(hg, u, [lax.dot_general(c2[tokh(u)], wd[...], (((1,), (1,)), ((), ())), preferred_element_type=F32)])

    def h3(u):
        c = tokh(u)
        hfx[c] = r3x(hg, u)[0]
        hfy[c] = r3y(hg, u)[0]

    def p0(t):
        c = tok(t)
        spot = pos_ref[pl.ds(pl.multiple_of(c * 128, 128), 128), :]
        pick = jnp.where(lax.broadcasted_iota(jnp.int32, (128, 2048), 1) == spot, 1.0, 0.0).astype(BF)
        own = jnp.dot(pick, pool[...].reshape(2048, 512), preferred_element_type=F32)
        xin[c, :, 0:512] = own.astype(BF)
        start(t, XIN)
        pltpu.make_async_copy(xin.at[c, :, 0:512], xo_ref.at[c], osem.at[1, t]).start()

    def s0(t):
        arrive(t, XIN)
        x_t = xin[tok(t)]
        r0(gu, t, [jnp.dot(x_t, w[...], preferred_element_type=F32) for w in (wg, wu)])

    def activate(c, full, hgrad, cols):
        gate, up = full[0], full[1]
        sigma = jax.nn.sigmoid(gate)
        act[c, x, y, 0, :, cols] = (gate * sigma * up).astype(BF)
        act[c, x, y, 1, :, cols] = (hgrad * up * sigma * (1.0 + gate * (1.0 - sigma))).astype(BF)
        act[c, x, y, 2, :, cols] = (hgrad * gate * sigma).astype(BF)

    def s3(t):
        c = tok(t)
        activate(c, r3x(gu, t), hfx[c], cx)
        start(t, AXY)
        activate(c, r3y(gu, t), hfy[c], cy)
        start(t, AYP, AYM)

    def s4(t):
        arrive(t, AXY)
        start(t, AXP, AXM)
        arrive(t, AYP)
        start(t, AYF)
        arrive(t, AYM)

    def s5(t):
        arrive(t, AXP)
        start(t, AXF)
        arrive(t, AXM)
        arrive(t, AYF)
        start(t, AYY)

    def s6(t):
        arrive(t, AXF, AYY)
        start(t, CORE)

    def s7(t):
        c = tok(t)
        arrive(t, CORE)
        pltpu.make_async_copy(act.at[c], o_ref.at[c], osem.at[0, t]).start()
        hidden = act[c, :, :, 0].reshape(128, 2 * HALF)
        lo[t] = jnp.dot(hidden, wdo[...], preferred_element_type=F32)

        @pl.when(rem(t, 4) < 3)
        def _():
            start(t, LOZ)

        @pl.when(t == 7)
        def _():
            arrive(4, LOZ)
            arrive(5, LOZ)
            arrive(6, LOZ)
            arrive1(LOY)
            out_ref[...] = (lo[7] + rz[4] + rz[5] + rz[6] + rh[...]).astype(BF)

    def s8(t):
        @pl.when(t == 3)
        def _():
            arrive(0, LOZ)
            arrive(1, LOZ)
            arrive(2, LOZ)
            zs[...] = lo[3] + rz[0] + rz[1] + rz[2]
            start1(LOY)

    def spread(i, carry):
        to = rem(row + i, 16)
        pltpu.make_async_remote_copy(
            src_ref=v_ref.at[:, pl.ds(pl.multiple_of(to * 512, 512), 512)],
            dst_ref=pool.at[yh, z, row],
            send_sem=sa.at[i], recv_sem=ra.at[i], device_id={"row": to}, device_id_type=MESH,
        ).start()
        return carry

    def spread_in(i, carry):
        place = pool.at[yh, z, rem(row + 16 - i, 16)]
        pltpu.make_async_remote_copy(
            src_ref=place, dst_ref=place, send_sem=sa.at[i], recv_sem=ra.at[i],
            device_id=y_dev, device_id_type=MESH,
        ).wait_recv()
        return carry

    def spread_out(i, carry):
        place = v_ref.at[:, 0:512]
        pltpu.make_async_remote_copy(
            src_ref=place, dst_ref=pool.at[yh, z, row], send_sem=sa.at[i], recv_sem=ra.at[i],
            device_id=y_dev, device_id_type=MESH,
        ).wait_send()
        return carry

    lax.fori_loop(1, 16, spread, 0)
    start1(WD, CP, CM, CY)
    for c in here[1:]:
        c.start()

    def c_1():
        arrive1(CP)
        start1(CF1)
        arrive1(CM)
        start1(CF2)
        arrive1(CY)
        start1(DP, DM)

    def c_3():
        arrive1(CF1, CF2, DP)
        start1(DF1)
        arrive1(DM)
        start1(DF2)

    def c_7():
        arrive1(DF1, DF2)
        pltpu.make_async_copy(c2.at[:, :, 0:512], co_ref, lsem.at[4]).start()

    def v_0():
        lax.fori_loop(1, 16, spread_in, 0)
        start1(VY, VP, VM)

    def v_2():
        arrive1(VY)
        start1(WP, WM)
        arrive1(VP)
        start1(VF1)
        arrive1(VM)
        start1(VF2)

    def v_4():
        arrive1(VF1, VF2)
        start1(VH)
        arrive1(WP)
        start1(WF1)
        arrive1(WM)
        start1(WF2)

    def v_6():
        arrive1(WF1, WF2, VH)

    def w_1():
        here[0].wait()
        arrive1(WD)
        start1(WG, WU)

    def w_8():
        here[1].wait()
        here[2].wait()
        here[3].wait()
        arrive1(WG, WU)

    def each(n, lag, stage):
        t = n - lag

        @pl.when((t >= 0) & (t < CHUNKS))
        def _():
            stage(t)

    def at(n, when, stage):
        @pl.when(n == when)
        def _():
            stage()

    def step(n, carry):
        at(n, 1, c_1)
        at(n, 3, c_3)
        at(n, 7, c_7)
        at(n, 1, w_1)
        for lag, stage in enumerate(
            [hx, h0, lambda u: r1(hg, u), lambda u: r2(hg, u), h3]
        ):
            each(n, lag, stage)
        at(n, 0, v_0)
        at(n, 2, v_2)
        at(n, 4, v_4)
        at(n, 6, v_6)
        at(n, FIRST + 1, w_8)
        for lag, stage in enumerate(
            [p0, s0, lambda t: r1(gu, t), lambda t: r2(gu, t), s3, s4, s5, s6, s7, s8]
        ):
            each(n, FIRST + lag, stage)
        return carry

    lax.fori_loop(0, FIRST + CHUNKS + 9, step, 0)

    def sent(kind, t):
        src, dst, dev, _ = table(kind, t)
        copy(kind, t, src, dst, dev).wait_send()

    def finish(t, carry):
        for kind in range(KINDS):
            if kind != LOZ:
                sent(kind, t)

        @pl.when(rem(t, 4) < 3)
        def _():
            sent(LOZ, t)

        c = tok(t)
        pltpu.make_async_copy(act.at[c], o_ref.at[c], osem.at[0, t]).wait()
        pltpu.make_async_copy(xin.at[c, :, 0:512], xo_ref.at[c], osem.at[1, t]).wait()
        return carry

    lax.fori_loop(0, CHUNKS, finish, 0)
    lax.fori_loop(1, 16, spread_out, 0)
    for kind in range(ONCE):
        src, dst, dev, _ = single[kind]()
        once(kind, src, dst, dev).wait_send()
    pltpu.make_async_copy(c2.at[:, :, 0:512], co_ref, lsem.at[4]).wait()


def main_call(v, pos, og, gate, up, down):
    n = CHUNKS
    vm = lambda *s: pltpu.VMEM(s, BF)
    vf = lambda *s: pltpu.VMEM(s, F32)

    def row_sum(mats):
        xb, xq, yb = (n, mats, 32, XW), (n, mats, 16, XW), (n, mats, 16, YW)
        moves = [vm(*xb), vm(*xb), vm(*xb), vm(*xq), vm(n, 4, mats, 16, YW), vm(*yb), vm(*yb), vm(*yb)]
        return [vf(4, 4, mats, 32, XW), vf(4, 2, 4, mats, 16, YW), *moves, *moves]

    dma = pltpu.SemaphoreType.DMA
    vmem = pl.BlockSpec(memory_space=pltpu.VMEM)
    hbm = pl.BlockSpec(memory_space=pl.ANY)
    return pl.pallas_call(
        main_kernel,
        out_shape=(
            jax.ShapeDtypeStruct((128, 512), BF),
            jax.ShapeDtypeStruct((n, 4, 2, 3, 16, 2 * HALF), BF),
            jax.ShapeDtypeStruct((n, 128, 512), BF),
            jax.ShapeDtypeStruct((n, 128, 512), BF),
        ),
        in_specs=[vmem, vmem, vmem, hbm, hbm, hbm],
        out_specs=(vmem, hbm, hbm, hbm),
        scratch_shapes=[
            vm(n, 4, 2, 3, 16, 2 * HALF), vm(2, 4, 16, 16, 512), vm(n, 128, 1024), vm(n, 128, 1024),
            vm(1024, HALF), vm(1024, HALF), vm(HALF, 1024), vm(2 * HALF, 512),
            vf(n, 16, XW), vf(n, 16, YW),
            vf(n, 128, 512), vf(n, 128, 512), vf(128, 512), vf(128, 512),
            *row_sum(2), *row_sum(1),
            dma((KINDS, n)), dma((KINDS, n)), dma((ONCE,)), dma((ONCE,)), dma((16,)), dma((16,)),
            dma((2, n)), dma((5,)),
        ],
        compiler_params=pltpu.CompilerParams(
            collective_id=0, has_side_effects=True, vmem_limit_bytes=60 << 20
        ),
        cost_estimate=pl.CostEstimate(flops=10**10, bytes_accessed=30 * 10**6, transcendentals=0),
        name="row_sums",
    )(v, pos, og, gate, up, down)


def grads_kernel(x_ref, c_ref, h_ref, gg_ref, ug_ref, gate_ref, up_ref, down_ref, xt):
    @pl.when(pl.program_id(0) == 0)
    def _():
        xt[...] = x_ref[...].reshape(1024, 512).T

    width = h_ref.shape[-1]
    gate_ref[...] = jnp.dot(xt[...], gg_ref[...].reshape(1024, width), preferred_element_type=F32)
    up_ref[...] = jnp.dot(xt[...], ug_ref[...].reshape(1024, width), preferred_element_type=F32)
    down_ref[...] = lax.dot_general(
        h_ref[...].reshape(1024, width), c_ref[...].reshape(1024, 512), (((0,), (0,)), ((), ())), preferred_element_type=F32
    )


def grads_call(x, c, o):
    width = 256
    n = CHUNKS
    part = lambda m: pl.BlockSpec((n, 4, 2, 1, 16, width), lambda j: (0, 0, 0, m, 0, j))
    return pl.pallas_call(
        grads_kernel,
        grid=(1792 // width,),
        out_shape=(
            jax.ShapeDtypeStruct((512, 1792), F32),
            jax.ShapeDtypeStruct((512, 1792), F32),
            jax.ShapeDtypeStruct((1792, 512), F32),
        ),
        in_specs=[
            pl.BlockSpec((n, 128, 512), lambda j: (0, 0, 0)),
            pl.BlockSpec((n, 128, 512), lambda j: (0, 0, 0)),
            part(0), part(1), part(2),
        ],
        out_specs=(
            pl.BlockSpec((512, width), lambda j: (0, j)),
            pl.BlockSpec((512, width), lambda j: (0, j)),
            pl.BlockSpec((width, 512), lambda j: (j, 0)),
        ),
        scratch_shapes=[pltpu.VMEM((512, 1024), BF)],
        compiler_params=pltpu.CompilerParams(vmem_limit_bytes=60 << 20),
        cost_estimate=pl.CostEstimate(flops=6 * 10**9, bytes_accessed=24 * 10**6, transcendentals=0),
        name="weight_grads",
    )(x, c, o, o, o)


def local(vision_tokens, image_counts, image_owner, gate_weight, up_weight, down_weight, out_grad):
    slots = vision_tokens.shape[0]
    row_count = lax.axis_size("row")
    col_count = lax.axis_size("col")
    token_total = out_grad.shape[0] * col_count
    owner, slot = token_place(image_counts, image_owner, token_total)
    owner_row = owner // col_count
    owner_col = owner % col_count
    pool_index = owner_col * (row_count * slots) + owner_row * slots + slot
    layer_out, o, x, c = main_call(
        vision_tokens, pool_index[:, None], out_grad, gate_weight, up_weight, down_weight
    )
    grad_gate, grad_up, grad_down = grads_call(x, c, o)
    return (layer_out, grad_gate, grad_up, grad_down)


def solution(mesh):
    in_specs = (
        P(("row", "col"), None),
        P(),
        P(),
        P("row", "col"),
        P("row", "col"),
        P("col", "row"),
        P("col", "row"),
    )
    out_specs = (P("col", "row"), P("row", "col"), P("row", "col"), P("col", "row"))
    return jax.shard_map(local, mesh=mesh, in_specs=in_specs, out_specs=out_specs, check_vma=False)
```

```python
import functools
import jax
import jax.numpy as jnp
from jax import lax
from jax.experimental import pallas as pl
from jax.experimental.pallas import tpu as pltpu
from jax.sharding import PartitionSpec as P

BF = jnp.bfloat16
F32 = jnp.float32
MESH = pl.DeviceIdType.MESH

CHUNKS = 8
HALF = 896
XW = 512
YW = HALF - XW

XD, XR, X2, XY, YY, YD, YR, Y2 = range(8)
HG = 8
AXY, AXP, AXM, AXF, AYP, AYM, AYF, AYY, CORE, XIN, CIN, LOZ = range(16, 28)
KINDS = 28
CP, CM, CY, CF1, CF2, DP, DM, DF1, DF2 = range(9)
TP, TM, TY, TF1, TF2, UP, UM, UF1, UF2 = range(9, 18)
RZ1, RZ2, RZ3, RZY, RY, RYZ1, RYZ2, RYZ3 = range(18, 26)
WG, WU, WD, LOY = range(26, 30)
ONCE = 30
FIRST = 5

def rem(a, n):
    return lax.rem(a, n)


class RowSum:
    def __init__(self, base, refs):
        self.base = base
        (self.px, self.py, self.sxd, self.sxr, self.sx2, self.sxy, self.syy, self.syd, self.syr,
         self.sy2, self.rxd, self.rxr, self.rx2, self.rxy, self.ryy, self.ryd, self.ryr, self.ry2) = refs


def main_kernel(
    v_ref, counts_ref, owner_ref, og_ref, gate_hbm, up_hbm, down_hbm,
    out_ref, o_ref, ht_ref, xt_ref, co_ref,
    act, pool, xin, c2, wg, wu, wd, wdo,
    part, rtz, rty, stz, rtyz, rtzy, ht, xt,
    hfx, hfy, lo, rz, zs, rh,
    *rest,
):
    gu, hg = RowSum(0, rest[:18]), RowSum(HG, rest[18:36])
    ssem, rsem, ssem1, rsem1, sa, ra, osem, lsem = rest[36:]
    row = lax.axis_index("row")
    col = lax.axis_index("col")
    x, y, k = row // 4, rem(row // 2, 2), rem(row, 2)
    yh, z = col // 4, rem(col, 4)
    yo, ko, ho = 1 - y, 1 - k, 1 - yh
    far = rem(x + 2, 4)
    zp, zm, zf = rem(z + 1, 4), rem(z + 3, 4), rem(z + 2, 4)

    def at_row(xx, yy, kk):
        return {"row": xx * 4 + yy * 2 + kk}

    def at_col(hh, zz):
        return {"col": hh * 4 + zz}

    y_dev, core_dev = at_row(x, yo, k), at_row(x, y, ko)
    up_dev, down_dev, hi_dev = at_col(yh, zp), at_col(yh, zm), at_col(ho, z)
    barrier = pltpu.get_barrier_semaphore()

    def greet(i, carry):
        pl.semaphore_signal(barrier, inc=1, device_id={"row": rem(row + i, 16)}, device_id_type=MESH)
        return carry

    lax.fori_loop(1, 16, greet, 0)
    for dev in (up_dev, down_dev, at_col(yh, zf), hi_dev):
        pl.semaphore_signal(barrier, inc=1, device_id=dev, device_id_type=MESH)

    mine = pl.ds(pl.multiple_of(k * HALF, 128), HALF)
    theirs = pl.ds(pl.multiple_of(ko * HALF, 128), HALF)
    here = [
        pltpu.make_async_copy(down_hbm.at[mine, :], wd.at[:, 0:512], lsem.at[0]),
        pltpu.make_async_copy(gate_hbm.at[:, mine], wg.at[0:512, :], lsem.at[1]),
        pltpu.make_async_copy(up_hbm.at[:, mine], wu.at[0:512, :], lsem.at[2]),
        pltpu.make_async_copy(down_hbm, wdo, lsem.at[3]),
    ]
    here[0].start()
    c2[col, :, 0:512] = og_ref[...]
    pool[row] = v_ref[:, pl.ds(pl.multiple_of(row * 512, 512), 512)]
    pl.semaphore_wait(barrier, 19)

    cx = pl.ds(pl.multiple_of(k * HALF, 128), XW)
    cy = pl.ds(pl.multiple_of(k * HALF + XW, 128), YW)

    def copy(kind, t, src, dst, dev):
        return pltpu.make_async_remote_copy(
            src_ref=src, dst_ref=dst, send_sem=ssem.at[kind, t], recv_sem=rsem.at[kind, t],
            device_id=dev, device_id_type=MESH,
        )

    def once(kind, src, dst, dev):
        return pltpu.make_async_remote_copy(
            src_ref=src, dst_ref=dst, send_sem=ssem1.at[kind], recv_sem=rsem1.at[kind],
            device_id=dev, device_id_type=MESH,
        )

    def same(ref):
        return ref, ref

    def cblk(hh, zz, at=0, n=128):
        return c2.at[hh * 4 + zz, at:at + n, 0:512]

    def tblk(hh, zz, at=0, n=128):
        return xin.at[hh * 4 + zz, at:at + n, 0:512]

    single = {
        WD: lambda: (down_hbm.at[theirs, :], wd.at[:, 512:1024], core_dev, wd.at[:, 512:1024]),
        WG: lambda: (gate_hbm.at[:, theirs], wg.at[512:1024, :], core_dev, wg.at[512:1024, :]),
        WU: lambda: (up_hbm.at[:, theirs], wu.at[512:1024, :], core_dev, wu.at[512:1024, :]),
        CP: lambda: (*same(cblk(yh, z)), up_dev, cblk(yh, zm)),
        CM: lambda: (*same(cblk(yh, z)), down_dev, cblk(yh, zp)),
        CY: lambda: (*same(cblk(yh, z)), hi_dev, cblk(ho, z)),
        CF1: lambda: (*same(cblk(yh, zm, 0, 64)), up_dev, cblk(yh, zf, 0, 64)),
        CF2: lambda: (*same(cblk(yh, zp, 64, 64)), down_dev, cblk(yh, zf, 64, 64)),
        DP: lambda: (*same(cblk(ho, z)), up_dev, cblk(ho, zm)),
        DM: lambda: (*same(cblk(ho, z)), down_dev, cblk(ho, zp)),
        DF1: lambda: (*same(cblk(ho, zm, 0, 64)), up_dev, cblk(ho, zf, 0, 64)),
        DF2: lambda: (*same(cblk(ho, zp, 64, 64)), down_dev, cblk(ho, zf, 64, 64)),
        TP: lambda: (*same(tblk(yh, z)), up_dev, tblk(yh, zm)),
        TM: lambda: (*same(tblk(yh, z)), down_dev, tblk(yh, zp)),
        TY: lambda: (*same(tblk(yh, z)), hi_dev, tblk(ho, z)),
        TF1: lambda: (*same(tblk(yh, zm, 0, 64)), up_dev, tblk(yh, zf, 0, 64)),
        TF2: lambda: (*same(tblk(yh, zp, 64, 64)), down_dev, tblk(yh, zf, 64, 64)),
        UP: lambda: (*same(tblk(ho, z)), up_dev, tblk(ho, zm)),
        UM: lambda: (*same(tblk(ho, z)), down_dev, tblk(ho, zp)),
        UF1: lambda: (*same(tblk(ho, zm, 0, 64)), up_dev, tblk(ho, zf, 0, 64)),
        UF2: lambda: (*same(tblk(ho, zp, 64, 64)), down_dev, tblk(ho, zf, 64, 64)),
        RZ1: lambda: (part.at[:, zp, :, 0:256], rtz.at[0], at_col(yh, zp), rtz.at[0]),
        RZ2: lambda: (part.at[:, zf, :, 0:256], rtz.at[1], at_col(yh, zf), rtz.at[1]),
        RZ3: lambda: (part.at[:, zm, :, 0:256], rtz.at[2], at_col(yh, zm), rtz.at[2]),
        RZY: lambda: (stz, rtzy, hi_dev, rtzy),
        RY: lambda: (part.at[ho, :, :, 256:512], rty, hi_dev, rty),
        RYZ1: lambda: (part.at[yh, zp, :, 256:512], rtyz.at[0], at_col(yh, zp), rtyz.at[0]),
        RYZ2: lambda: (part.at[yh, zf, :, 256:512], rtyz.at[1], at_col(yh, zf), rtyz.at[1]),
        RYZ3: lambda: (part.at[yh, zm, :, 256:512], rtyz.at[2], at_col(yh, zm), rtyz.at[2]),
        LOY: lambda: (zs, rh, hi_dev, rh),
    }

    def start1(*kinds):
        for kind in kinds:
            src, dst, dev, _ = single[kind]()
            once(kind, src, dst, dev).start()

    def arrive1(*kinds):
        for kind in kinds:
            place = single[kind]()[3]
            once(kind, place, place, y_dev).wait_recv()

    def sides(t):
        s = 1 - 2 * rem(t, 2)
        return rem(x + s + 4, 4), rem(x - s + 4, 4)

    def tokh(u):
        there = jnp.where((u >= 2) & (u < 6), ho, yh)
        off = jnp.where((u == 1) | (u == 3), 1, 0)
        off = off + jnp.where((u == 4) | (u == 6), 3, 0) + jnp.where((u == 5) | (u == 7), 2, 0)
        return there * 4 + rem(z + off, 4)

    def tok(t):
        return tokh(rem(t + 1, 8))

    def tokens(c):
        return pl.ds(pl.multiple_of(c * 128, 128), 128)

    def table(kind, t):
        ahead, back = sides(t)
        to_ahead, to_back = at_row(ahead, y, k), at_row(back, y, k)
        if kind < 16:
            r = gu if kind < HG else hg
            src, dst, dev = {
                XD: lambda: (r.sxd, r.rxd, to_ahead), XR: lambda: (r.sxr, r.rxr, to_back),
                X2: lambda: (r.sx2, r.rx2, to_back), XY: lambda: (r.sxy, r.rxy, y_dev),
                YY: lambda: (r.syy, r.ryy, y_dev), YD: lambda: (r.syd, r.ryd, to_ahead),
                YR: lambda: (r.syr, r.ryr, to_back), Y2: lambda: (r.sy2, r.ry2, to_back),
            }[kind % HG]()
            return src.at[t], dst.at[t], dev, dst.at[t]
        if kind == CIN:
            c = tokh(t)
            return c2.at[c, :, 0:512], c2.at[c, :, 512:1024], core_dev, c2.at[c, :, 512:1024]
        c = tok(t)
        return {
            AXY: lambda: (*same(act.at[c, x, y, :, :, cx]), y_dev, act.at[c, x, yo, :, :, cx]),
            AXP: lambda: (*same(act.at[c, x, :, :, :, cx]), to_ahead, act.at[c, back, :, :, :, cx]),
            AXM: lambda: (*same(act.at[c, x, :, :, :, cx]), to_back, act.at[c, ahead, :, :, :, cx]),
            AXF: lambda: (*same(act.at[c, back, :, :, :, cx]), to_ahead, act.at[c, far, :, :, :, cx]),
            AYP: lambda: (*same(act.at[c, x, y, :, :, cy]), to_ahead, act.at[c, back, y, :, :, cy]),
            AYM: lambda: (*same(act.at[c, x, y, :, :, cy]), to_back, act.at[c, ahead, y, :, :, cy]),
            AYF: lambda: (*same(act.at[c, back, y, :, :, cy]), to_ahead, act.at[c, far, y, :, :, cy]),
            AYY: lambda: (*same(act.at[c, :, y, :, :, cy]), y_dev, act.at[c, :, yo, :, :, cy]),
            CORE: lambda: (*same(act.at[c, :, :, :, :, mine]), core_dev, act.at[c, :, :, :, :, theirs]),
            XIN: lambda: (xin.at[c, :, 0:512], xin.at[c, :, 512:1024], core_dev, xin.at[c, :, 512:1024]),
            LOZ: lambda: (lo.at[t], rz.at[t], at_col(yh, rem(c, 4)), rz.at[t]),
        }[kind]()

    def start(t, *kinds):
        for kind in kinds:
            src, dst, dev, _ = table(kind, t)
            copy(kind, t, src, dst, dev).start()

    def arrive(t, *kinds):
        for kind in kinds:
            place = table(kind, t)[3]
            copy(kind, t, place, place, y_dev).wait_recv()

    def r0(r, t, parts):
        b = rem(t, 4)
        ahead, _ = sides(t)
        for m, g in enumerate(parts):
            r.px[b, :, m] = g[:, :XW].reshape(4, 32, XW)
            gy = g[:, XW:].reshape(4, 2, 16, YW)
            for yy in range(2):
                r.py[b, yy, :, m] = gy[:, yy]
        r.sxd[t] = r.px[b, ahead].astype(BF)
        r.sxr[t] = r.px[b, far].astype(BF)
        start(t, r.base + XD, r.base + XR)
        r.syy[t] = r.py[b, yo].astype(BF)
        start(t, r.base + YY)

    def r1(r, t):
        b = rem(t, 4)
        ahead, back = sides(t)
        arrive(t, r.base + XR)
        r.sx2[t] = (r.px[b, back] + r.rxr[t].astype(F32)).astype(BF)
        start(t, r.base + X2)
        arrive(t, r.base + YY)
        r.py[b, y] = r.py[b, y] + r.ryy[t].astype(F32)
        r.syd[t] = r.py[b, y, ahead].astype(BF)
        r.syr[t] = r.py[b, y, far].astype(BF)
        start(t, r.base + YD, r.base + YR)

    def r2(r, t):
        b = rem(t, 4)
        _, back = sides(t)
        arrive(t, r.base + XD, r.base + X2)
        r.px[b, x] = r.px[b, x] + r.rxd[t].astype(F32) + r.rx2[t].astype(F32)
        r.sxy[t] = r.px[b, x, :, pl.ds(pl.multiple_of(yo * 16, 16), 16), :].astype(BF)
        start(t, r.base + XY)
        arrive(t, r.base + YR)
        r.sy2[t] = (r.py[b, y, back] + r.ryr[t].astype(F32)).astype(BF)
        start(t, r.base + Y2)

    def r3x(r, t):
        b = rem(t, 4)
        arrive(t, r.base + XY)
        return r.px[b, x, :, pl.ds(pl.multiple_of(y * 16, 16), 16), :] + r.rxy[t].astype(F32)

    def r3y(r, t):
        b = rem(t, 4)
        arrive(t, r.base + YD, r.base + Y2)
        return r.py[b, y, x] + r.ryd[t].astype(F32) + r.ry2[t].astype(F32)

    def hx(u):
        start(u, CIN)

    def h0(u):
        arrive(u, CIN)
        r0(hg, u, [lax.dot_general(c2[tokh(u)], wd[...], (((1,), (1,)), ((), ())), preferred_element_type=F32)])

    def h3(u):
        c = tokh(u)
        hfx[c] = r3x(hg, u)[0]
        hfy[c] = r3y(hg, u)[0]

    def place(c, ends, starts, counts, owners):
        spot = lax.broadcasted_iota(jnp.int32, (128, 64), 0).astype(F32) + (c * 128).astype(F32)
        member = jnp.where((spot >= starts) & (spot < ends), 1.0, 0.0)

        def pick(values):
            return jnp.sum(member * values, axis=1, keepdims=True).astype(jnp.int32)

        count, begin = pick(counts), pick(starts)
        within = lax.broadcasted_iota(jnp.int32, (128, 1), 0) + c * 128 - begin
        first = (count + 1) >> 1
        second = within >= first
        slot = jnp.where(second, within - first, within)
        owner = jnp.where(second, pick(owners[1]), pick(owners[0]))
        index = jnp.where((owner & 7) == col, (owner >> 3) * 16 + slot, -1)
        hot = jnp.where(lax.broadcasted_iota(jnp.int32, (128, 256), 1) == index, 1.0, 0.0).astype(BF)
        rows = jnp.dot(hot, pool[...].reshape(256, 512), preferred_element_type=F32)
        part[c // 4, rem(c, 4)] = rows.astype(BF)

    def v_0():
        lax.fori_loop(1, 16, spread_in, 0)
        counts = jnp.broadcast_to(counts_ref[...].astype(F32), (8, 64))
        owner = jnp.broadcast_to(owner_ref[...].astype(F32), (8, 128))
        upto = lax.broadcasted_iota(jnp.int32, (64, 64), 0) <= lax.broadcasted_iota(jnp.int32, (64, 64), 1)
        ends = jnp.dot(counts, jnp.where(upto, 1.0, 0.0), preferred_element_type=F32)
        starts = ends - counts
        i0 = lax.broadcasted_iota(jnp.int32, (128, 64), 0)
        i1 = lax.broadcasted_iota(jnp.int32, (128, 64), 1) * 2
        owners = [
            jnp.dot(owner, jnp.where(i0 == i1 + j, 1.0, 0.0), preferred_element_type=F32)[0:1] for j in range(2)
        ]

        def body(c, carry):
            place(c, ends[0:1], starts[0:1], counts[0:1], owners)
            return carry

        lax.fori_loop(0, 8, body, 0)
        start1(RY, RZ1, RZ2, RZ3)

    def v_2():
        arrive1(RY)
        part[yh, :, :, 256:512] = part[yh, :, :, 256:512] + rty[...]
        start1(RYZ1, RYZ2, RYZ3)
        arrive1(RZ1, RZ2, RZ3)
        stz[...] = part[ho, z, :, 0:256] + rtz[0, ho] + rtz[1, ho] + rtz[2, ho]
        start1(RZY)

    def v_4():
        arrive1(RYZ1, RYZ2, RYZ3)
        xin[col, :, 256:512] = part[yh, z, :, 256:512] + rtyz[0] + rtyz[1] + rtyz[2]
        arrive1(RZY)
        xin[col, :, 0:256] = part[yh, z, :, 0:256] + rtz[0, yh] + rtz[1, yh] + rtz[2, yh] + rtzy[...]
        start1(TP, TM, TY)

    def t_0():
        arrive1(TM)
        start1(TF2)
        arrive1(TY)
        start1(UP, UM)
        arrive1(TP)
        start1(TF1)

    def t_2():
        arrive1(UP)
        start1(UF1)
        arrive1(UM)
        start1(UF2)

    def t_4():
        arrive1(UF1, UF2)

    def t_6():
        arrive1(TF1, TF2)

    def p0(t):
        start(t, XIN)

    def s0(t):
        arrive(t, XIN)
        c = tok(t)
        x_t = xin[c]
        xt[t] = x_t[:, 0:512].T
        pltpu.make_async_copy(xt.at[t], xt_ref.at[:, tokens(c)], osem.at[1, t]).start()
        r0(gu, t, [jnp.dot(x_t, w[...], preferred_element_type=F32) for w in (wg, wu)])

    def activate(c, full, hgrad, cols):
        gate, up = full[0], full[1]
        sigma = jax.nn.sigmoid(gate)
        act[c, x, y, 0, :, cols] = (gate * sigma * up).astype(BF)
        act[c, x, y, 1, :, cols] = (hgrad * up * sigma * (1.0 + gate * (1.0 - sigma))).astype(BF)
        act[c, x, y, 2, :, cols] = (hgrad * gate * sigma).astype(BF)

    def s3(t):
        c = tok(t)
        activate(c, r3x(gu, t), hfx[c], cx)
        start(t, AXY)
        activate(c, r3y(gu, t), hfy[c], cy)
        start(t, AYP, AYM)

    def s4(t):
        arrive(t, AXY)
        start(t, AXP, AXM)
        arrive(t, AYP)
        start(t, AYF)
        arrive(t, AYM)

    def s5(t):
        arrive(t, AXP)
        start(t, AXF)
        arrive(t, AXM)
        arrive(t, AYF)
        start(t, AYY)

    def s6(t):
        arrive(t, AXF, AYY)
        start(t, CORE)

    def s7(t):
        c = tok(t)
        arrive(t, CORE)
        pltpu.make_async_copy(act.at[c, :, :, 1:3], o_ref.at[c], osem.at[0, t]).start()
        hidden = act[c, :, :, 0].reshape(128, 2 * HALF)
        lo[t] = jnp.dot(hidden, wdo[...], preferred_element_type=F32)

        @pl.when((t != 1) & (t != 7))
        def _():
            start(t, LOZ)

        ht[t] = hidden.T
        pltpu.make_async_copy(ht.at[t], ht_ref.at[:, tokens(c)], osem.at[2, t]).start()

        @pl.when(t == 7)
        def _():
            arrive(0, LOZ)
            arrive(5, LOZ)
            arrive(6, LOZ)
            arrive1(LOY)
            out_ref[...] = (lo[7] + rz[0] + rz[5] + rz[6] + rh[...]).astype(BF)

    def s8(t):
        @pl.when(t == 4)
        def _():
            arrive(2, LOZ)
            arrive(3, LOZ)
            arrive(4, LOZ)
            zs[...] = lo[1] + rz[2] + rz[3] + rz[4]
            start1(LOY)

    def spread(i, carry):
        to = rem(row + i, 16)
        pltpu.make_async_remote_copy(
            src_ref=v_ref.at[:, pl.ds(pl.multiple_of(to * 512, 512), 512)],
            dst_ref=pool.at[row],
            send_sem=sa.at[i], recv_sem=ra.at[i], device_id={"row": to}, device_id_type=MESH,
        ).start()
        return carry

    def spread_in(i, carry):
        place = pool.at[rem(row + 16 - i, 16)]
        pltpu.make_async_remote_copy(
            src_ref=place, dst_ref=place, send_sem=sa.at[i], recv_sem=ra.at[i],
            device_id=y_dev, device_id_type=MESH,
        ).wait_recv()
        return carry

    def spread_out(i, carry):
        place = v_ref.at[:, 0:512]
        pltpu.make_async_remote_copy(
            src_ref=place, dst_ref=pool.at[row], send_sem=sa.at[i], recv_sem=ra.at[i],
            device_id=y_dev, device_id_type=MESH,
        ).wait_send()
        return carry

    lax.fori_loop(1, 16, spread, 0)
    start1(WD, CP, CM, CY)
    for c in here[1:]:
        c.start()

    def c_1():
        arrive1(CM)
        start1(CF2)
        arrive1(CY)
        start1(DP, DM)
        arrive1(CP)
        start1(CF1)

    def c_3():
        arrive1(DP)
        start1(DF1)
        arrive1(DM)
        start1(DF2)

    def c_5():
        arrive1(DF1, DF2)

    def c_7():
        arrive1(CF1, CF2)
        pltpu.make_async_copy(c2.at[:, :, 0:512], co_ref, lsem.at[4]).start()

    def w_1():
        here[0].wait()
        arrive1(WD)
        start1(WG, WU)

    def w_8():
        here[1].wait()
        here[2].wait()
        here[3].wait()
        arrive1(WG, WU)

    def each(n, lag, stage):
        t = n - lag

        @pl.when((t >= 0) & (t < CHUNKS))
        def _():
            stage(t)

    def at(n, when, stage):
        @pl.when(n == when)
        def _():
            stage()

    def step(n, carry):
        at(n, 1, c_1)
        at(n, 3, c_3)
        at(n, 5, c_5)
        at(n, 7, c_7)
        at(n, 1, w_1)
        for lag, stage in enumerate(
            [hx, h0, lambda u: r1(hg, u), lambda u: r2(hg, u), h3]
        ):
            each(n, lag, stage)
        at(n, 0, v_0)
        at(n, 2, v_2)
        at(n, 4, v_4)
        at(n, FIRST, t_0)
        at(n, FIRST + 2, t_2)
        at(n, FIRST + 4, t_4)
        at(n, FIRST + 6, t_6)
        at(n, FIRST + 1, w_8)
        for lag, stage in enumerate(
            [p0, s0, lambda t: r1(gu, t), lambda t: r2(gu, t), s3, s4, s5, s6, s7, s8]
        ):
            each(n, FIRST + lag, stage)
        return carry

    lax.fori_loop(0, FIRST + CHUNKS + 9, step, 0)

    def sent(kind, t):
        src, dst, dev, _ = table(kind, t)
        copy(kind, t, src, dst, dev).wait_send()

    def finish(t, carry):
        for kind in range(KINDS):
            if kind != LOZ:
                sent(kind, t)

        @pl.when((t != 1) & (t != 7))
        def _():
            sent(LOZ, t)

        c = tok(t)
        pltpu.make_async_copy(act.at[c, :, :, 1:3], o_ref.at[c], osem.at[0, t]).wait()
        pltpu.make_async_copy(ht.at[t], ht_ref.at[:, tokens(c)], osem.at[2, t]).wait()
        pltpu.make_async_copy(xt.at[t], xt_ref.at[:, tokens(c)], osem.at[1, t]).wait()
        return carry

    lax.fori_loop(0, CHUNKS, finish, 0)
    lax.fori_loop(1, 16, spread_out, 0)
    for kind in range(ONCE):
        src, dst, dev, _ = single[kind]()
        once(kind, src, dst, dev).wait_send()
    pltpu.make_async_copy(c2.at[:, :, 0:512], co_ref, lsem.at[4]).wait()


def main_call(v, counts, owner, og, gate, up, down):
    n = CHUNKS
    vm = lambda *s: pltpu.VMEM(s, BF)
    vf = lambda *s: pltpu.VMEM(s, F32)

    def row_sum(mats):
        xb, xq, yb = (n, mats, 32, XW), (n, mats, 16, XW), (n, mats, 16, YW)
        moves = [vm(*xb), vm(*xb), vm(*xb), vm(*xq), vm(n, 4, mats, 16, YW), vm(*yb), vm(*yb), vm(*yb)]
        return [vf(4, 4, mats, 32, XW), vf(4, 2, 4, mats, 16, YW), *moves, *moves]

    dma = pltpu.SemaphoreType.DMA
    vmem = pl.BlockSpec(memory_space=pltpu.VMEM)
    hbm = pl.BlockSpec(memory_space=pl.ANY)
    return pl.pallas_call(
        main_kernel,
        out_shape=(
            jax.ShapeDtypeStruct((128, 512), BF),
            jax.ShapeDtypeStruct((n, 4, 2, 2, 16, 2 * HALF), BF),
            jax.ShapeDtypeStruct((2 * HALF, 1024), BF),
            jax.ShapeDtypeStruct((512, 1024), BF),
            jax.ShapeDtypeStruct((n, 128, 512), BF),
        ),
        in_specs=[vmem, vmem, vmem, vmem, hbm, hbm, hbm],
        out_specs=(vmem, hbm, hbm, hbm, hbm),
        scratch_shapes=[
            vm(n, 4, 2, 3, 16, 2 * HALF), vm(16, 16, 512), vm(n, 128, 1024), vm(n, 128, 1024),
            vm(1024, HALF), vm(1024, HALF), vm(HALF, 1024), vm(2 * HALF, 512),
            vm(2, 4, 128, 512), vm(3, 2, 128, 256), vm(4, 128, 256), vm(128, 256), vm(3, 128, 256), vm(128, 256),
            vm(n, 2 * HALF, 128), vm(n, 512, 128),
            vf(n, 16, XW), vf(n, 16, YW),
            vf(n, 128, 512), vf(n, 128, 512), vf(128, 512), vf(128, 512),
            *row_sum(2), *row_sum(1),
            dma((KINDS, n)), dma((KINDS, n)), dma((ONCE,)), dma((ONCE,)), dma((16,)), dma((16,)),
            dma((3, n)), dma((5,)),
        ],
        compiler_params=pltpu.CompilerParams(
            collective_id=0, has_side_effects=True, vmem_limit_bytes=60 << 20
        ),
        cost_estimate=pl.CostEstimate(flops=10**10, bytes_accessed=30 * 10**6, transcendentals=0),
        name="row_sums",
    )(v, counts, owner, og, gate, up, down)


def grads_kernel(xt_ref, c_ref, ht_ref, gg_ref, ug_ref, gate_ref, up_ref, down_ref):
    width = ht_ref.shape[0]
    gate_ref[...] = jnp.dot(xt_ref[...], gg_ref[...].reshape(1024, width), preferred_element_type=F32)
    up_ref[...] = jnp.dot(xt_ref[...], ug_ref[...].reshape(1024, width), preferred_element_type=F32)
    down_ref[...] = jnp.dot(ht_ref[...], c_ref[...].reshape(1024, 512), preferred_element_type=F32)


def grads_call(xt, c, ht, o):
    width = 256
    n = CHUNKS
    part = lambda m: pl.BlockSpec((n, 4, 2, 1, 16, width), lambda j: (0, 0, 0, m, 0, j))
    return pl.pallas_call(
        grads_kernel,
        grid=(1792 // width,),
        out_shape=(
            jax.ShapeDtypeStruct((512, 1792), F32),
            jax.ShapeDtypeStruct((512, 1792), F32),
            jax.ShapeDtypeStruct((1792, 512), F32),
        ),
        in_specs=[
            pl.BlockSpec((512, 1024), lambda j: (0, 0)),
            pl.BlockSpec((n, 128, 512), lambda j: (0, 0, 0)),
            pl.BlockSpec((width, 1024), lambda j: (j, 0)),
            part(0), part(1),
        ],
        out_specs=(
            pl.BlockSpec((512, width), lambda j: (0, j)),
            pl.BlockSpec((512, width), lambda j: (0, j)),
            pl.BlockSpec((width, 512), lambda j: (j, 0)),
        ),
        compiler_params=pltpu.CompilerParams(vmem_limit_bytes=60 << 20),
        cost_estimate=pl.CostEstimate(flops=6 * 10**9, bytes_accessed=24 * 10**6, transcendentals=0),
        name="weight_grads",
    )(xt, c, ht, o, o)


def local(vision_tokens, image_counts, image_owner, gate_weight, up_weight, down_weight, out_grad):
    layer_out, o, ht, xt, c = main_call(
        vision_tokens, image_counts[None, :], image_owner[None, :], out_grad, gate_weight, up_weight, down_weight
    )
    grad_gate, grad_up, grad_down = grads_call(xt, c, ht, o)
    return (layer_out, grad_gate, grad_up, grad_down)


def solution(mesh):
    in_specs = (
        P(("row", "col"), None),
        P(),
        P(),
        P("row", "col"),
        P("row", "col"),
        P("col", "row"),
        P("col", "row"),
    )
    out_specs = (P("col", "row"), P("row", "col"), P("row", "col"), P("col", "row"))
    return jax.shard_map(local, mesh=mesh, in_specs=in_specs, out_specs=out_specs, check_vma=False)
```

```python
import functools
import jax
import jax.numpy as jnp
from jax import lax
from jax.experimental import pallas as pl
from jax.experimental.pallas import tpu as pltpu
from jax.sharding import PartitionSpec as P

BF = jnp.bfloat16
F32 = jnp.float32
MESH = pl.DeviceIdType.MESH

CHUNKS = 8
HALF = 896
XW = 512
YW = HALF - XW

XD, XR, X2, XY, YY, YD, YR, Y2 = range(8)
HG = 8
AXY, AXP, AXM, AXF, AYP, AYM, AYF, AYY, CORE, XIN, CIN, LOZ = range(16, 28)
KINDS = 28
CP, CM, CY, CF1, CF2, DP, DM, DF1, DF2 = range(9)
TP, TM, TY, TF1, TF2, UP, UM, UF1, UF2 = range(9, 18)
RZ1, RZ2, RZ3, RZY, RY, RYZ1, RYZ2, RYZ3 = range(18, 26)
WG, WU, WD, LOY, AXL, AYL = range(26, 32)
ONCE = 32
SLOTS = 4
FIRST = 5

def rem(a, n):
    return lax.rem(a, n)


class RowSum:
    def __init__(self, base, refs):
        self.base = base
        (self.px, self.py, self.sxd, self.sxr, self.sx2, self.sxy, self.syy, self.syd, self.syr,
         self.sy2, self.rxd, self.rxr, self.rx2, self.rxy, self.ryy, self.ryd, self.ryr, self.ry2) = refs


def main_kernel(
    v_ref, counts_ref, owner_ref, og_ref, gate_hbm, up_hbm, down_hbm,
    out_ref, o_ref, ht_ref, xt_ref, co_ref,
    act, pool, xin, c2, wg, wu, wd, wdo,
    hot, part, rtz, rty, stz, rtyz, rtzy, ht, xt,
    hfx, hfy, lo, rz, zs, rh,
    *rest,
):
    gu, hg = RowSum(0, rest[:18]), RowSum(HG, rest[18:36])
    ssem, rsem, zsem, ssem1, rsem1, asem, osem, lsem = rest[36:]
    row = lax.axis_index("row")
    col = lax.axis_index("col")
    x, y, k = row // 4, rem(row // 2, 2), rem(row, 2)
    yh, z = col // 4, rem(col, 4)
    yo, ko, ho = 1 - y, 1 - k, 1 - yh
    far = rem(x + 2, 4)
    zp, zm, zf = rem(z + 1, 4), rem(z + 3, 4), rem(z + 2, 4)

    def at_row(xx, yy, kk):
        return {"row": xx * 4 + yy * 2 + kk}

    def at_col(hh, zz):
        return {"col": hh * 4 + zz}

    y_dev, core_dev = at_row(x, yo, k), at_row(x, y, ko)
    far_dev = at_row(far, y, k)
    up_dev, down_dev, hi_dev = at_col(yh, zp), at_col(yh, zm), at_col(ho, z)
    barrier = pltpu.get_barrier_semaphore()

    def greet(i, carry):
        pl.semaphore_signal(barrier, inc=1, device_id={"row": rem(row + i, 16)}, device_id_type=MESH)
        return carry

    lax.fori_loop(1, 16, greet, 0)
    for dev in (up_dev, down_dev, at_col(yh, zf), hi_dev):
        pl.semaphore_signal(barrier, inc=1, device_id=dev, device_id_type=MESH)

    mine = pl.ds(pl.multiple_of(k * HALF, 128), HALF)
    theirs = pl.ds(pl.multiple_of(ko * HALF, 128), HALF)
    here = [
        pltpu.make_async_copy(down_hbm.at[mine, :], wd.at[:, 0:512], lsem.at[0]),
        pltpu.make_async_copy(gate_hbm.at[:, mine], wg.at[0:512, :], lsem.at[1]),
        pltpu.make_async_copy(up_hbm.at[:, mine], wu.at[0:512, :], lsem.at[2]),
        pltpu.make_async_copy(down_hbm, wdo, lsem.at[3]),
    ]
    here[0].start()
    c2[col, :, 0:512] = og_ref[...]
    pool[row] = v_ref[:, pl.ds(pl.multiple_of(row * 512, 512), 512)]
    pl.semaphore_wait(barrier, 19)

    cx = pl.ds(pl.multiple_of(k * HALF, 128), XW)
    cy = pl.ds(pl.multiple_of(k * HALF + XW, 128), YW)

    def copy(kind, t, src, dst, dev):
        return pltpu.make_async_remote_copy(
            src_ref=src, dst_ref=dst, send_sem=ssem.at[kind], recv_sem=rsem.at[kind, rem(t, SLOTS)] if kind != LOZ else zsem.at[t],
            device_id=dev, device_id_type=MESH,
        )

    def once(kind, src, dst, dev):
        return pltpu.make_async_remote_copy(
            src_ref=src, dst_ref=dst, send_sem=ssem1.at[kind], recv_sem=rsem1.at[kind],
            device_id=dev, device_id_type=MESH,
        )

    def same(ref):
        return ref, ref

    def cblk(hh, zz, at=0, n=128):
        return c2.at[hh * 4 + zz, at:at + n, 0:512]

    def tblk(hh, zz, at=0, n=128):
        return xin.at[hh * 4 + zz, at:at + n, 0:512]

    single = {
        WD: lambda: (down_hbm.at[theirs, :], wd.at[:, 512:1024], core_dev, wd.at[:, 512:1024]),
        WG: lambda: (gate_hbm.at[:, theirs], wg.at[512:1024, :], core_dev, wg.at[512:1024, :]),
        WU: lambda: (up_hbm.at[:, theirs], wu.at[512:1024, :], core_dev, wu.at[512:1024, :]),
        CP: lambda: (*same(cblk(yh, z)), up_dev, cblk(yh, zm)),
        CM: lambda: (*same(cblk(yh, z)), down_dev, cblk(yh, zp)),
        CY: lambda: (*same(cblk(yh, z)), hi_dev, cblk(ho, z)),
        CF1: lambda: (*same(cblk(yh, zm, 0, 64)), up_dev, cblk(yh, zf, 0, 64)),
        CF2: lambda: (*same(cblk(yh, zp, 64, 64)), down_dev, cblk(yh, zf, 64, 64)),
        DP: lambda: (*same(cblk(ho, z)), up_dev, cblk(ho, zm)),
        DM: lambda: (*same(cblk(ho, z)), down_dev, cblk(ho, zp)),
        DF1: lambda: (*same(cblk(ho, zm, 0, 64)), up_dev, cblk(ho, zf, 0, 64)),
        DF2: lambda: (*same(cblk(ho, zp, 64, 64)), down_dev, cblk(ho, zf, 64, 64)),
        TP: lambda: (*same(tblk(yh, z)), up_dev, tblk(yh, zm)),
        TM: lambda: (*same(tblk(yh, z)), down_dev, tblk(yh, zp)),
        TY: lambda: (*same(tblk(yh, z)), hi_dev, tblk(ho, z)),
        TF1: lambda: (*same(tblk(yh, zm, 0, 64)), up_dev, tblk(yh, zf, 0, 64)),
        TF2: lambda: (*same(tblk(yh, zp, 64, 64)), down_dev, tblk(yh, zf, 64, 64)),
        UP: lambda: (*same(tblk(ho, z)), up_dev, tblk(ho, zm)),
        UM: lambda: (*same(tblk(ho, z)), down_dev, tblk(ho, zp)),
        UF1: lambda: (*same(tblk(ho, zm, 0, 64)), up_dev, tblk(ho, zf, 0, 64)),
        UF2: lambda: (*same(tblk(ho, zp, 64, 64)), down_dev, tblk(ho, zf, 64, 64)),
        RZ1: lambda: (part.at[:, zp, :, 0:256], rtz.at[0], at_col(yh, zp), rtz.at[0]),
        RZ2: lambda: (part.at[:, zf, :, 0:256], rtz.at[1], at_col(yh, zf), rtz.at[1]),
        RZ3: lambda: (part.at[:, zm, :, 0:256], rtz.at[2], at_col(yh, zm), rtz.at[2]),
        RZY: lambda: (stz, rtzy, hi_dev, rtzy),
        RY: lambda: (part.at[ho, :, :, 256:512], rty, hi_dev, rty),
        RYZ1: lambda: (part.at[yh, zp, :, 256:512], rtyz.at[0], at_col(yh, zp), rtyz.at[0]),
        RYZ2: lambda: (part.at[yh, zf, :, 256:512], rtyz.at[1], at_col(yh, zf), rtyz.at[1]),
        RYZ3: lambda: (part.at[yh, zm, :, 256:512], rtyz.at[2], at_col(yh, zm), rtyz.at[2]),
        LOY: lambda: (zs, rh, hi_dev, rh),
        AXL: lambda: (*same(act.at[col, x, :, :, :, cx]), far_dev, act.at[col, far, :, :, :, cx]),
        AYL: lambda: (*same(act.at[col, x, y, :, :, cy]), far_dev, act.at[col, far, y, :, :, cy]),
    }

    def start1(*kinds):
        for kind in kinds:
            src, dst, dev, _ = single[kind]()
            once(kind, src, dst, dev).start()

    def arrive1(*kinds):
        for kind in kinds:
            place = single[kind]()[3]
            once(kind, place, place, y_dev).wait_recv()

    def sides(t):
        s = 1 - 2 * rem(t, 2)
        return rem(x + s + 4, 4), rem(x - s + 4, 4)

    def tokh(u):
        there = jnp.where((u >= 2) & (u < 6), ho, yh)
        off = jnp.where((u == 1) | (u == 3), 1, 0)
        off = off + jnp.where((u == 4) | (u == 6), 3, 0) + jnp.where((u == 5) | (u == 7), 2, 0)
        return there * 4 + rem(z + off, 4)

    def tok(t):
        return tokh(rem(t + 1, 8))

    def tokens(c):
        return pl.ds(pl.multiple_of(c * 128, 128), 128)

    def table(kind, t):
        ahead, back = sides(t)
        to_ahead, to_back = at_row(ahead, y, k), at_row(back, y, k)
        if kind < 16:
            r = gu if kind < HG else hg
            src, dst, dev = {
                XD: lambda: (r.sxd, r.rxd, to_ahead), XR: lambda: (r.sxr, r.rxr, to_back),
                X2: lambda: (r.sx2, r.rx2, to_back), XY: lambda: (r.sxy, r.rxy, y_dev),
                YY: lambda: (r.syy, r.ryy, y_dev), YD: lambda: (r.syd, r.ryd, to_ahead),
                YR: lambda: (r.syr, r.ryr, to_back), Y2: lambda: (r.sy2, r.ry2, to_back),
            }[kind % HG]()
            return src.at[t], dst.at[t], dev, dst.at[t]
        if kind == CIN:
            c = tokh(t)
            return c2.at[c, :, 0:512], c2.at[c, :, 512:1024], core_dev, c2.at[c, :, 512:1024]
        c = tok(t)
        return {
            AXY: lambda: (*same(act.at[c, x, y, :, :, cx]), y_dev, act.at[c, x, yo, :, :, cx]),
            AXP: lambda: (*same(act.at[c, x, :, :, :, cx]), to_ahead, act.at[c, back, :, :, :, cx]),
            AXM: lambda: (*same(act.at[c, x, :, :, :, cx]), to_back, act.at[c, ahead, :, :, :, cx]),
            AXF: lambda: (*same(act.at[c, back, :, :, :, cx]), to_ahead, act.at[c, far, :, :, :, cx]),
            AYP: lambda: (*same(act.at[c, x, y, :, :, cy]), to_ahead, act.at[c, back, y, :, :, cy]),
            AYM: lambda: (*same(act.at[c, x, y, :, :, cy]), to_back, act.at[c, ahead, y, :, :, cy]),
            AYF: lambda: (*same(act.at[c, back, y, :, :, cy]), to_ahead, act.at[c, far, y, :, :, cy]),
            AYY: lambda: (*same(act.at[c, :, y, :, :, cy]), y_dev, act.at[c, :, yo, :, :, cy]),
            CORE: lambda: (*same(act.at[c, :, :, :, :, mine]), core_dev, act.at[c, :, :, :, :, theirs]),
            XIN: lambda: (xin.at[c, :, 0:512], xin.at[c, :, 512:1024], core_dev, xin.at[c, :, 512:1024]),
            LOZ: lambda: (lo.at[t], rz.at[t], at_col(yh, rem(c, 4)), rz.at[t]),
        }[kind]()

    def start(t, *kinds):
        for kind in kinds:
            src, dst, dev, _ = table(kind, t)
            copy(kind, t, src, dst, dev).start()

    def arrive(t, *kinds):
        for kind in kinds:
            place = table(kind, t)[3]
            copy(kind, t, place, place, y_dev).wait_recv()

    def r0(r, t, parts):
        b = rem(t, 4)
        ahead, _ = sides(t)
        for m, g in enumerate(parts):
            r.px[b, :, m] = g[:, :XW].reshape(4, 32, XW)
            gy = g[:, XW:].reshape(4, 2, 16, YW)
            for yy in range(2):
                r.py[b, yy, :, m] = gy[:, yy]
        r.sxd[t] = r.px[b, ahead].astype(BF)
        r.sxr[t] = r.px[b, far].astype(BF)
        start(t, r.base + XD, r.base + XR)
        r.syy[t] = r.py[b, yo].astype(BF)
        start(t, r.base + YY)

    def r1(r, t):
        b = rem(t, 4)
        ahead, back = sides(t)
        arrive(t, r.base + XR)
        r.sx2[t] = (r.px[b, back] + r.rxr[t].astype(F32)).astype(BF)
        start(t, r.base + X2)
        arrive(t, r.base + YY)
        r.py[b, y] = r.py[b, y] + r.ryy[t].astype(F32)
        r.syd[t] = r.py[b, y, ahead].astype(BF)
        r.syr[t] = r.py[b, y, far].astype(BF)
        start(t, r.base + YD, r.base + YR)

    def r2(r, t):
        b = rem(t, 4)
        _, back = sides(t)
        arrive(t, r.base + XD, r.base + X2)
        r.px[b, x] = r.px[b, x] + r.rxd[t].astype(F32) + r.rx2[t].astype(F32)
        r.sxy[t] = r.px[b, x, :, pl.ds(pl.multiple_of(yo * 16, 16), 16), :].astype(BF)
        start(t, r.base + XY)
        arrive(t, r.base + YR)
        r.sy2[t] = (r.py[b, y, back] + r.ryr[t].astype(F32)).astype(BF)
        start(t, r.base + Y2)

    def r3x(r, t):
        b = rem(t, 4)
        arrive(t, r.base + XY)
        return r.px[b, x, :, pl.ds(pl.multiple_of(y * 16, 16), 16), :] + r.rxy[t].astype(F32)

    def r3y(r, t):
        b = rem(t, 4)
        arrive(t, r.base + YD, r.base + Y2)
        return r.py[b, y, x] + r.ryd[t].astype(F32) + r.ry2[t].astype(F32)

    def h0(u):
        arrive(u, CIN)
        r0(hg, u, [lax.dot_general(c2[tokh(u)], wd[...], (((1,), (1,)), ((), ())), preferred_element_type=F32)])

    def h3(u):
        c = tokh(u)
        hfx[c] = r3x(hg, u)[0]
        hfy[c] = r3y(hg, u)[0]

    def place(c, ends, starts, counts, owners):
        spot = lax.broadcasted_iota(jnp.int32, (128, 64), 0).astype(F32) + (c * 128).astype(F32)
        member = jnp.where((spot >= starts) & (spot < ends), 1.0, 0.0)

        def pick(values):
            return jnp.sum(member * values, axis=1, keepdims=True).astype(jnp.int32)

        count, begin = pick(counts), pick(starts)
        within = lax.broadcasted_iota(jnp.int32, (128, 1), 0) + c * 128 - begin
        first = (count + 1) >> 1
        second = within >= first
        slot = jnp.where(second, within - first, within)
        owner = jnp.where(second, pick(owners[1]), pick(owners[0]))
        index = jnp.where((owner & 7) == col, (owner >> 3) * 16 + slot, -1)
        hot[c] = jnp.where(lax.broadcasted_iota(jnp.int32, (128, 256), 1) == index, 1.0, 0.0).astype(BF)

    def find_places():
        counts = jnp.broadcast_to(counts_ref[...].astype(F32), (8, 64))
        owner = jnp.broadcast_to(owner_ref[...].astype(F32), (8, 128))
        upto = lax.broadcasted_iota(jnp.int32, (64, 64), 0) <= lax.broadcasted_iota(jnp.int32, (64, 64), 1)
        ends = jnp.dot(counts, jnp.where(upto, 1.0, 0.0), preferred_element_type=F32)
        starts = ends - counts
        i0 = lax.broadcasted_iota(jnp.int32, (128, 64), 0)
        i1 = lax.broadcasted_iota(jnp.int32, (128, 64), 1) * 2
        owners = [
            jnp.dot(owner, jnp.where(i0 == i1 + j, 1.0, 0.0), preferred_element_type=F32)[0:1] for j in range(2)
        ]

        def body(c, carry):
            place(c, ends[0:1], starts[0:1], counts[0:1], owners)
            return carry

        lax.fori_loop(0, 8, body, 0)

    def v_0():
        spread_all().wait_recv()
        rows = jnp.dot(hot[...].reshape(1024, 256), pool[...].reshape(256, 512), preferred_element_type=F32)
        part[...] = rows.astype(BF).reshape(2, 4, 128, 512)
        start1(RY, RZ1, RZ2, RZ3)

    def v_2():
        arrive1(RY)
        part[yh, :, :, 256:512] = part[yh, :, :, 256:512] + rty[...]
        start1(RYZ1, RYZ2, RYZ3)
        arrive1(RZ1, RZ2, RZ3)
        stz[...] = part[ho, z, :, 0:256] + rtz[0, ho] + rtz[1, ho] + rtz[2, ho]
        start1(RZY)

    def v_3():
        arrive1(RYZ1, RYZ2, RYZ3)
        xin[col, :, 256:512] = part[yh, z, :, 256:512] + rtyz[0] + rtyz[1] + rtyz[2]
        arrive1(RZY)
        xin[col, :, 0:256] = part[yh, z, :, 0:256] + rtz[0, yh] + rtz[1, yh] + rtz[2, yh] + rtzy[...]
        start1(TP, TM, TY)

    def t_0():
        arrive1(TM)
        start1(TF2)
        arrive1(TY)
        start1(UP, UM)
        arrive1(TP)
        start1(TF1)

    def t_2():
        arrive1(UP)
        start1(UF1)
        arrive1(UM)
        start1(UF2)

    def t_4():
        arrive1(UF1, UF2)

    def t_6():
        arrive1(TF1, TF2)

    def p0(t):
        start(t, XIN)

    def s0(t):
        arrive(t, XIN)
        c = tok(t)
        x_t = xin[c]
        xt[t] = x_t[:, 0:512].T
        pltpu.make_async_copy(xt.at[t], xt_ref.at[:, tokens(c)], osem.at[1]).start()
        r0(gu, t, [jnp.dot(x_t, w[...], preferred_element_type=F32) for w in (wg, wu)])

    def activate(c, full, hgrad, cols):
        gate, up = full[0], full[1]
        sigma = jax.nn.sigmoid(gate)
        act[c, x, y, 0, :, cols] = (gate * sigma * up).astype(BF)
        act[c, x, y, 1, :, cols] = (hgrad * up * sigma * (1.0 + gate * (1.0 - sigma))).astype(BF)
        act[c, x, y, 2, :, cols] = (hgrad * gate * sigma).astype(BF)

    def s3(t):
        c = tok(t)
        activate(c, r3x(gu, t), hfx[c], cx)
        start(t, AXY)
        activate(c, r3y(gu, t), hfy[c], cy)
        start(t, AYP, AYM)

        @pl.when(t == 7)
        def _():
            start1(AYL)

    def s4(t):
        arrive(t, AXY)
        start(t, AXP, AXM)

        @pl.when(t == 7)
        def _():
            start1(AXL)

        arrive(t, AYP)

        @pl.when(t < 7)
        def _():
            start(t, AYF)

        arrive(t, AYM)

        @pl.when(t == 7)
        def _():
            arrive1(AYL)
            start(t, AYY)

    def s5(t):
        arrive(t, AXP)

        @pl.when(t < 7)
        def _():
            start(t, AXF)

        arrive(t, AXM)

        @pl.when(t < 7)
        def _():
            arrive(t, AYF)
            start(t, AYY)

        @pl.when(t == 7)
        def _():
            arrive1(AXL)
            arrive(t, AYY)
            start(t, CORE)

    def s6(t):
        @pl.when(t < 7)
        def _():
            arrive(t, AXF, AYY)
            start(t, CORE)

        @pl.when(t == 7)
        def _():
            project(t)

    def s7(t):
        @pl.when(t < 7)
        def _():
            project(t)

    def project(t):
        c = tok(t)
        arrive(t, CORE)
        pltpu.make_async_copy(act.at[c, :, :, 1:3], o_ref.at[c], osem.at[0]).start()
        hidden = act[c, :, :, 0].reshape(128, 2 * HALF)
        lo[t] = jnp.dot(hidden, wdo[...], preferred_element_type=F32)

        @pl.when((t != 1) & (t != 7))
        def _():
            start(t, LOZ)

        ht[t] = hidden.T
        pltpu.make_async_copy(ht.at[t], ht_ref.at[:, tokens(c)], osem.at[2]).start()

    def s8(t):
        @pl.when(t == 4)
        def _():
            arrive(2, LOZ)
            arrive(3, LOZ)
            arrive(4, LOZ)
            zs[...] = lo[1] + rz[2] + rz[3] + rz[4]
            start1(LOY)

    def spread(i, carry):
        to = rem(row + i, 16)
        pltpu.make_async_remote_copy(
            src_ref=v_ref.at[:, pl.ds(pl.multiple_of(to * 512, 512), 512)],
            dst_ref=pool.at[row],
            send_sem=asem.at[0], recv_sem=asem.at[1], device_id={"row": to}, device_id_type=MESH,
        ).start()
        return carry

    def spread_all():
        return pltpu.make_async_remote_copy(
            src_ref=pool.at[0:15], dst_ref=pool.at[0:15], send_sem=asem.at[0], recv_sem=asem.at[1],
            device_id=y_dev, device_id_type=MESH,
        )

    def c_0():
        arrive1(CM)
        start1(CF2)
        arrive1(CY)
        start1(DP, DM)
        arrive1(CP)
        start1(CF1)

    def c_2():
        arrive1(DP)
        start1(DF1)
        arrive1(DM)
        start1(DF2)

    def c_4():
        arrive1(DF1, DF2)

    def c_6():
        arrive1(CF1, CF2)
        pltpu.make_async_copy(c2.at[:, :, 0:512], co_ref, lsem.at[4]).start()

    def w_0():
        here[0].wait()
        arrive1(WD)
        start1(WG, WU)

    def w_1():
        here[1].wait()
        here[2].wait()
        here[3].wait()
        arrive1(WG, WU)

    start(0, CIN)
    lax.fori_loop(1, 16, spread, 0)
    start1(WD, CP, CM, CY)
    find_places()
    for c in here[1:]:
        c.start()

    def each(n, lag, stage):
        t = n - lag

        @pl.when((t >= 0) & (t < CHUNKS))
        def _():
            stage(t)

    def at(n, when, stage):
        @pl.when(n == when)
        def _():
            stage()

    def step(n, carry):
        at(n, 0, w_0)
        for lag, stage in enumerate([h0, lambda u: r1(hg, u), lambda u: r2(hg, u), h3]):
            each(n, lag, stage)
        at(n, 0, c_0)
        at(n, 2, c_2)
        at(n, 4, c_4)
        at(n, 6, c_6)

        @pl.when(n < CHUNKS - 1)
        def _():
            start(n + 1, CIN)

        at(n, 0, v_0)
        at(n, 2, v_2)
        at(n, 3, v_3)
        at(n, FIRST, t_0)
        at(n, FIRST + 2, t_2)
        at(n, FIRST + 4, t_4)
        at(n, FIRST + 6, t_6)
        at(n, FIRST + 1, w_1)
        for lag, stage in [
            (0, p0), (1, s0), (2, lambda t: r1(gu, t)), (3, lambda t: r2(gu, t)), (4, s3), (5, s4), (6, s5),
            (8, s7), (7, s6), (9, s8),
        ]:
            each(n, FIRST + lag, stage)
        return carry

    lax.fori_loop(0, FIRST + CHUNKS + 7, step, 0)
    arrive(0, LOZ)
    arrive(5, LOZ)
    arrive(6, LOZ)
    arrive1(LOY)
    out_ref[...] = (lo[7] + rz[0] + rz[5] + rz[6] + rh[...]).astype(BF)

    def all_sent(kind):
        if kind < 16:
            r = gu if kind < HG else hg
            return (r.sxd, r.sxr, r.sx2, r.sxy, r.syy, r.syd, r.syr, r.sy2)[kind % HG]
        if kind in (AXP, AXM, AXF):
            return act.at[0:7 if kind == AXF else 8, x, :, :, :, cx]
        if kind in (AYP, AYM, AYF):
            return act.at[0:7 if kind == AYF else 8, x, y, :, :, cy]
        return {
            AXY: lambda: act.at[:, x, y, :, :, cx], AYY: lambda: act.at[:, :, y, :, :, cy],
            CORE: lambda: act.at[:, :, :, :, :, mine], XIN: lambda: xin.at[:, :, 0:512],
            CIN: lambda: c2.at[:, :, 0:512], LOZ: lambda: lo.at[0:6],
        }[kind]()

    for kind in range(KINDS):
        ref = all_sent(kind)
        copy(kind, 0, ref, ref, y_dev).wait_send()
    for kind in range(ONCE):
        src, dst, dev, _ = single[kind]()
        once(kind, src, dst, dev).wait_send()
    spread_all().wait_send()
    pltpu.make_async_copy(act.at[:, :, :, 1:3], o_ref, osem.at[0]).wait()
    pltpu.make_async_copy(xt, xt, osem.at[1]).wait()
    pltpu.make_async_copy(ht, ht, osem.at[2]).wait()
    pltpu.make_async_copy(c2.at[:, :, 0:512], co_ref, lsem.at[4]).wait()


def main_call(v, counts, owner, og, gate, up, down):
    n = CHUNKS
    vm = lambda *s: pltpu.VMEM(s, BF)
    vf = lambda *s: pltpu.VMEM(s, F32)

    def row_sum(mats):
        xb, xq, yb = (n, mats, 32, XW), (n, mats, 16, XW), (n, mats, 16, YW)
        moves = [vm(*xb), vm(*xb), vm(*xb), vm(*xq), vm(n, 4, mats, 16, YW), vm(*yb), vm(*yb), vm(*yb)]
        return [vf(4, 4, mats, 32, XW), vf(4, 2, 4, mats, 16, YW), *moves, *moves]

    dma = pltpu.SemaphoreType.DMA
    vmem = pl.BlockSpec(memory_space=pltpu.VMEM)
    hbm = pl.BlockSpec(memory_space=pl.ANY)
    return pl.pallas_call(
        main_kernel,
        out_shape=(
            jax.ShapeDtypeStruct((128, 512), BF),
            jax.ShapeDtypeStruct((n, 4, 2, 2, 16, 2 * HALF), BF),
            jax.ShapeDtypeStruct((2 * HALF, 1024), BF),
            jax.ShapeDtypeStruct((512, 1024), BF),
            jax.ShapeDtypeStruct((n, 128, 512), BF),
        ),
        in_specs=[vmem, vmem, vmem, vmem, hbm, hbm, hbm],
        out_specs=(vmem, hbm, hbm, hbm, hbm),
        scratch_shapes=[
            vm(n, 4, 2, 3, 16, 2 * HALF), vm(16, 16, 512), vm(n, 128, 1024), vm(n, 128, 1024),
            vm(1024, HALF), vm(1024, HALF), vm(HALF, 1024), vm(2 * HALF, 512),
            vm(8, 128, 256), vm(2, 4, 128, 512), vm(3, 2, 128, 256), vm(4, 128, 256), vm(128, 256), vm(3, 128, 256), vm(128, 256),
            vm(n, 2 * HALF, 128), vm(n, 512, 128),
            vf(n, 16, XW), vf(n, 16, YW),
            vf(n, 128, 512), vf(n, 128, 512), vf(128, 512), vf(128, 512),
            *row_sum(2), *row_sum(1),
            dma((KINDS,)), dma((KINDS, SLOTS)), dma((n,)), dma((ONCE,)), dma((ONCE,)), dma((2,)),
            dma((3,)), dma((5,)),
        ],
        compiler_params=pltpu.CompilerParams(
            collective_id=0, has_side_effects=True, vmem_limit_bytes=60 << 20
        ),
        cost_estimate=pl.CostEstimate(flops=10**10, bytes_accessed=30 * 10**6, transcendentals=0),
        name="row_sums",
    )(v, counts, owner, og, gate, up, down)


def grads_kernel(xt_ref, c_ref, ht_ref, o_ref, gate_ref, up_ref, down_ref, og, sem):
    step = pl.program_id(0)

    def fetch():
        return pltpu.make_async_copy(o_ref, og, sem)

    @pl.when(step == 0)
    def _():
        fetch().start()

    @pl.when(step < DOWN)
    def _():
        down_ref[...] = jnp.dot(ht_ref[...], c_ref[...].reshape(1024, 512), preferred_element_type=F32)

    @pl.when(step == DOWN)
    def _():
        fetch().wait()

    @pl.when((step >= DOWN) & (step < DOWN + 2))
    def _():
        gate_ref[...] = jnp.dot(xt_ref[...], og[:, :, :, 0].reshape(1024, 2 * HALF), preferred_element_type=F32)

    @pl.when(step >= DOWN + 2)
    def _():
        up_ref[...] = jnp.dot(xt_ref[...], og[:, :, :, 1].reshape(1024, 2 * HALF), preferred_element_type=F32)


DOWN = 4


def grads_call(xt, c, ht, o):
    n = CHUNKS
    rows = 2 * HALF // DOWN
    down = lambda j: (jnp.minimum(j, DOWN - 1), 0)
    gate = lambda j: (jnp.clip(j - DOWN, 0, 1), 0)
    up = lambda j: (jnp.clip(j - DOWN - 2, 0, 1), 0)
    return pl.pallas_call(
        grads_kernel,
        grid=(DOWN + 4,),
        out_shape=(
            jax.ShapeDtypeStruct((512, 2 * HALF), F32),
            jax.ShapeDtypeStruct((512, 2 * HALF), F32),
            jax.ShapeDtypeStruct((2 * HALF, 512), F32),
        ),
        in_specs=[
            pl.BlockSpec((256, 1024), lambda j: (jnp.maximum(j - DOWN, 0) % 2, 0)),
            pl.BlockSpec((n, 128, 512), lambda j: (0, 0, 0)),
            pl.BlockSpec((rows, 1024), down),
            pl.BlockSpec(memory_space=pl.ANY),
        ],
        out_specs=(
            pl.BlockSpec((256, 2 * HALF), gate),
            pl.BlockSpec((256, 2 * HALF), up),
            pl.BlockSpec((rows, 512), down),
        ),
        scratch_shapes=[pltpu.VMEM((n, 4, 2, 2, 16, 2 * HALF), BF), pltpu.SemaphoreType.DMA],
        compiler_params=pltpu.CompilerParams(vmem_limit_bytes=60 << 20),
        cost_estimate=pl.CostEstimate(flops=6 * 10**9, bytes_accessed=24 * 10**6, transcendentals=0),
        name="weight_grads",
    )(xt, c, ht, o)


def local(vision_tokens, image_counts, image_owner, gate_weight, up_weight, down_weight, out_grad):
    layer_out, o, ht, xt, c = main_call(
        vision_tokens, image_counts[None, :], image_owner[None, :], out_grad, gate_weight, up_weight, down_weight
    )
    grad_gate, grad_up, grad_down = grads_call(xt, c, ht, o)
    return (layer_out, grad_gate, grad_up, grad_down)


def solution(mesh):
    in_specs = (
        P(("row", "col"), None),
        P(),
        P(),
        P("row", "col"),
        P("row", "col"),
        P("col", "row"),
        P("col", "row"),
    )
    out_specs = (P("col", "row"), P("row", "col"), P("row", "col"), P("col", "row"))
    return jax.shard_map(local, mesh=mesh, in_specs=in_specs, out_specs=out_specs, check_vma=False)
```

```python
import functools
import jax
import jax.numpy as jnp
from jax import lax
from jax.experimental import pallas as pl
from jax.experimental.pallas import tpu as pltpu
from jax.sharding import PartitionSpec as P

BF = jnp.bfloat16
F32 = jnp.float32
MESH = pl.DeviceIdType.MESH

CHUNKS = 8
HALF = 896
XW = 512
YW = HALF - XW

XD, XR, X2, XY, YY, YD, YR, Y2 = range(8)
HG = 8
AXY, AXP, AXM, AXF, AYP, AYM, AYF, AYY, CORE, XIN, CIN, LOZ = range(16, 28)
KINDS = 28
CP, CM, CY, CF1, CF2, DP, DM, DF1, DF2 = range(9)
TP, TM, TY, TF1, TF2, UP, UM, UF1, UF2 = range(9, 18)
RZ1, RZ2, RZ3, RZY, RY, RYZ1, RYZ2, RYZ3 = range(18, 26)
WG, WU, WD, LOY, AXL, AYL = range(26, 32)
ONCE = 32
SLOTS = 4
FIRST = 4

def rem(a, n):
    return lax.rem(a, n)


class RowSum:
    def __init__(self, base, refs):
        self.base = base
        (self.px, self.py, self.sxd, self.sxr, self.sx2, self.sxy, self.syy, self.syd, self.syr,
         self.sy2, self.rxd, self.rxr, self.rx2, self.rxy, self.ryy, self.ryd, self.ryr, self.ry2) = refs


def main_kernel(
    v_ref, counts_ref, owner_ref, og_ref, gate_hbm, up_hbm, down_hbm,
    out_ref, o_ref, ht_ref, xt_ref, co_ref,
    act, pool, xin, c2, wg, wu, wd, wdo,
    hot, part, rtz, rty, stz, rtyz, rtzy, ht, xt,
    hfx, hfy, lo, rz, zs, rh,
    *rest,
):
    gu, hg = RowSum(0, rest[:18]), RowSum(HG, rest[18:36])
    ssem, rsem, hsem, ssem1, rsem1, asem, osem, lsem = rest[36:]
    row = lax.axis_index("row")
    col = lax.axis_index("col")
    x, y, k = row // 4, rem(row // 2, 2), rem(row, 2)
    yh, z = col // 4, rem(col, 4)
    yo, ko, ho = 1 - y, 1 - k, 1 - yh
    far = rem(x + 2, 4)
    zp, zm, zf = rem(z + 1, 4), rem(z + 3, 4), rem(z + 2, 4)

    def at_row(xx, yy, kk):
        return {"row": xx * 4 + yy * 2 + kk}

    def at_col(hh, zz):
        return {"col": hh * 4 + zz}

    y_dev, core_dev = at_row(x, yo, k), at_row(x, y, ko)
    far_dev = at_row(far, y, k)
    up_dev, down_dev, hi_dev = at_col(yh, zp), at_col(yh, zm), at_col(ho, z)
    barrier = pltpu.get_barrier_semaphore()

    def greet(i, carry):
        pl.semaphore_signal(barrier, inc=1, device_id={"row": rem(row + i, 16)}, device_id_type=MESH)
        return carry

    lax.fori_loop(1, 16, greet, 0)
    for dev in (up_dev, down_dev, at_col(yh, zf), hi_dev):
        pl.semaphore_signal(barrier, inc=1, device_id=dev, device_id_type=MESH)

    mine = pl.ds(pl.multiple_of(k * HALF, 128), HALF)
    theirs = pl.ds(pl.multiple_of(ko * HALF, 128), HALF)
    here = [
        pltpu.make_async_copy(down_hbm.at[mine, :], wd.at[:, 0:512], lsem.at[0]),
        pltpu.make_async_copy(gate_hbm.at[:, mine], wg.at[0:512, :], lsem.at[1]),
        pltpu.make_async_copy(up_hbm.at[:, mine], wu.at[0:512, :], lsem.at[2]),
        pltpu.make_async_copy(down_hbm, wdo, lsem.at[3]),
    ]
    here[0].start()
    c2[col, :, 0:512] = og_ref[...]
    pool[row] = v_ref[:, pl.ds(pl.multiple_of(row * 512, 512), 512)]
    pl.semaphore_wait(barrier, 19)

    cx = pl.ds(pl.multiple_of(k * HALF, 128), XW)
    cy = pl.ds(pl.multiple_of(k * HALF + XW, 128), YW)

    def landing(kind, t):
        if HG <= kind < AXY:
            return hsem.at[kind - HG, t]
        if kind in (CIN, LOZ):
            return hsem.at[8 + (kind == LOZ), t]
        return rsem.at[kind, rem(t, SLOTS)]

    def copy(kind, t, src, dst, dev):
        return pltpu.make_async_remote_copy(
            src_ref=src, dst_ref=dst, send_sem=ssem.at[kind], recv_sem=landing(kind, t),
            device_id=dev, device_id_type=MESH,
        )

    def once(kind, src, dst, dev):
        return pltpu.make_async_remote_copy(
            src_ref=src, dst_ref=dst, send_sem=ssem1.at[kind], recv_sem=rsem1.at[kind],
            device_id=dev, device_id_type=MESH,
        )

    def same(ref):
        return ref, ref

    def cblk(hh, zz, at=0, n=128):
        return c2.at[hh * 4 + zz, at:at + n, 0:512]

    def tblk(hh, zz, at=0, n=128):
        return xin.at[hh * 4 + zz, at:at + n, 0:512]

    single = {
        WD: lambda: (down_hbm.at[theirs, :], wd.at[:, 512:1024], core_dev, wd.at[:, 512:1024]),
        WG: lambda: (gate_hbm.at[:, theirs], wg.at[512:1024, :], core_dev, wg.at[512:1024, :]),
        WU: lambda: (up_hbm.at[:, theirs], wu.at[512:1024, :], core_dev, wu.at[512:1024, :]),
        CP: lambda: (*same(cblk(yh, z)), up_dev, cblk(yh, zm)),
        CM: lambda: (*same(cblk(yh, z)), down_dev, cblk(yh, zp)),
        CY: lambda: (*same(cblk(yh, z)), hi_dev, cblk(ho, z)),
        CF1: lambda: (*same(cblk(yh, zm, 0, 64)), up_dev, cblk(yh, zf, 0, 64)),
        CF2: lambda: (*same(cblk(yh, zp, 64, 64)), down_dev, cblk(yh, zf, 64, 64)),
        DP: lambda: (*same(cblk(ho, z)), up_dev, cblk(ho, zm)),
        DM: lambda: (*same(cblk(ho, z)), down_dev, cblk(ho, zp)),
        DF1: lambda: (*same(cblk(ho, zm, 0, 64)), up_dev, cblk(ho, zf, 0, 64)),
        DF2: lambda: (*same(cblk(ho, zp, 64, 64)), down_dev, cblk(ho, zf, 64, 64)),
        TP: lambda: (*same(tblk(yh, z)), up_dev, tblk(yh, zm)),
        TM: lambda: (*same(tblk(yh, z)), down_dev, tblk(yh, zp)),
        TY: lambda: (*same(tblk(yh, z)), hi_dev, tblk(ho, z)),
        TF1: lambda: (*same(tblk(yh, zm, 0, 64)), up_dev, tblk(yh, zf, 0, 64)),
        TF2: lambda: (*same(tblk(yh, zp, 64, 64)), down_dev, tblk(yh, zf, 64, 64)),
        UP: lambda: (*same(tblk(ho, z)), up_dev, tblk(ho, zm)),
        UM: lambda: (*same(tblk(ho, z)), down_dev, tblk(ho, zp)),
        UF1: lambda: (*same(tblk(ho, zm, 0, 64)), up_dev, tblk(ho, zf, 0, 64)),
        UF2: lambda: (*same(tblk(ho, zp, 64, 64)), down_dev, tblk(ho, zf, 64, 64)),
        RZ1: lambda: (part.at[:, zp, :, 0:256], rtz.at[0], at_col(yh, zp), rtz.at[0]),
        RZ2: lambda: (part.at[:, zf, :, 0:256], rtz.at[1], at_col(yh, zf), rtz.at[1]),
        RZ3: lambda: (part.at[:, zm, :, 0:256], rtz.at[2], at_col(yh, zm), rtz.at[2]),
        RZY: lambda: (stz, rtzy, hi_dev, rtzy),
        RY: lambda: (part.at[ho, :, :, 256:512], rty, hi_dev, rty),
        RYZ1: lambda: (part.at[yh, zp, :, 256:512], rtyz.at[0], at_col(yh, zp), rtyz.at[0]),
        RYZ2: lambda: (part.at[yh, zf, :, 256:512], rtyz.at[1], at_col(yh, zf), rtyz.at[1]),
        RYZ3: lambda: (part.at[yh, zm, :, 256:512], rtyz.at[2], at_col(yh, zm), rtyz.at[2]),
        LOY: lambda: (zs, rh, hi_dev, rh),
        AXL: lambda: (*same(act.at[col, x, :, :, :, cx]), far_dev, act.at[col, far, :, :, :, cx]),
        AYL: lambda: (*same(act.at[col, x, y, :, :, cy]), far_dev, act.at[col, far, y, :, :, cy]),
    }

    def start1(*kinds):
        for kind in kinds:
            src, dst, dev, _ = single[kind]()
            once(kind, src, dst, dev).start()

    def arrive1(*kinds):
        for kind in kinds:
            place = single[kind]()[3]
            once(kind, place, place, y_dev).wait_recv()

    def sides(t):
        s = 1 - 2 * rem(t, 2)
        return rem(x + s + 4, 4), rem(x - s + 4, 4)

    def tokh(u):
        there = jnp.where((u < 3) | (u == 6), yh, ho)
        off = jnp.where((u == 1) | (u == 4), 1, 0)
        off = off + jnp.where((u == 2) | (u == 5), 3, 0) + jnp.where(u >= 6, 2, 0)
        return there * 4 + rem(z + off, 4)

    def tok(t):
        there = jnp.where((t >= 1) & (t < 5), ho, yh)
        off = jnp.where((t == 0) | (t == 2), 1, 0)
        off = off + jnp.where((t == 3) | (t == 5), 3, 0) + jnp.where((t == 4) | (t == 6), 2, 0)
        return there * 4 + rem(z + off, 4)

    def tokens(c):
        return pl.ds(pl.multiple_of(c * 128, 128), 128)

    def table(kind, t):
        ahead, back = sides(t)
        to_ahead, to_back = at_row(ahead, y, k), at_row(back, y, k)
        if kind < 16:
            r = gu if kind < HG else hg
            src, dst, dev = {
                XD: lambda: (r.sxd, r.rxd, to_ahead), XR: lambda: (r.sxr, r.rxr, to_back),
                X2: lambda: (r.sx2, r.rx2, to_back), XY: lambda: (r.sxy, r.rxy, y_dev),
                YY: lambda: (r.syy, r.ryy, y_dev), YD: lambda: (r.syd, r.ryd, to_ahead),
                YR: lambda: (r.syr, r.ryr, to_back), Y2: lambda: (r.sy2, r.ry2, to_back),
            }[kind % HG]()
            return src.at[t], dst.at[t], dev, dst.at[t]
        if kind == CIN:
            c = tokh(t)
            return c2.at[c, :, 0:512], c2.at[c, :, 512:1024], core_dev, c2.at[c, :, 512:1024]
        c = tok(t)
        return {
            AXY: lambda: (*same(act.at[c, x, y, :, :, cx]), y_dev, act.at[c, x, yo, :, :, cx]),
            AXP: lambda: (*same(act.at[c, x, :, :, :, cx]), to_ahead, act.at[c, back, :, :, :, cx]),
            AXM: lambda: (*same(act.at[c, x, :, :, :, cx]), to_back, act.at[c, ahead, :, :, :, cx]),
            AXF: lambda: (*same(act.at[c, back, :, :, :, cx]), to_ahead, act.at[c, far, :, :, :, cx]),
            AYP: lambda: (*same(act.at[c, x, y, :, :, cy]), to_ahead, act.at[c, back, y, :, :, cy]),
            AYM: lambda: (*same(act.at[c, x, y, :, :, cy]), to_back, act.at[c, ahead, y, :, :, cy]),
            AYF: lambda: (*same(act.at[c, back, y, :, :, cy]), to_ahead, act.at[c, far, y, :, :, cy]),
            AYY: lambda: (*same(act.at[c, :, y, :, :, cy]), y_dev, act.at[c, :, yo, :, :, cy]),
            CORE: lambda: (*same(act.at[c, :, :, :, :, mine]), core_dev, act.at[c, :, :, :, :, theirs]),
            XIN: lambda: (xin.at[c, :, 0:512], xin.at[c, :, 512:1024], core_dev, xin.at[c, :, 512:1024]),
            LOZ: lambda: (lo.at[t], rz.at[t], at_col(yh, rem(c, 4)), rz.at[t]),
        }[kind]()

    def start(t, *kinds):
        for kind in kinds:
            src, dst, dev, _ = table(kind, t)
            copy(kind, t, src, dst, dev).start()

    def arrive(t, *kinds):
        for kind in kinds:
            place = table(kind, t)[3]
            copy(kind, t, place, place, y_dev).wait_recv()

    def r0(r, t, parts):
        b = t
        ahead, _ = sides(t)
        for m, g in enumerate(parts):
            r.px[b, :, m] = g[:, :XW].reshape(4, 32, XW)
            gy = g[:, XW:].reshape(4, 2, 16, YW)
            for yy in range(2):
                r.py[b, yy, :, m] = gy[:, yy]
        r.sxd[t] = r.px[b, ahead].astype(BF)
        r.sxr[t] = r.px[b, far].astype(BF)
        start(t, r.base + XD, r.base + XR)
        r.syy[t] = r.py[b, yo].astype(BF)
        start(t, r.base + YY)

    def r1(r, t):
        b = t
        ahead, back = sides(t)
        arrive(t, r.base + XR)
        r.sx2[t] = (r.px[b, back] + r.rxr[t].astype(F32)).astype(BF)
        start(t, r.base + X2)
        arrive(t, r.base + YY)
        r.py[b, y] = r.py[b, y] + r.ryy[t].astype(F32)
        r.syd[t] = r.py[b, y, ahead].astype(BF)
        r.syr[t] = r.py[b, y, far].astype(BF)
        start(t, r.base + YD, r.base + YR)

    def r2(r, t):
        b = t
        _, back = sides(t)
        arrive(t, r.base + XD, r.base + X2)
        r.px[b, x] = r.px[b, x] + r.rxd[t].astype(F32) + r.rx2[t].astype(F32)
        r.sxy[t] = r.px[b, x, :, pl.ds(pl.multiple_of(yo * 16, 16), 16), :].astype(BF)
        start(t, r.base + XY)
        arrive(t, r.base + YR)
        r.sy2[t] = (r.py[b, y, back] + r.ryr[t].astype(F32)).astype(BF)
        start(t, r.base + Y2)

    def r3x(r, t):
        b = t
        arrive(t, r.base + XY)
        return r.px[b, x, :, pl.ds(pl.multiple_of(y * 16, 16), 16), :] + r.rxy[t].astype(F32)

    def r3y(r, t):
        b = t
        arrive(t, r.base + YD, r.base + Y2)
        return r.py[b, y, x] + r.ryd[t].astype(F32) + r.ry2[t].astype(F32)

    def h0(u):
        arrive(u, CIN)
        r0(hg, u, [lax.dot_general(c2[tokh(u)], wd[...], (((1,), (1,)), ((), ())), preferred_element_type=F32)])

    def h3(u):
        c = tokh(u)
        hfx[c] = r3x(hg, u)[0]
        hfy[c] = r3y(hg, u)[0]

    def place(c, ends, starts, counts, owners):
        spot = lax.broadcasted_iota(jnp.int32, (128, 64), 0).astype(F32) + (c * 128).astype(F32)
        member = jnp.where((spot >= starts) & (spot < ends), 1.0, 0.0)

        def pick(values):
            return jnp.sum(member * values, axis=1, keepdims=True).astype(jnp.int32)

        count, begin = pick(counts), pick(starts)
        within = lax.broadcasted_iota(jnp.int32, (128, 1), 0) + c * 128 - begin
        first = (count + 1) >> 1
        second = within >= first
        slot = jnp.where(second, within - first, within)
        owner = jnp.where(second, pick(owners[1]), pick(owners[0]))
        index = jnp.where((owner & 7) == col, (owner >> 3) * 16 + slot, -1)
        hot[c] = jnp.where(lax.broadcasted_iota(jnp.int32, (128, 256), 1) == index, 1.0, 0.0).astype(BF)

    def find_places():
        counts = jnp.broadcast_to(counts_ref[...].astype(F32), (8, 64))
        owner = jnp.broadcast_to(owner_ref[...].astype(F32), (8, 128))
        upto = lax.broadcasted_iota(jnp.int32, (64, 64), 0) <= lax.broadcasted_iota(jnp.int32, (64, 64), 1)
        ends = jnp.dot(counts, jnp.where(upto, 1.0, 0.0), preferred_element_type=F32)
        starts = ends - counts
        i0 = lax.broadcasted_iota(jnp.int32, (128, 64), 0)
        i1 = lax.broadcasted_iota(jnp.int32, (128, 64), 1) * 2
        owners = [
            jnp.dot(owner, jnp.where(i0 == i1 + j, 1.0, 0.0), preferred_element_type=F32)[0:1] for j in range(2)
        ]

        def body(c, carry):
            place(c, ends[0:1], starts[0:1], counts[0:1], owners)
            return carry

        lax.fori_loop(0, 8, body, 0)

    def v_0():
        spread_all().wait_recv()
        rows = jnp.dot(hot[...].reshape(1024, 256), pool[...].reshape(256, 512), preferred_element_type=F32)
        part[...] = rows.astype(BF).reshape(2, 4, 128, 512)
        start1(RY, RZ1, RZ2, RZ3)

    def v_2():
        arrive1(RY)
        part[yh, :, :, 256:512] = part[yh, :, :, 256:512] + rty[...]
        start1(RYZ1, RYZ2, RYZ3)
        arrive1(RZ1, RZ2, RZ3)
        stz[...] = part[ho, z, :, 0:256] + rtz[0, ho] + rtz[1, ho] + rtz[2, ho]
        start1(RZY)

    def v_3():
        arrive1(RYZ1, RYZ2, RYZ3)
        xin[col, :, 256:512] = part[yh, z, :, 256:512] + rtyz[0] + rtyz[1] + rtyz[2]
        arrive1(RZY)
        xin[col, :, 0:256] = part[yh, z, :, 0:256] + rtz[0, yh] + rtz[1, yh] + rtz[2, yh] + rtzy[...]
        start1(TP, TM, TY)

    def t_0():
        arrive1(TM)
        start1(TF2)
        arrive1(TY)
        start1(UP, UM)
        arrive1(TP)
        start1(TF1)

    def t_2():
        arrive1(UP)
        start1(UF1)
        arrive1(UM)
        start1(UF2)

    def t_4():
        arrive1(UF1, UF2)

    def t_6():
        arrive1(TF1, TF2)

    def p0(t):
        start(t, XIN)

    def s0(t):
        arrive(t, XIN)
        c = tok(t)
        x_t = xin[c]
        xt[t] = x_t[:, 0:512].T
        pltpu.make_async_copy(xt.at[t], xt_ref.at[:, tokens(c)], osem.at[1]).start()
        r0(gu, t, [jnp.dot(x_t, w[...], preferred_element_type=F32) for w in (wg, wu)])

    def activate(c, full, hgrad, cols):
        gate, up = full[0], full[1]
        sigma = jax.nn.sigmoid(gate)
        act[c, x, y, 0, :, cols] = (gate * sigma * up).astype(BF)
        act[c, x, y, 1, :, cols] = (hgrad * up * sigma * (1.0 + gate * (1.0 - sigma))).astype(BF)
        act[c, x, y, 2, :, cols] = (hgrad * gate * sigma).astype(BF)

    def s3(t):
        c = tok(t)
        activate(c, r3x(gu, t), hfx[c], cx)
        start(t, AXY)
        activate(c, r3y(gu, t), hfy[c], cy)
        start(t, AYP, AYM)

        @pl.when(t == 7)
        def _():
            start1(AYL)

    def s4(t):
        arrive(t, AXY)
        start(t, AXP, AXM)

        @pl.when(t == 7)
        def _():
            start1(AXL)

        arrive(t, AYP)

        @pl.when(t < 7)
        def _():
            start(t, AYF)

        arrive(t, AYM)

        @pl.when(t == 7)
        def _():
            arrive1(AYL)
            start(t, AYY)

    def s5(t):
        arrive(t, AXP)

        @pl.when(t < 7)
        def _():
            start(t, AXF)

        arrive(t, AXM)

        @pl.when(t < 7)
        def _():
            arrive(t, AYF)
            start(t, AYY)

        @pl.when(t == 7)
        def _():
            arrive1(AXL)
            arrive(t, AYY)
            start(t, CORE)

    def s6(t):
        @pl.when(t < 7)
        def _():
            arrive(t, AXF, AYY)
            start(t, CORE)

        @pl.when(t == 7)
        def _():
            project(t)

    def s7(t):
        @pl.when(t < 7)
        def _():
            project(t)

    def project(t):
        c = tok(t)
        arrive(t, CORE)
        pltpu.make_async_copy(act.at[c, :, :, 1:3], o_ref.at[c], osem.at[0]).start()
        hidden = act[c, :, :, 0].reshape(128, 2 * HALF)
        lo[t] = jnp.dot(hidden, wdo[...], preferred_element_type=F32)

        @pl.when((t != 1) & (t != 7))
        def _():
            start(t, LOZ)

        ht[t] = hidden.T
        pltpu.make_async_copy(ht.at[t], ht_ref.at[:, tokens(c)], osem.at[2]).start()

    def s8(t):
        @pl.when(t == 4)
        def _():
            arrive(2, LOZ)
            arrive(3, LOZ)
            arrive(4, LOZ)
            zs[...] = lo[1] + rz[2] + rz[3] + rz[4]
            start1(LOY)

    def spread(i, carry):
        to = rem(row + i, 16)
        pltpu.make_async_remote_copy(
            src_ref=v_ref.at[:, pl.ds(pl.multiple_of(to * 512, 512), 512)],
            dst_ref=pool.at[row],
            send_sem=asem.at[0], recv_sem=asem.at[1], device_id={"row": to}, device_id_type=MESH,
        ).start()
        return carry

    def spread_all():
        return pltpu.make_async_remote_copy(
            src_ref=pool.at[0:15], dst_ref=pool.at[0:15], send_sem=asem.at[0], recv_sem=asem.at[1],
            device_id=y_dev, device_id_type=MESH,
        )

    def c_0():
        arrive1(CM)
        start1(CF2)
        arrive1(CP)
        start1(CF1)
        start(1, CIN)
        start(2, CIN)
        arrive1(CY)
        start1(DP, DM)
        start(3, CIN)

    def c_1():
        arrive1(DM)
        start1(DF2)
        arrive1(DP)
        start1(DF1)
        start(4, CIN)

    def c_2():
        arrive1(CF1, CF2)
        start(5, CIN)
        start(6, CIN)

    def c_3():
        arrive1(DF1, DF2)
        start(7, CIN)
        pltpu.make_async_copy(c2.at[:, :, 0:512], co_ref, lsem.at[4]).start()

    def w_0():
        here[0].wait()
        arrive1(WD)
        start1(WG, WU)

    def w_1():
        here[1].wait()
        here[2].wait()
        here[3].wait()
        arrive1(WG, WU)

    start(0, CIN)
    lax.fori_loop(1, 16, spread, 0)
    start1(WD, CP, CM, CY)
    find_places()
    for c in here[1:]:
        c.start()

    def each(n, lag, stage):
        t = n - lag

        @pl.when((t >= 0) & (t < CHUNKS))
        def _():
            stage(t)

    def at(n, when, stage):
        @pl.when(n == when)
        def _():
            stage()

    def step(n, carry):
        at(n, 0, w_0)
        for lag, stage in enumerate([h0, lambda u: r1(hg, u), lambda u: r2(hg, u), h3]):
            each(2 * (n - lag) - 1, 0, stage)
            each(2 * (n - lag), 0, stage)
        at(n, 0, c_0)
        at(n, 1, c_1)
        at(n, 2, c_2)
        at(n, 3, c_3)
        at(n, 0, v_0)
        at(n, 2, v_2)
        at(n, 3, v_3)
        at(n, FIRST, t_0)
        at(n, FIRST + 2, t_2)
        at(n, FIRST + 4, t_4)
        at(n, FIRST + 6, t_6)
        at(n, FIRST + 1, w_1)
        for lag, stage in [
            (0, p0), (1, s0), (2, lambda t: r1(gu, t)), (3, lambda t: r2(gu, t)), (4, s3), (5, s4), (6, s5),
            (8, s7), (7, s6), (9, s8),
        ]:
            each(n, FIRST + lag, stage)
        return carry

    lax.fori_loop(0, FIRST + CHUNKS + 7, step, 0)
    arrive(0, LOZ)
    arrive(5, LOZ)
    arrive(6, LOZ)
    arrive1(LOY)
    out_ref[...] = (lo[7] + rz[0] + rz[5] + rz[6] + rh[...]).astype(BF)

    def all_sent(kind):
        if kind < 16:
            r = gu if kind < HG else hg
            return (r.sxd, r.sxr, r.sx2, r.sxy, r.syy, r.syd, r.syr, r.sy2)[kind % HG]
        if kind in (AXP, AXM, AXF):
            return act.at[0:7 if kind == AXF else 8, x, :, :, :, cx]
        if kind in (AYP, AYM, AYF):
            return act.at[0:7 if kind == AYF else 8, x, y, :, :, cy]
        return {
            AXY: lambda: act.at[:, x, y, :, :, cx], AYY: lambda: act.at[:, :, y, :, :, cy],
            CORE: lambda: act.at[:, :, :, :, :, mine], XIN: lambda: xin.at[:, :, 0:512],
            CIN: lambda: c2.at[:, :, 0:512], LOZ: lambda: lo.at[0:6],
        }[kind]()

    for kind in range(KINDS):
        ref = all_sent(kind)
        copy(kind, 0, ref, ref, y_dev).wait_send()
    for kind in range(ONCE):
        src, dst, dev, _ = single[kind]()
        once(kind, src, dst, dev).wait_send()
    spread_all().wait_send()
    pltpu.make_async_copy(act.at[:, :, :, 1:3], o_ref, osem.at[0]).wait()
    pltpu.make_async_copy(xt, xt, osem.at[1]).wait()
    pltpu.make_async_copy(ht, ht, osem.at[2]).wait()
    pltpu.make_async_copy(c2.at[:, :, 0:512], co_ref, lsem.at[4]).wait()


def main_call(v, counts, owner, og, gate, up, down):
    n = CHUNKS
    vm = lambda *s: pltpu.VMEM(s, BF)
    vf = lambda *s: pltpu.VMEM(s, F32)

    def row_sum(mats):
        xb, xq, yb = (n, mats, 32, XW), (n, mats, 16, XW), (n, mats, 16, YW)
        moves = [vm(*xb), vm(*xb), vm(*xb), vm(*xq), vm(n, 4, mats, 16, YW), vm(*yb), vm(*yb), vm(*yb)]
        return [vf(8, 4, mats, 32, XW), vf(8, 2, 4, mats, 16, YW), *moves, *moves]

    dma = pltpu.SemaphoreType.DMA
    vmem = pl.BlockSpec(memory_space=pltpu.VMEM)
    hbm = pl.BlockSpec(memory_space=pl.ANY)
    return pl.pallas_call(
        main_kernel,
        out_shape=(
            jax.ShapeDtypeStruct((128, 512), BF),
            jax.ShapeDtypeStruct((n, 4, 2, 2, 16, 2 * HALF), BF),
            jax.ShapeDtypeStruct((2 * HALF, 1024), BF),
            jax.ShapeDtypeStruct((512, 1024), BF),
            jax.ShapeDtypeStruct((n, 128, 512), BF),
        ),
        in_specs=[vmem, vmem, vmem, vmem, hbm, hbm, hbm],
        out_specs=(vmem, hbm, hbm, hbm, hbm),
        scratch_shapes=[
            vm(n, 4, 2, 3, 16, 2 * HALF), vm(16, 16, 512), vm(n, 128, 1024), vm(n, 128, 1024),
            vm(1024, HALF), vm(1024, HALF), vm(HALF, 1024), vm(2 * HALF, 512),
            vm(8, 128, 256), vm(2, 4, 128, 512), vm(3, 2, 128, 256), vm(4, 128, 256), vm(128, 256), vm(3, 128, 256), vm(128, 256),
            vm(n, 2 * HALF, 128), vm(n, 512, 128),
            vf(n, 16, XW), vf(n, 16, YW),
            vf(n, 128, 512), vf(n, 128, 512), vf(128, 512), vf(128, 512),
            *row_sum(2), *row_sum(1),
            dma((KINDS,)), dma((KINDS, SLOTS)), dma((10, n)), dma((ONCE,)), dma((ONCE,)), dma((2,)),
            dma((3,)), dma((5,)),
        ],
        compiler_params=pltpu.CompilerParams(
            collective_id=0, has_side_effects=True, vmem_limit_bytes=60 << 20
        ),
        cost_estimate=pl.CostEstimate(flops=10**10, bytes_accessed=30 * 10**6, transcendentals=0),
        name="row_sums",
    )(v, counts, owner, og, gate, up, down)


def grads_kernel(xt_hbm, c_hbm, ht_hbm, o_hbm, gate_hbm, up_hbm, down_hbm, xt, c, ht, o, gate, up, down, lsem, wsem):
    load = pltpu.make_async_copy
    strips = [slice(0, HALF), slice(HALF, 2 * HALF)]
    x_in, c_in = load(xt_hbm, xt, lsem.at[0]), load(c_hbm, c, lsem.at[1])
    ht_in = [load(ht_hbm.at[s], ht.at[s], lsem.at[2 + i]) for i, s in enumerate(strips)]
    o_in = [
        [load(o_hbm.at[:, :, :, m, :, s], o.at[:, :, :, m, :, s], lsem.at[4 + 2 * i + m]) for m in range(2)]
        for i, s in enumerate(strips)
    ]
    c_in.start()
    ht_in[0].start()
    x_in.start()
    for copies in (o_in[0], ht_in[1:], o_in[1]):
        for copy in copies:
            copy.start()
    out = []

    def write(src, dst):
        out.append(pltpu.make_async_copy(src, dst, wsem.at[len(out)]))
        out[-1].start()

    c_in.wait()
    for i, s in enumerate(strips):
        ht_in[i].wait()
        down[s] = jnp.dot(ht[s], c[...].reshape(1024, 512), preferred_element_type=F32)
        write(down.at[s], down_hbm.at[s])
        if i == 0:
            x_in.wait()
        for m, (grad, hbm) in enumerate(((gate, gate_hbm), (up, up_hbm))):
            o_in[i][m].wait()
            grad[:, s] = jnp.dot(xt[...], o[:, :, :, m, :, s].reshape(1024, HALF), preferred_element_type=F32)
            write(grad.at[:, s], hbm.at[:, s])
    for copy in out:
        copy.wait()


def grads_call(xt, c, ht, o):
    hbm = pl.BlockSpec(memory_space=pl.ANY)
    up, down = (512, 2 * HALF), (2 * HALF, 512)
    return pl.pallas_call(
        grads_kernel,
        out_shape=tuple(jax.ShapeDtypeStruct(shape, F32) for shape in (up, up, down)),
        in_specs=[hbm] * 4,
        out_specs=(hbm, hbm, hbm),
        scratch_shapes=[
            *(pltpu.VMEM(a.shape, BF) for a in (xt, c, ht, o)),
            *(pltpu.VMEM(shape, F32) for shape in (up, up, down)),
            pltpu.SemaphoreType.DMA((8,)), pltpu.SemaphoreType.DMA((6,)),
        ],
        compiler_params=pltpu.CompilerParams(vmem_limit_bytes=60 << 20),
        cost_estimate=pl.CostEstimate(flops=8 * 10**9, bytes_accessed=24 * 10**6, transcendentals=0),
        name="weight_grads",
    )(xt, c, ht, o)


def local(vision_tokens, image_counts, image_owner, gate_weight, up_weight, down_weight, out_grad):
    layer_out, o, ht, xt, c = main_call(
        vision_tokens, image_counts[None, :], image_owner[None, :], out_grad, gate_weight, up_weight, down_weight
    )
    grad_gate, grad_up, grad_down = grads_call(xt, c, ht, o)
    return (layer_out, grad_gate, grad_up, grad_down)


def solution(mesh):
    in_specs = (
        P(("row", "col"), None),
        P(),
        P(),
        P("row", "col"),
        P("row", "col"),
        P("col", "row"),
        P("col", "row"),
    )
    out_specs = (P("col", "row"), P("row", "col"), P("row", "col"), P("col", "row"))
    return jax.shard_map(local, mesh=mesh, in_specs=in_specs, out_specs=out_specs, check_vma=False)
```

```python
import functools
import jax
import jax.numpy as jnp
from jax import lax
from jax.experimental import pallas as pl
from jax.experimental.pallas import tpu as pltpu
from jax.sharding import PartitionSpec as P

BF = jnp.bfloat16
F32 = jnp.float32
MESH = pl.DeviceIdType.MESH

CHUNKS = 8
HALF = 896
XW = 512
YW = HALF - XW

XD, XR, X2, XY, YY, YD, YR, Y2 = range(8)
HG = 8
AXY, AXP, AXM, AXF, AYP, AYM, AYF, AYY, CORE, XIN, CIN, LOZ = range(16, 28)
KINDS = 28
CP, CM, CY, CF1, CF2, DP, DM, DF1, DF2 = range(9)
TP, TM, TY, TF1, TF2, UP, UM, UF1, UF2 = range(9, 18)
RZ1, RZ2, RZ3, RZY, RY, RYZ1, RYZ2, RYZ3 = range(18, 26)
WG, WU, WD, LOY, AXL, AYL, LO6 = range(26, 33)
ONCE = 33
SLOTS = 4
FIRST = 4

def rem(a, n):
    return lax.rem(a, n)


class RowSum:
    def __init__(self, base, refs):
        self.base = base
        (self.px, self.py, self.sxd, self.sxr, self.sx2, self.sxy, self.syy, self.syd, self.syr,
         self.sy2, self.rxd, self.rxr, self.rx2, self.rxy, self.ryy, self.ryd, self.ryr, self.ry2) = refs


def main_kernel(
    v_ref, counts_ref, owner_ref, og_ref, gate_hbm, up_hbm, down_hbm,
    out_ref, o_ref, ht_ref, xt_ref, co_ref,
    act, pool, xin, c2, wg, wu, wd, wdo,
    hot, part, rtz, rty, stz, rtyz, rtzy, ht, xt,
    hfx, hfy, lo, rz, zs, rh, lo6, rz6,
    *rest,
):
    gu, hg = RowSum(0, rest[:18]), RowSum(HG, rest[18:36])
    ssem, rsem, hsem, ssem1, rsem1, asem, osem, lsem = rest[36:]
    row = lax.axis_index("row")
    col = lax.axis_index("col")
    x, y, k = row // 4, rem(row // 2, 2), rem(row, 2)
    yh, z = col // 4, rem(col, 4)
    yo, ko, ho = 1 - y, 1 - k, 1 - yh
    far = rem(x + 2, 4)
    zp, zm, zf = rem(z + 1, 4), rem(z + 3, 4), rem(z + 2, 4)

    def at_row(xx, yy, kk):
        return {"row": xx * 4 + yy * 2 + kk}

    def at_col(hh, zz):
        return {"col": hh * 4 + zz}

    y_dev, core_dev = at_row(x, yo, k), at_row(x, y, ko)
    far_dev = at_row(far, y, k)
    up_dev, down_dev, hi_dev = at_col(yh, zp), at_col(yh, zm), at_col(ho, z)
    barrier = pltpu.get_barrier_semaphore()

    def greet(i, carry):
        pl.semaphore_signal(barrier, inc=1, device_id={"row": rem(row + i, 16)}, device_id_type=MESH)
        return carry

    lax.fori_loop(1, 16, greet, 0)
    for dev in (up_dev, down_dev, at_col(yh, zf), hi_dev):
        pl.semaphore_signal(barrier, inc=1, device_id=dev, device_id_type=MESH)

    mine = pl.ds(pl.multiple_of(k * HALF, 128), HALF)
    theirs = pl.ds(pl.multiple_of(ko * HALF, 128), HALF)
    here = [
        pltpu.make_async_copy(down_hbm.at[mine, :], wd.at[:, 0:512], lsem.at[0]),
        pltpu.make_async_copy(gate_hbm.at[:, mine], wg.at[0:512, :], lsem.at[1]),
        pltpu.make_async_copy(up_hbm.at[:, mine], wu.at[0:512, :], lsem.at[2]),
        pltpu.make_async_copy(down_hbm, wdo, lsem.at[3]),
    ]
    here[0].start()
    c2[col, :, 0:512] = og_ref[...]
    pool[row] = v_ref[:, pl.ds(pl.multiple_of(row * 512, 512), 512)]
    pl.semaphore_wait(barrier, 19)

    cx = pl.ds(pl.multiple_of(k * HALF, 128), XW)
    cy = pl.ds(pl.multiple_of(k * HALF + XW, 128), YW)

    def landing(kind, t):
        if HG <= kind < AXY:
            return hsem.at[kind - HG, t]
        if kind in (CIN, LOZ, CORE):
            return hsem.at[8 + (CIN, LOZ, CORE).index(kind), t]
        return rsem.at[kind if kind < HG else kind - AXY + HG, rem(t, SLOTS)]

    def copy(kind, t, src, dst, dev):
        return pltpu.make_async_remote_copy(
            src_ref=src, dst_ref=dst, send_sem=ssem.at[kind], recv_sem=landing(kind, t),
            device_id=dev, device_id_type=MESH,
        )

    def once(kind, src, dst, dev):
        return pltpu.make_async_remote_copy(
            src_ref=src, dst_ref=dst, send_sem=ssem1.at[kind], recv_sem=rsem1.at[kind],
            device_id=dev, device_id_type=MESH,
        )

    def same(ref):
        return ref, ref

    def cblk(hh, zz, at=0, n=128):
        return c2.at[hh * 4 + zz, at:at + n, 0:512]

    def tblk(hh, zz, at=0, n=128):
        return xin.at[hh * 4 + zz, at:at + n, 0:512]

    single = {
        WD: lambda: (down_hbm.at[theirs, :], wd.at[:, 512:1024], core_dev, wd.at[:, 512:1024]),
        WG: lambda: (gate_hbm.at[:, theirs], wg.at[512:1024, :], core_dev, wg.at[512:1024, :]),
        WU: lambda: (up_hbm.at[:, theirs], wu.at[512:1024, :], core_dev, wu.at[512:1024, :]),
        CP: lambda: (*same(cblk(yh, z)), up_dev, cblk(yh, zm)),
        CM: lambda: (*same(cblk(yh, z)), down_dev, cblk(yh, zp)),
        CY: lambda: (*same(cblk(yh, z)), hi_dev, cblk(ho, z)),
        CF1: lambda: (*same(cblk(yh, zm, 0, 64)), up_dev, cblk(yh, zf, 0, 64)),
        CF2: lambda: (*same(cblk(yh, zp, 64, 64)), down_dev, cblk(yh, zf, 64, 64)),
        DP: lambda: (*same(cblk(ho, z)), up_dev, cblk(ho, zm)),
        DM: lambda: (*same(cblk(ho, z)), down_dev, cblk(ho, zp)),
        DF1: lambda: (*same(cblk(ho, zm, 0, 64)), up_dev, cblk(ho, zf, 0, 64)),
        DF2: lambda: (*same(cblk(ho, zp, 64, 64)), down_dev, cblk(ho, zf, 64, 64)),
        TP: lambda: (*same(tblk(yh, z)), up_dev, tblk(yh, zm)),
        TM: lambda: (*same(tblk(yh, z)), down_dev, tblk(yh, zp)),
        TY: lambda: (*same(tblk(yh, z)), hi_dev, tblk(ho, z)),
        TF1: lambda: (*same(tblk(yh, zm, 0, 64)), up_dev, tblk(yh, zf, 0, 64)),
        TF2: lambda: (*same(tblk(yh, zp, 64, 64)), down_dev, tblk(yh, zf, 64, 64)),
        UP: lambda: (*same(tblk(ho, z)), up_dev, tblk(ho, zm)),
        UM: lambda: (*same(tblk(ho, z)), down_dev, tblk(ho, zp)),
        UF1: lambda: (*same(tblk(ho, zm, 0, 64)), up_dev, tblk(ho, zf, 0, 64)),
        UF2: lambda: (*same(tblk(ho, zp, 64, 64)), down_dev, tblk(ho, zf, 64, 64)),
        RZ1: lambda: (part.at[:, zp, :, 0:256], rtz.at[0], at_col(yh, zp), rtz.at[0]),
        RZ2: lambda: (part.at[:, zf, :, 0:256], rtz.at[1], at_col(yh, zf), rtz.at[1]),
        RZ3: lambda: (part.at[:, zm, :, 0:256], rtz.at[2], at_col(yh, zm), rtz.at[2]),
        RZY: lambda: (stz, rtzy, hi_dev, rtzy),
        RY: lambda: (part.at[ho, :, :, 256:512], rty, hi_dev, rty),
        RYZ1: lambda: (part.at[yh, zp, :, 256:512], rtyz.at[0], at_col(yh, zp), rtyz.at[0]),
        RYZ2: lambda: (part.at[yh, zf, :, 256:512], rtyz.at[1], at_col(yh, zf), rtyz.at[1]),
        RYZ3: lambda: (part.at[yh, zm, :, 256:512], rtyz.at[2], at_col(yh, zm), rtyz.at[2]),
        LOY: lambda: (zs, rh, hi_dev, rh),
        LO6: lambda: (lo6, rz6, at_col(yh, zf), rz6),
        AXL: lambda: (*same(act.at[col, x, :, :, :, cx]), far_dev, act.at[col, far, :, :, :, cx]),
        AYL: lambda: (*same(act.at[col, x, y, :, :, cy]), far_dev, act.at[col, far, y, :, :, cy]),
    }

    def start1(*kinds):
        for kind in kinds:
            src, dst, dev, _ = single[kind]()
            once(kind, src, dst, dev).start()

    def arrive1(*kinds):
        for kind in kinds:
            place = single[kind]()[3]
            once(kind, place, place, y_dev).wait_recv()

    def sides(t):
        s = 1 - 2 * rem(t, 2)
        return rem(x + s + 4, 4), rem(x - s + 4, 4)

    def tokh(u):
        there = jnp.where((u < 3) | (u == 4), yh, ho)
        off = jnp.where((u == 1) | (u == 5), 1, 0)
        off = off + jnp.where((u == 2) | (u == 6), 3, 0) + jnp.where((u == 4) | (u == 7), 2, 0)
        return there * 4 + rem(z + off, 4)

    def tok(t):
        there = jnp.where((t >= 1) & (t < 5), ho, yh)
        off = jnp.where((t == 0) | (t == 2), 1, 0)
        off = off + jnp.where((t == 3) | (t == 5), 3, 0) + jnp.where((t == 4) | (t == 6), 2, 0)
        return there * 4 + rem(z + off, 4)

    def tokens(c):
        return pl.ds(pl.multiple_of(c * 128, 128), 128)

    def table(kind, t):
        ahead, back = sides(t)
        to_ahead, to_back = at_row(ahead, y, k), at_row(back, y, k)
        if kind < 16:
            r = gu if kind < HG else hg
            src, dst, dev = {
                XD: lambda: (r.sxd, r.rxd, to_ahead), XR: lambda: (r.sxr, r.rxr, to_back),
                X2: lambda: (r.sx2, r.rx2, to_back), XY: lambda: (r.sxy, r.rxy, y_dev),
                YY: lambda: (r.syy, r.ryy, y_dev), YD: lambda: (r.syd, r.ryd, to_ahead),
                YR: lambda: (r.syr, r.ryr, to_back), Y2: lambda: (r.sy2, r.ry2, to_back),
            }[kind % HG]()
            return src.at[t], dst.at[t], dev, dst.at[t]
        if kind == CIN:
            c = tokh(t)
            return c2.at[c, :, 0:512], c2.at[c, :, 512:1024], core_dev, c2.at[c, :, 512:1024]
        c = tok(t)
        return {
            AXY: lambda: (*same(act.at[c, x, y, :, :, cx]), y_dev, act.at[c, x, yo, :, :, cx]),
            AXP: lambda: (*same(act.at[c, x, :, :, :, cx]), to_ahead, act.at[c, back, :, :, :, cx]),
            AXM: lambda: (*same(act.at[c, x, :, :, :, cx]), to_back, act.at[c, ahead, :, :, :, cx]),
            AXF: lambda: (*same(act.at[c, back, :, :, :, cx]), to_ahead, act.at[c, far, :, :, :, cx]),
            AYP: lambda: (*same(act.at[c, x, y, :, :, cy]), to_ahead, act.at[c, back, y, :, :, cy]),
            AYM: lambda: (*same(act.at[c, x, y, :, :, cy]), to_back, act.at[c, ahead, y, :, :, cy]),
            AYF: lambda: (*same(act.at[c, back, y, :, :, cy]), to_ahead, act.at[c, far, y, :, :, cy]),
            AYY: lambda: (*same(act.at[c, :, y, :, :, cy]), y_dev, act.at[c, :, yo, :, :, cy]),
            CORE: lambda: (*same(act.at[c, :, :, :, :, mine]), core_dev, act.at[c, :, :, :, :, theirs]),
            XIN: lambda: (xin.at[c, :, 0:512], xin.at[c, :, 512:1024], core_dev, xin.at[c, :, 512:1024]),
            LOZ: lambda: (lo.at[t], rz.at[t], at_col(yh, rem(c, 4)), rz.at[t]),
        }[kind]()

    def start(t, *kinds):
        for kind in kinds:
            src, dst, dev, _ = table(kind, t)
            copy(kind, t, src, dst, dev).start()

    def arrive(t, *kinds):
        for kind in kinds:
            place = table(kind, t)[3]
            copy(kind, t, place, place, y_dev).wait_recv()

    def r0(r, t, parts):
        b = t
        ahead, _ = sides(t)
        for m, g in enumerate(parts):
            r.px[b, :, m] = g[:, :XW].reshape(4, 32, XW)
            gy = g[:, XW:].reshape(4, 2, 16, YW)
            for yy in range(2):
                r.py[b, yy, :, m] = gy[:, yy]
        r.sxd[t] = r.px[b, ahead].astype(BF)
        r.sxr[t] = r.px[b, far].astype(BF)
        start(t, r.base + XD, r.base + XR)
        r.syy[t] = r.py[b, yo].astype(BF)
        start(t, r.base + YY)

    def r1(r, t):
        b = t
        ahead, back = sides(t)
        arrive(t, r.base + XR)
        r.sx2[t] = (r.px[b, back] + r.rxr[t].astype(F32)).astype(BF)
        start(t, r.base + X2)
        arrive(t, r.base + YY)
        r.py[b, y] = r.py[b, y] + r.ryy[t].astype(F32)
        r.syd[t] = r.py[b, y, ahead].astype(BF)
        r.syr[t] = r.py[b, y, far].astype(BF)
        start(t, r.base + YD, r.base + YR)

    def r2(r, t):
        b = t
        _, back = sides(t)
        arrive(t, r.base + XD, r.base + X2)
        r.px[b, x] = r.px[b, x] + r.rxd[t].astype(F32) + r.rx2[t].astype(F32)
        r.sxy[t] = r.px[b, x, :, pl.ds(pl.multiple_of(yo * 16, 16), 16), :].astype(BF)
        start(t, r.base + XY)
        arrive(t, r.base + YR)
        r.sy2[t] = (r.py[b, y, back] + r.ryr[t].astype(F32)).astype(BF)
        start(t, r.base + Y2)

    def r3x(r, t):
        b = t
        arrive(t, r.base + XY)
        return r.px[b, x, :, pl.ds(pl.multiple_of(y * 16, 16), 16), :] + r.rxy[t].astype(F32)

    def r3y(r, t):
        b = t
        arrive(t, r.base + YD, r.base + Y2)
        return r.py[b, y, x] + r.ryd[t].astype(F32) + r.ry2[t].astype(F32)

    def h0(u):
        arrive(u, CIN)
        r0(hg, u, [lax.dot_general(c2[tokh(u)], wd[...], (((1,), (1,)), ((), ())), preferred_element_type=F32)])

    def h3(u):
        c = tokh(u)
        hfx[c] = r3x(hg, u)[0]
        hfy[c] = r3y(hg, u)[0]

    def place(c, ends, starts, counts, owners):
        spot = lax.broadcasted_iota(jnp.int32, (128, 64), 0).astype(F32) + (c * 128).astype(F32)
        member = jnp.where((spot >= starts) & (spot < ends), 1.0, 0.0)

        def pick(values):
            return jnp.sum(member * values, axis=1, keepdims=True).astype(jnp.int32)

        count, begin = pick(counts), pick(starts)
        within = lax.broadcasted_iota(jnp.int32, (128, 1), 0) + c * 128 - begin
        first = (count + 1) >> 1
        second = within >= first
        slot = jnp.where(second, within - first, within)
        owner = jnp.where(second, pick(owners[1]), pick(owners[0]))
        index = jnp.where((owner & 7) == col, (owner >> 3) * 16 + slot, -1)
        hot[c] = jnp.where(lax.broadcasted_iota(jnp.int32, (128, 256), 1) == index, 1.0, 0.0).astype(BF)

    def find_places():
        counts = jnp.broadcast_to(counts_ref[...].astype(F32), (8, 64))
        owner = jnp.broadcast_to(owner_ref[...].astype(F32), (8, 128))
        upto = lax.broadcasted_iota(jnp.int32, (64, 64), 0) <= lax.broadcasted_iota(jnp.int32, (64, 64), 1)
        ends = jnp.dot(counts, jnp.where(upto, 1.0, 0.0), preferred_element_type=F32)
        starts = ends - counts
        i0 = lax.broadcasted_iota(jnp.int32, (128, 64), 0)
        i1 = lax.broadcasted_iota(jnp.int32, (128, 64), 1) * 2
        owners = [
            jnp.dot(owner, jnp.where(i0 == i1 + j, 1.0, 0.0), preferred_element_type=F32)[0:1] for j in range(2)
        ]

        def body(c, carry):
            place(c, ends[0:1], starts[0:1], counts[0:1], owners)
            return carry

        lax.fori_loop(0, 8, body, 0)

    def v_0():
        spread_all().wait_recv()
        rows = jnp.dot(hot[...].reshape(1024, 256), pool[...].reshape(256, 512), preferred_element_type=F32)
        part[...] = rows.astype(BF).reshape(2, 4, 128, 512)
        start1(RY, RZ1, RZ2, RZ3)

    def v_2():
        arrive1(RY)
        part[yh, :, :, 256:512] = part[yh, :, :, 256:512] + rty[...]
        start1(RYZ1, RYZ2, RYZ3)
        arrive1(RZ1, RZ2, RZ3)
        stz[...] = part[ho, z, :, 0:256] + rtz[0, ho] + rtz[1, ho] + rtz[2, ho]
        start1(RZY)

    def v_3():
        arrive1(RYZ1, RYZ2, RYZ3)
        xin[col, :, 256:512] = part[yh, z, :, 256:512] + rtyz[0] + rtyz[1] + rtyz[2]
        arrive1(RZY)
        xin[col, :, 0:256] = part[yh, z, :, 0:256] + rtz[0, yh] + rtz[1, yh] + rtz[2, yh] + rtzy[...]
        start1(TP, TM, TY)

    def t_0():
        arrive1(TM)
        start1(TF2)
        arrive1(TY)
        start1(UP, UM)
        arrive1(TP)
        start1(TF1)

    def t_2():
        arrive1(UP)
        start1(UF1)
        arrive1(UM)
        start1(UF2)

    def t_4():
        arrive1(UF1, UF2)

    def t_6():
        arrive1(TF1, TF2)

    def p0(t):
        start(t, XIN)

    def s0(t):
        arrive(t, XIN)
        c = tok(t)
        x_t = xin[c]
        xt[t] = x_t[:, 0:512].T
        pltpu.make_async_copy(xt.at[t], xt_ref.at[:, tokens(c)], osem.at[1]).start()
        r0(gu, t, [jnp.dot(x_t, w[...], preferred_element_type=F32) for w in (wg, wu)])

    def activate(c, full, hgrad, cols):
        gate, up = full[0], full[1]
        sigma = jax.nn.sigmoid(gate)
        act[c, x, y, 0, :, cols] = (gate * sigma * up).astype(BF)
        act[c, x, y, 1, :, cols] = (hgrad * up * sigma * (1.0 + gate * (1.0 - sigma))).astype(BF)
        act[c, x, y, 2, :, cols] = (hgrad * gate * sigma).astype(BF)

    def s3(t):
        c = tok(t)
        activate(c, r3x(gu, t), hfx[c], cx)
        start(t, AXY)
        activate(c, r3y(gu, t), hfy[c], cy)
        start(t, AYP, AYM)

        @pl.when(t == 7)
        def _():
            start1(AYL)

    def s4(t):
        arrive(t, AXY)
        start(t, AXP, AXM)

        @pl.when(t == 7)
        def _():
            start1(AXL)

        arrive(t, AYP)

        @pl.when(t < 7)
        def _():
            start(t, AYF)

        arrive(t, AYM)

        @pl.when(t == 7)
        def _():
            arrive1(AYL)
            start(t, AYY)

    def s5(t):
        arrive(t, AXP)

        @pl.when(t < 7)
        def _():
            start(t, AXF)

        arrive(t, AXM)

        @pl.when(t < 7)
        def _():
            arrive(t, AYF)
            start(t, AYY)

        @pl.when(t == 7)
        def _():
            arrive1(AXL)
            arrive(t, AYY)
            start(t, CORE)

    def s6(t):
        @pl.when(t < 7)
        def _():
            arrive(t, AXF, AYY)
            start(t, CORE)

        @pl.when(t == 7)
        def _():
            project(t)

    def s7(t):
        @pl.when(t < 7)
        def _():
            project(t)

    def project(t):
        c = tok(t)
        arrive(t, CORE)
        pltpu.make_async_copy(act.at[c, :, :, 1:3], o_ref.at[c], osem.at[0]).start()
        hidden = act[c, :, :, 0].reshape(128, 2 * HALF)
        lo[t] = jnp.dot(hidden, wdo[...], preferred_element_type=F32)

        @pl.when((t != 1) & (t < 6))
        def _():
            start(t, LOZ)

        @pl.when(t == 6)
        def _():
            lo6[...] = lo[6].astype(BF)
            start1(LO6)

        ht[t] = hidden.T
        pltpu.make_async_copy(ht.at[t], ht_ref.at[:, tokens(c)], osem.at[2]).start()

    def s8(t):
        @pl.when(t == 4)
        def _():
            arrive(2, LOZ)
            arrive(3, LOZ)
            arrive(4, LOZ)
            zs[...] = lo[1] + rz[2] + rz[3] + rz[4]
            start1(LOY)

    def spread(i, carry):
        to = rem(row + i, 16)
        pltpu.make_async_remote_copy(
            src_ref=v_ref.at[:, pl.ds(pl.multiple_of(to * 512, 512), 512)],
            dst_ref=pool.at[row],
            send_sem=asem.at[0], recv_sem=asem.at[1], device_id={"row": to}, device_id_type=MESH,
        ).start()
        return carry

    def spread_all():
        return pltpu.make_async_remote_copy(
            src_ref=pool.at[0:15], dst_ref=pool.at[0:15], send_sem=asem.at[0], recv_sem=asem.at[1],
            device_id=y_dev, device_id_type=MESH,
        )

    def c_0():
        arrive1(CM)
        start1(CF2)
        arrive1(CP)
        start1(CF1)
        start(1, CIN)
        start(2, CIN)

    def c_1():
        arrive1(CY)
        start(3, CIN)
        arrive1(CF1, CF2)
        start(4, CIN)

    def c_2():
        start1(DP, DM)

    def c_3():
        arrive1(DM)
        start1(DF2)
        arrive1(DP)
        start1(DF1)
        start(5, CIN)
        start(6, CIN)

    def c_4():
        arrive1(DF1, DF2)
        start(7, CIN)
        pltpu.make_async_copy(c2.at[:, :, 0:512], co_ref, lsem.at[4]).start()

    def w_0():
        here[0].wait()
        arrive1(WD)
        start1(WG, WU)

    def w_1():
        here[1].wait()
        here[2].wait()
        here[3].wait()
        arrive1(WG, WU)

    start(0, CIN)
    lax.fori_loop(1, 16, spread, 0)
    start1(WD, CP, CM, CY)
    find_places()
    for c in here[1:]:
        c.start()

    def each(n, lag, stage):
        t = n - lag

        @pl.when((t >= 0) & (t < CHUNKS))
        def _():
            stage(t)

    def at(n, when, stage):
        @pl.when(n == when)
        def _():
            stage()

    def step(n, carry):
        at(n, 0, w_0)
        for lag, stage in enumerate([h0, lambda u: r1(hg, u), lambda u: r2(hg, u), h3]):
            q = n - lag
            m = jnp.where(q == 3, -1, jnp.where(q > 3, q - 1, q))
            each(2 * m - 1, 0, stage)
            each(2 * m, 0, stage)
        at(n, 0, c_0)
        at(n, 1, c_1)
        at(n, 0, v_0)
        at(n, 2, v_2)
        at(n, 2, c_2)
        at(n, 3, v_3)
        at(n, 3, c_3)
        at(n, 4, c_4)
        at(n, FIRST, t_0)
        at(n, FIRST + 2, t_2)
        at(n, FIRST + 4, t_4)
        at(n, FIRST + 6, t_6)
        at(n, FIRST + 1, w_1)
        for lag, stage in [
            (0, p0), (1, s0), (2, lambda t: r1(gu, t)), (3, lambda t: r2(gu, t)), (4, s3), (5, s4), (6, s5),
            (8, s7), (7, s6), (9, s8),
        ]:
            each(n, FIRST + lag, stage)
        return carry

    lax.fori_loop(0, FIRST + CHUNKS + 7, step, 0)
    arrive(0, LOZ)
    arrive(5, LOZ)
    arrive1(LOY)
    arrive1(LO6)
    out_ref[...] = (lo[7] + rz[0] + rz[5] + rz6[...].astype(F32) + rh[...]).astype(BF)

    def all_sent(kind):
        if kind < 16:
            r = gu if kind < HG else hg
            return (r.sxd, r.sxr, r.sx2, r.sxy, r.syy, r.syd, r.syr, r.sy2)[kind % HG]
        if kind in (AXP, AXM, AXF):
            return act.at[0:7 if kind == AXF else 8, x, :, :, :, cx]
        if kind in (AYP, AYM, AYF):
            return act.at[0:7 if kind == AYF else 8, x, y, :, :, cy]
        return {
            AXY: lambda: act.at[:, x, y, :, :, cx], AYY: lambda: act.at[:, :, y, :, :, cy],
            CORE: lambda: act.at[:, :, :, :, :, mine], XIN: lambda: xin.at[:, :, 0:512],
            CIN: lambda: c2.at[:, :, 0:512], LOZ: lambda: lo.at[0:5],
        }[kind]()

    for kind in range(KINDS):
        ref = all_sent(kind)
        copy(kind, 0, ref, ref, y_dev).wait_send()
    for kind in range(ONCE):
        src, dst, dev, _ = single[kind]()
        once(kind, src, dst, dev).wait_send()
    spread_all().wait_send()
    pltpu.make_async_copy(act.at[:, :, :, 1:3], o_ref, osem.at[0]).wait()
    pltpu.make_async_copy(xt, xt, osem.at[1]).wait()
    pltpu.make_async_copy(ht, ht, osem.at[2]).wait()
    pltpu.make_async_copy(c2.at[:, :, 0:512], co_ref, lsem.at[4]).wait()


def main_call(v, counts, owner, og, gate, up, down):
    n = CHUNKS
    vm = lambda *s: pltpu.VMEM(s, BF)
    vf = lambda *s: pltpu.VMEM(s, F32)

    def row_sum(mats):
        xb, xq, yb = (n, mats, 32, XW), (n, mats, 16, XW), (n, mats, 16, YW)
        moves = [vm(*xb), vm(*xb), vm(*xb), vm(*xq), vm(n, 4, mats, 16, YW), vm(*yb), vm(*yb), vm(*yb)]
        return [vf(8, 4, mats, 32, XW), vf(8, 2, 4, mats, 16, YW), *moves, *moves]

    dma = pltpu.SemaphoreType.DMA
    vmem = pl.BlockSpec(memory_space=pltpu.VMEM)
    hbm = pl.BlockSpec(memory_space=pl.ANY)
    return pl.pallas_call(
        main_kernel,
        out_shape=(
            jax.ShapeDtypeStruct((128, 512), BF),
            jax.ShapeDtypeStruct((n, 4, 2, 2, 16, 2 * HALF), BF),
            jax.ShapeDtypeStruct((2 * HALF, 1024), BF),
            jax.ShapeDtypeStruct((512, 1024), BF),
            jax.ShapeDtypeStruct((n, 128, 512), BF),
        ),
        in_specs=[vmem, vmem, vmem, vmem, hbm, hbm, hbm],
        out_specs=(vmem, hbm, hbm, hbm, hbm),
        scratch_shapes=[
            vm(n, 4, 2, 3, 16, 2 * HALF), vm(16, 16, 512), vm(n, 128, 1024), vm(n, 128, 1024),
            vm(1024, HALF), vm(1024, HALF), vm(HALF, 1024), vm(2 * HALF, 512),
            vm(8, 128, 256), vm(2, 4, 128, 512), vm(3, 2, 128, 256), vm(4, 128, 256), vm(128, 256), vm(3, 128, 256), vm(128, 256),
            vm(n, 2 * HALF, 128), vm(n, 512, 128),
            vf(n, 16, XW), vf(n, 16, YW),
            vf(n, 128, 512), vf(n, 128, 512), vf(128, 512), vf(128, 512), vm(128, 512), vm(128, 512),
            *row_sum(2), *row_sum(1),
            dma((KINDS,)), dma((18, SLOTS)), dma((11, n)), dma((ONCE,)), dma((ONCE,)), dma((2,)),
            dma((3,)), dma((5,)),
        ],
        compiler_params=pltpu.CompilerParams(
            collective_id=0, has_side_effects=True, vmem_limit_bytes=60 << 20
        ),
        cost_estimate=pl.CostEstimate(flops=10**10, bytes_accessed=30 * 10**6, transcendentals=0),
        name="row_sums",
    )(v, counts, owner, og, gate, up, down)


def grads_kernel(xt_hbm, c_hbm, ht_hbm, o_hbm, y_hbm, gate_hbm, up_hbm, down_hbm, out_hbm, xt, c, ht, o, gate, up, down, lsem, wsem):
    load = pltpu.make_async_copy
    strips = [slice(0, HALF), slice(HALF, 2 * HALF)]
    x_in, c_in = load(xt_hbm, xt, lsem.at[0]), load(c_hbm, c, lsem.at[1])
    ht_in = [load(ht_hbm.at[s], ht.at[s], lsem.at[2 + i]) for i, s in enumerate(strips)]
    o_in = [
        [load(o_hbm.at[:, :, :, m, :, s], o.at[:, :, :, m, :, s], lsem.at[4 + 2 * i + m]) for m in range(2)]
        for i, s in enumerate(strips)
    ]
    c_in.start()
    ht_in[0].start()
    x_in.start()
    for copies in (o_in[0], ht_in[1:], o_in[1]):
        for copy in copies:
            copy.start()
    out = []

    def write(src, dst):
        out.append(pltpu.make_async_copy(src, dst, wsem.at[len(out)]))
        out[-1].start()

    write(y_hbm, out_hbm)
    c_in.wait()
    for i, s in enumerate(strips):
        ht_in[i].wait()
        down[s] = jnp.dot(ht[s], c[...].reshape(1024, 512), preferred_element_type=F32)
        write(down.at[s], down_hbm.at[s])
        if i == 0:
            x_in.wait()
        for m, (grad, hbm) in enumerate(((gate, gate_hbm), (up, up_hbm))):
            o_in[i][m].wait()
            grad[:, s] = jnp.dot(xt[...], o[:, :, :, m, :, s].reshape(1024, HALF), preferred_element_type=F32)
            write(grad.at[:, s], hbm.at[:, s])
    for copy in out:
        copy.wait()


def grads_call(xt, c, ht, o, y):
    hbm = pl.BlockSpec(memory_space=pl.ANY)
    up, down = (512, 2 * HALF), (2 * HALF, 512)
    return pl.pallas_call(
        grads_kernel,
        out_shape=(
            *(jax.ShapeDtypeStruct(shape, F32) for shape in (up, up, down)),
            jax.ShapeDtypeStruct(y.shape, y.dtype),
        ),
        in_specs=[hbm] * 5,
        out_specs=(hbm, hbm, hbm, hbm),
        scratch_shapes=[
            *(pltpu.VMEM(a.shape, BF) for a in (xt, c, ht, o)),
            *(pltpu.VMEM(shape, F32) for shape in (up, up, down)),
            pltpu.SemaphoreType.DMA((8,)), pltpu.SemaphoreType.DMA((7,)),
        ],
        compiler_params=pltpu.CompilerParams(vmem_limit_bytes=60 << 20),
        cost_estimate=pl.CostEstimate(flops=8 * 10**9, bytes_accessed=24 * 10**6, transcendentals=0),
        name="weight_grads",
    )(xt, c, ht, o, y)


def local(vision_tokens, image_counts, image_owner, gate_weight, up_weight, down_weight, out_grad):
    y, o, ht, xt, c = main_call(
        vision_tokens, image_counts[None, :], image_owner[None, :], out_grad, gate_weight, up_weight, down_weight
    )
    grad_gate, grad_up, grad_down, layer_out = grads_call(xt, c, ht, o, y)
    return (layer_out, grad_gate, grad_up, grad_down)


def solution(mesh):
    in_specs = (
        P(("row", "col"), None),
        P(),
        P(),
        P("row", "col"),
        P("row", "col"),
        P("col", "row"),
        P("col", "row"),
    )
    out_specs = (P("col", "row"), P("row", "col"), P("row", "col"), P("col", "row"))
    return jax.shard_map(local, mesh=mesh, in_specs=in_specs, out_specs=out_specs, check_vma=False)
```

```python
import functools
import jax
import jax.numpy as jnp
from jax import lax
from jax.experimental import pallas as pl
from jax.experimental.pallas import tpu as pltpu
from jax.sharding import PartitionSpec as P

BF = jnp.bfloat16
F32 = jnp.float32
MESH = pl.DeviceIdType.MESH

CHUNKS = 8
HALF = 896
XW = 512
YW = HALF - XW

XD, XR, X2, XY, YY, YD, YR, Y2 = range(8)
HG = 8
AXY, AXP, AXM, AXF, AYP, AYM, AYF, AYY, CORE, XIN, CIN, LOZ = range(16, 28)
KINDS = 28
CP, CM, CY, CF1, CF2, DP, DM, DF1, DF2 = range(9)
TP, TM, TY, TF1, TF2, UP, UM, UF1, UF2 = range(9, 18)
RZ1, RZ2, RZ3, RZY, RY, RYZ1, RYZ2, RYZ3 = range(18, 26)
WG, WU, WD, LOY, AXL, AYL, LO6 = range(26, 33)
ONCE = 33
SLOTS = 4
FIRST = 4

def rem(a, n):
    return lax.rem(a, n)


class RowSum:
    def __init__(self, base, refs):
        self.base = base
        (self.px, self.py, self.sxd, self.sxr, self.sx2, self.sxy, self.syy, self.syd, self.syr,
         self.sy2, self.rxd, self.rxr, self.rx2, self.rxy, self.ryy, self.ryd, self.ryr, self.ry2) = refs


def main_kernel(
    v_ref, counts_ref, owner_ref, og_ref, gate_hbm, up_hbm, down_hbm,
    out_ref, o_ref, ht_ref, xt_ref, co_ref,
    act, pool, xin, c2, wg, wu, wd, wdo,
    hot, part, rtz, rty, stz, rtyz, rtzy, ht, xt,
    hfx, hfy, lo, rz, zs, rh, lo6, rz6,
    *rest,
):
    gu, hg = RowSum(0, rest[:18]), RowSum(HG, rest[18:36])
    ssem, rsem, hsem, ssem1, rsem1, asem, osem, lsem = rest[36:]
    row = lax.axis_index("row")
    col = lax.axis_index("col")
    x, y, k = row // 4, rem(row // 2, 2), rem(row, 2)
    yh, z = col // 4, rem(col, 4)
    yo, ko, ho = 1 - y, 1 - k, 1 - yh
    far = rem(x + 2, 4)
    zp, zm, zf = rem(z + 1, 4), rem(z + 3, 4), rem(z + 2, 4)

    def at_row(xx, yy, kk):
        return {"row": xx * 4 + yy * 2 + kk}

    def at_col(hh, zz):
        return {"col": hh * 4 + zz}

    y_dev, core_dev = at_row(x, yo, k), at_row(x, y, ko)
    far_dev = at_row(far, y, k)
    up_dev, down_dev, hi_dev = at_col(yh, zp), at_col(yh, zm), at_col(ho, z)
    barrier = pltpu.get_barrier_semaphore()

    def greet(i, carry):
        pl.semaphore_signal(barrier, inc=1, device_id={"row": rem(row + i, 16)}, device_id_type=MESH)
        return carry

    lax.fori_loop(1, 16, greet, 0)
    for dev in (up_dev, down_dev, at_col(yh, zf), hi_dev):
        pl.semaphore_signal(barrier, inc=1, device_id=dev, device_id_type=MESH)

    mine = pl.ds(pl.multiple_of(k * HALF, 128), HALF)
    theirs = pl.ds(pl.multiple_of(ko * HALF, 128), HALF)
    here = [
        pltpu.make_async_copy(down_hbm.at[mine, :], wd.at[:, 0:512], lsem.at[0]),
        pltpu.make_async_copy(gate_hbm.at[:, mine], wg.at[0:512, :], lsem.at[1]),
        pltpu.make_async_copy(up_hbm.at[:, mine], wu.at[0:512, :], lsem.at[2]),
        pltpu.make_async_copy(down_hbm, wdo, lsem.at[3]),
    ]
    here[0].start()
    c2[col, :, 0:512] = og_ref[...]
    pool[row] = v_ref[:, pl.ds(pl.multiple_of(row * 512, 512), 512)]
    pl.semaphore_wait(barrier, 19)

    cx = pl.ds(pl.multiple_of(k * HALF, 128), XW)
    cy = pl.ds(pl.multiple_of(k * HALF + XW, 128), YW)

    def landing(kind, t):
        if kind < AXY:
            return hsem.at[kind, t]
        if kind in (CIN, LOZ, CORE):
            return hsem.at[16 + (CIN, LOZ, CORE).index(kind), t]
        return rsem.at[kind - AXY, rem(t, SLOTS)]

    def copy(kind, t, src, dst, dev):
        return pltpu.make_async_remote_copy(
            src_ref=src, dst_ref=dst, send_sem=ssem.at[kind], recv_sem=landing(kind, t),
            device_id=dev, device_id_type=MESH,
        )

    def once(kind, src, dst, dev):
        return pltpu.make_async_remote_copy(
            src_ref=src, dst_ref=dst, send_sem=ssem1.at[kind], recv_sem=rsem1.at[kind],
            device_id=dev, device_id_type=MESH,
        )

    def same(ref):
        return ref, ref

    def cblk(hh, zz, at=0, n=128):
        return c2.at[hh * 4 + zz, at:at + n, 0:512]

    def tblk(hh, zz, at=0, n=128):
        return xin.at[hh * 4 + zz, at:at + n, 0:512]

    single = {
        WD: lambda: (down_hbm.at[theirs, :], wd.at[:, 512:1024], core_dev, wd.at[:, 512:1024]),
        WG: lambda: (gate_hbm.at[:, theirs], wg.at[512:1024, :], core_dev, wg.at[512:1024, :]),
        WU: lambda: (up_hbm.at[:, theirs], wu.at[512:1024, :], core_dev, wu.at[512:1024, :]),
        CP: lambda: (*same(cblk(yh, z)), up_dev, cblk(yh, zm)),
        CM: lambda: (*same(cblk(yh, z)), down_dev, cblk(yh, zp)),
        CY: lambda: (*same(cblk(yh, z)), hi_dev, cblk(ho, z)),
        CF1: lambda: (*same(cblk(yh, zm, 0, 64)), up_dev, cblk(yh, zf, 0, 64)),
        CF2: lambda: (*same(cblk(yh, zp, 64, 64)), down_dev, cblk(yh, zf, 64, 64)),
        DP: lambda: (*same(cblk(ho, z)), up_dev, cblk(ho, zm)),
        DM: lambda: (*same(cblk(ho, z)), down_dev, cblk(ho, zp)),
        DF1: lambda: (*same(cblk(ho, zm, 0, 64)), up_dev, cblk(ho, zf, 0, 64)),
        DF2: lambda: (*same(cblk(ho, zp, 64, 64)), down_dev, cblk(ho, zf, 64, 64)),
        TP: lambda: (*same(tblk(yh, z)), up_dev, tblk(yh, zm)),
        TM: lambda: (*same(tblk(yh, z)), down_dev, tblk(yh, zp)),
        TY: lambda: (*same(tblk(yh, z)), hi_dev, tblk(ho, z)),
        TF1: lambda: (*same(tblk(yh, zm, 0, 64)), up_dev, tblk(yh, zf, 0, 64)),
        TF2: lambda: (*same(tblk(yh, zp, 64, 64)), down_dev, tblk(yh, zf, 64, 64)),
        UP: lambda: (*same(tblk(ho, z)), up_dev, tblk(ho, zm)),
        UM: lambda: (*same(tblk(ho, z)), down_dev, tblk(ho, zp)),
        UF1: lambda: (*same(tblk(ho, zm, 0, 64)), up_dev, tblk(ho, zf, 0, 64)),
        UF2: lambda: (*same(tblk(ho, zp, 64, 64)), down_dev, tblk(ho, zf, 64, 64)),
        RZ1: lambda: (part.at[:, zp, :, 0:256], rtz.at[0], at_col(yh, zp), rtz.at[0]),
        RZ2: lambda: (part.at[:, zf, :, 0:256], rtz.at[1], at_col(yh, zf), rtz.at[1]),
        RZ3: lambda: (part.at[:, zm, :, 0:256], rtz.at[2], at_col(yh, zm), rtz.at[2]),
        RZY: lambda: (stz, rtzy, hi_dev, rtzy),
        RY: lambda: (part.at[ho, :, :, 256:512], rty, hi_dev, rty),
        RYZ1: lambda: (part.at[yh, zp, :, 256:512], rtyz.at[0], at_col(yh, zp), rtyz.at[0]),
        RYZ2: lambda: (part.at[yh, zf, :, 256:512], rtyz.at[1], at_col(yh, zf), rtyz.at[1]),
        RYZ3: lambda: (part.at[yh, zm, :, 256:512], rtyz.at[2], at_col(yh, zm), rtyz.at[2]),
        LOY: lambda: (zs, rh, hi_dev, rh),
        LO6: lambda: (lo6, rz6, at_col(yh, zf), rz6),
        AXL: lambda: (*same(act.at[col, x, :, :, :, cx]), far_dev, act.at[col, far, :, :, :, cx]),
        AYL: lambda: (*same(act.at[col, x, y, :, :, cy]), far_dev, act.at[col, far, y, :, :, cy]),
    }

    def start1(*kinds):
        for kind in kinds:
            src, dst, dev, _ = single[kind]()
            once(kind, src, dst, dev).start()

    def arrive1(*kinds):
        for kind in kinds:
            place = single[kind]()[3]
            once(kind, place, place, y_dev).wait_recv()

    def sides(t):
        s = 1 - 2 * rem(t, 2)
        return rem(x + s + 4, 4), rem(x - s + 4, 4)

    def tokh(u):
        there = jnp.where((u < 3) | (u == 4), yh, ho)
        off = jnp.where((u == 1) | (u == 5), 1, 0)
        off = off + jnp.where((u == 2) | (u == 6), 3, 0) + jnp.where((u == 4) | (u == 7), 2, 0)
        return there * 4 + rem(z + off, 4)

    def tok(t):
        there = jnp.where((t >= 1) & (t < 5), ho, yh)
        off = jnp.where((t == 0) | (t == 2), 1, 0)
        off = off + jnp.where((t == 3) | (t == 5), 3, 0) + jnp.where((t == 4) | (t == 6), 2, 0)
        return there * 4 + rem(z + off, 4)

    def tokens(c):
        return pl.ds(pl.multiple_of(c * 128, 128), 128)

    def table(kind, t):
        ahead, back = sides(t)
        to_ahead, to_back = at_row(ahead, y, k), at_row(back, y, k)
        if kind < 16:
            r = gu if kind < HG else hg
            src, dst, dev = {
                XD: lambda: (r.sxd, r.rxd, to_ahead), XR: lambda: (r.sxr, r.rxr, to_back),
                X2: lambda: (r.sx2, r.rx2, to_back), XY: lambda: (r.sxy, r.rxy, y_dev),
                YY: lambda: (r.syy, r.ryy, y_dev), YD: lambda: (r.syd, r.ryd, to_ahead),
                YR: lambda: (r.syr, r.ryr, to_back), Y2: lambda: (r.sy2, r.ry2, to_back),
            }[kind % HG]()
            return src.at[t], dst.at[t], dev, dst.at[t]
        if kind == CIN:
            c = tokh(t)
            return c2.at[c, :, 0:512], c2.at[c, :, 512:1024], core_dev, c2.at[c, :, 512:1024]
        c = tok(t)
        return {
            AXY: lambda: (*same(act.at[c, x, y, :, :, cx]), y_dev, act.at[c, x, yo, :, :, cx]),
            AXP: lambda: (*same(act.at[c, x, :, :, :, cx]), to_ahead, act.at[c, back, :, :, :, cx]),
            AXM: lambda: (*same(act.at[c, x, :, :, :, cx]), to_back, act.at[c, ahead, :, :, :, cx]),
            AXF: lambda: (*same(act.at[c, back, :, :, :, cx]), to_ahead, act.at[c, far, :, :, :, cx]),
            AYP: lambda: (*same(act.at[c, x, y, :, :, cy]), to_ahead, act.at[c, back, y, :, :, cy]),
            AYM: lambda: (*same(act.at[c, x, y, :, :, cy]), to_back, act.at[c, ahead, y, :, :, cy]),
            AYF: lambda: (*same(act.at[c, back, y, :, :, cy]), to_ahead, act.at[c, far, y, :, :, cy]),
            AYY: lambda: (*same(act.at[c, :, y, :, :, cy]), y_dev, act.at[c, :, yo, :, :, cy]),
            CORE: lambda: (*same(act.at[c, :, :, :, :, mine]), core_dev, act.at[c, :, :, :, :, theirs]),
            XIN: lambda: (xin.at[c, :, 0:512], xin.at[c, :, 512:1024], core_dev, xin.at[c, :, 512:1024]),
            LOZ: lambda: (lo.at[t], rz.at[t], at_col(yh, rem(c, 4)), rz.at[t]),
        }[kind]()

    def start(t, *kinds):
        for kind in kinds:
            src, dst, dev, _ = table(kind, t)
            copy(kind, t, src, dst, dev).start()

    def arrive(t, *kinds):
        for kind in kinds:
            place = table(kind, t)[3]
            copy(kind, t, place, place, y_dev).wait_recv()

    def r0(r, t, parts):
        b = t
        ahead, _ = sides(t)
        for m, g in enumerate(parts):
            r.px[b, :, m] = g[:, :XW].reshape(4, 32, XW)
            gy = g[:, XW:].reshape(4, 2, 16, YW)
            for yy in range(2):
                r.py[b, yy, :, m] = gy[:, yy]
        r.sxd[t] = r.px[b, ahead].astype(BF)
        r.sxr[t] = r.px[b, far].astype(BF)
        start(t, r.base + XD, r.base + XR)
        r.syy[t] = r.py[b, yo].astype(BF)
        start(t, r.base + YY)

    def r1(r, t):
        b = t
        ahead, back = sides(t)
        arrive(t, r.base + XR)
        r.sx2[t] = (r.px[b, back] + r.rxr[t].astype(F32)).astype(BF)
        start(t, r.base + X2)
        arrive(t, r.base + YY)
        r.py[b, y] = r.py[b, y] + r.ryy[t].astype(F32)
        r.syd[t] = r.py[b, y, ahead].astype(BF)
        r.syr[t] = r.py[b, y, far].astype(BF)
        start(t, r.base + YD, r.base + YR)

    def r2(r, t):
        b = t
        _, back = sides(t)
        arrive(t, r.base + XD, r.base + X2)
        r.px[b, x] = r.px[b, x] + r.rxd[t].astype(F32) + r.rx2[t].astype(F32)
        r.sxy[t] = r.px[b, x, :, pl.ds(pl.multiple_of(yo * 16, 16), 16), :].astype(BF)
        start(t, r.base + XY)
        arrive(t, r.base + YR)
        r.sy2[t] = (r.py[b, y, back] + r.ryr[t].astype(F32)).astype(BF)
        start(t, r.base + Y2)

    def r3x(r, t):
        b = t
        arrive(t, r.base + XY)
        return r.px[b, x, :, pl.ds(pl.multiple_of(y * 16, 16), 16), :] + r.rxy[t].astype(F32)

    def r3y(r, t):
        b = t
        arrive(t, r.base + YD, r.base + Y2)
        return r.py[b, y, x] + r.ryd[t].astype(F32) + r.ry2[t].astype(F32)

    def h0(u):
        arrive(u, CIN)
        r0(hg, u, [lax.dot_general(c2[tokh(u)], wd[...], (((1,), (1,)), ((), ())), preferred_element_type=F32)])

    def h3(u):
        c = tokh(u)
        hfx[c] = r3x(hg, u)[0]
        hfy[c] = r3y(hg, u)[0]

    def place(c, ends, starts, counts, owners):
        spot = lax.broadcasted_iota(jnp.int32, (128, 64), 0).astype(F32) + (c * 128).astype(F32)
        member = jnp.where((spot >= starts) & (spot < ends), 1.0, 0.0)

        def pick(values):
            return jnp.sum(member * values, axis=1, keepdims=True).astype(jnp.int32)

        count, begin = pick(counts), pick(starts)
        within = lax.broadcasted_iota(jnp.int32, (128, 1), 0) + c * 128 - begin
        first = (count + 1) >> 1
        second = within >= first
        slot = jnp.where(second, within - first, within)
        owner = jnp.where(second, pick(owners[1]), pick(owners[0]))
        index = jnp.where((owner & 7) == col, (owner >> 3) * 16 + slot, -1)
        hot[c] = jnp.where(lax.broadcasted_iota(jnp.int32, (128, 256), 1) == index, 1.0, 0.0).astype(BF)

    def find_places():
        counts = jnp.broadcast_to(counts_ref[...].astype(F32), (8, 64))
        owner = jnp.broadcast_to(owner_ref[...].astype(F32), (8, 128))
        upto = lax.broadcasted_iota(jnp.int32, (64, 64), 0) <= lax.broadcasted_iota(jnp.int32, (64, 64), 1)
        ends = jnp.dot(counts, jnp.where(upto, 1.0, 0.0), preferred_element_type=F32)
        starts = ends - counts
        i0 = lax.broadcasted_iota(jnp.int32, (128, 64), 0)
        i1 = lax.broadcasted_iota(jnp.int32, (128, 64), 1) * 2
        owners = [
            jnp.dot(owner, jnp.where(i0 == i1 + j, 1.0, 0.0), preferred_element_type=F32)[0:1] for j in range(2)
        ]

        def body(c, carry):
            place(c, ends[0:1], starts[0:1], counts[0:1], owners)
            return carry

        lax.fori_loop(0, 8, body, 0)

    def v_0():
        spread_all().wait_recv()
        rows = jnp.dot(hot[...].reshape(1024, 256), pool[...].reshape(256, 512), preferred_element_type=F32)
        part[...] = rows.astype(BF).reshape(2, 4, 128, 512)
        start1(RY, RZ1, RZ2, RZ3)

    def v_2():
        arrive1(RY)
        part[yh, :, :, 256:512] = part[yh, :, :, 256:512] + rty[...]
        start1(RYZ1, RYZ2, RYZ3)
        arrive1(RZ1, RZ2, RZ3)
        stz[...] = part[ho, z, :, 0:256] + rtz[0, ho] + rtz[1, ho] + rtz[2, ho]
        start1(RZY)

    def v_3():
        arrive1(RYZ1, RYZ2, RYZ3)
        xin[col, :, 256:512] = part[yh, z, :, 256:512] + rtyz[0] + rtyz[1] + rtyz[2]
        arrive1(RZY)
        xin[col, :, 0:256] = part[yh, z, :, 0:256] + rtz[0, yh] + rtz[1, yh] + rtz[2, yh] + rtzy[...]
        start1(TP, TM, TY)

    def t_0():
        arrive1(TM)
        start1(TF2)
        arrive1(TY)
        start1(UP, UM)
        arrive1(TP)
        start1(TF1)

    def t_2():
        arrive1(UP)
        start1(UF1)
        arrive1(UM)
        start1(UF2)

    def t_4():
        arrive1(UF1, UF2)

    def t_6():
        arrive1(TF1, TF2)

    def p0(t):
        start(t, XIN)

    def s0(t):
        arrive(t, XIN)
        c = tok(t)
        x_t = xin[c]
        xt[t] = x_t[:, 0:512].T
        pltpu.make_async_copy(xt.at[t], xt_ref.at[:, tokens(c)], osem.at[1]).start()
        r0(gu, t, [jnp.dot(x_t, w[...], preferred_element_type=F32) for w in (wg, wu)])

    def activate(c, full, hgrad, cols):
        gate, up = full[0], full[1]
        sigma = jax.nn.sigmoid(gate)
        act[c, x, y, 0, :, cols] = (gate * sigma * up).astype(BF)
        act[c, x, y, 1, :, cols] = (hgrad * up * sigma * (1.0 + gate * (1.0 - sigma))).astype(BF)
        act[c, x, y, 2, :, cols] = (hgrad * gate * sigma).astype(BF)

    def s3(t):
        c = tok(t)
        activate(c, r3x(gu, t), hfx[c], cx)
        start(t, AXY)
        activate(c, r3y(gu, t), hfy[c], cy)
        start(t, AYP, AYM)

        @pl.when(t == 7)
        def _():
            start1(AYL)

    def s4(t):
        arrive(t, AXY)
        start(t, AXP, AXM)

        @pl.when(t == 7)
        def _():
            start1(AXL)

        arrive(t, AYP)

        @pl.when(t < 7)
        def _():
            start(t, AYF)

        arrive(t, AYM)

        @pl.when(t == 7)
        def _():
            arrive1(AYL)
            start(t, AYY)

    def s5(t):
        arrive(t, AXP)

        @pl.when(t < 7)
        def _():
            start(t, AXF)

        arrive(t, AXM)

        @pl.when(t < 7)
        def _():
            arrive(t, AYF)
            start(t, AYY)

        @pl.when(t == 7)
        def _():
            arrive1(AXL)
            arrive(t, AYY)
            start(t, CORE)

    def s6(t):
        @pl.when(t < 7)
        def _():
            arrive(t, AXF, AYY)
            start(t, CORE)

        @pl.when(t == 7)
        def _():
            project(t)

    def s7(t):
        @pl.when(t < 7)
        def _():
            project(t)

    def project(t):
        c = tok(t)
        arrive(t, CORE)
        pltpu.make_async_copy(act.at[c, :, :, 1:3], o_ref.at[c], osem.at[0]).start()
        hidden = act[c, :, :, 0].reshape(128, 2 * HALF)
        lo[t] = jnp.dot(hidden, wdo[...], preferred_element_type=F32)

        @pl.when((t != 1) & (t < 6))
        def _():
            start(t, LOZ)

        @pl.when(t == 6)
        def _():
            lo6[...] = lo[6].astype(BF)
            start1(LO6)

        ht[t] = hidden.T
        pltpu.make_async_copy(ht.at[t], ht_ref.at[:, tokens(c)], osem.at[2]).start()

    def s8(t):
        @pl.when(t == 4)
        def _():
            arrive(2, LOZ)
            arrive(3, LOZ)
            arrive(4, LOZ)
            zs[...] = lo[1] + rz[2] + rz[3] + rz[4]
            start1(LOY)

    def spread(i, carry):
        to = rem(row + i, 16)
        pltpu.make_async_remote_copy(
            src_ref=v_ref.at[:, pl.ds(pl.multiple_of(to * 512, 512), 512)],
            dst_ref=pool.at[row],
            send_sem=asem.at[0], recv_sem=asem.at[1], device_id={"row": to}, device_id_type=MESH,
        ).start()
        return carry

    def spread_all():
        return pltpu.make_async_remote_copy(
            src_ref=pool.at[0:15], dst_ref=pool.at[0:15], send_sem=asem.at[0], recv_sem=asem.at[1],
            device_id=y_dev, device_id_type=MESH,
        )

    def c_0():
        arrive1(CM)
        start1(CF2)
        arrive1(CP)
        start1(CF1)
        start(1, CIN)
        start(2, CIN)

    def c_1():
        arrive1(CY)
        start(3, CIN)
        arrive1(CF1, CF2)
        start(4, CIN)

    def c_2():
        start1(DP, DM)

    def c_3():
        arrive1(DM)
        start1(DF2)
        arrive1(DP)
        start1(DF1)
        start(5, CIN)
        start(6, CIN)

    def c_4():
        arrive1(DF1, DF2)
        start(7, CIN)
        pltpu.make_async_copy(c2.at[:, :, 0:512], co_ref, lsem.at[4]).start()

    def w_0():
        here[0].wait()
        arrive1(WD)
        start1(WG, WU)

    def w_1():
        here[1].wait()
        here[2].wait()
        here[3].wait()
        arrive1(WG, WU)

    start(0, CIN)
    lax.fori_loop(1, 16, spread, 0)
    start1(WD, CP, CM, CY)
    find_places()
    for c in here[1:]:
        c.start()

    def each(n, lag, stage):
        t = n - lag

        @pl.when((t >= 0) & (t < CHUNKS))
        def _():
            stage(t)

    def at(n, when, stage):
        @pl.when(n == when)
        def _():
            stage()

    def step(n, carry):
        at(n, 0, w_0)
        for lag, stage in enumerate([h0, lambda u: r1(hg, u), lambda u: r2(hg, u), h3]):
            q = n - lag
            m = jnp.where(q == 3, -1, jnp.where(q > 3, q - 1, q))
            each(2 * m - 1, 0, stage)
            each(2 * m, 0, stage)
        at(n, 0, c_0)
        at(n, 1, c_1)
        at(n, 0, v_0)
        at(n, 2, v_2)
        at(n, 2, c_2)
        at(n, 3, v_3)
        at(n, 3, c_3)
        at(n, 4, c_4)
        at(n, FIRST, t_0)
        at(n, FIRST + 2, t_2)
        at(n, FIRST + 4, t_4)
        at(n, FIRST + 6, t_6)
        at(n, FIRST + 1, w_1)
        for lag, stage in [
            (0, p0), (1, s0), (2, lambda t: r1(gu, t)), (4, lambda t: r2(gu, t)), (6, s3), (7, s4), (8, s5),
            (10, s7), (9, s6), (11, s8),
        ]:
            each(n, FIRST + lag, stage)
        return carry

    lax.fori_loop(0, FIRST + CHUNKS + 9, step, 0)
    arrive(0, LOZ)
    arrive(5, LOZ)
    arrive1(LOY)
    arrive1(LO6)
    out_ref[...] = (lo[7] + rz[0] + rz[5] + rz6[...].astype(F32) + rh[...]).astype(BF)

    def all_sent(kind):
        if kind < 16:
            r = gu if kind < HG else hg
            return (r.sxd, r.sxr, r.sx2, r.sxy, r.syy, r.syd, r.syr, r.sy2)[kind % HG]
        if kind in (AXP, AXM, AXF):
            return act.at[0:7 if kind == AXF else 8, x, :, :, :, cx]
        if kind in (AYP, AYM, AYF):
            return act.at[0:7 if kind == AYF else 8, x, y, :, :, cy]
        return {
            AXY: lambda: act.at[:, x, y, :, :, cx], AYY: lambda: act.at[:, :, y, :, :, cy],
            CORE: lambda: act.at[:, :, :, :, :, mine], XIN: lambda: xin.at[:, :, 0:512],
            CIN: lambda: c2.at[:, :, 0:512], LOZ: lambda: lo.at[0:5],
        }[kind]()

    for kind in range(KINDS):
        ref = all_sent(kind)
        copy(kind, 0, ref, ref, y_dev).wait_send()
    for kind in range(ONCE):
        src, dst, dev, _ = single[kind]()
        once(kind, src, dst, dev).wait_send()
    spread_all().wait_send()
    pltpu.make_async_copy(act.at[:, :, :, 1:3], o_ref, osem.at[0]).wait()
    pltpu.make_async_copy(xt, xt, osem.at[1]).wait()
    pltpu.make_async_copy(ht, ht, osem.at[2]).wait()
    pltpu.make_async_copy(c2.at[:, :, 0:512], co_ref, lsem.at[4]).wait()


def main_call(v, counts, owner, og, gate, up, down):
    n = CHUNKS
    vm = lambda *s: pltpu.VMEM(s, BF)
    vf = lambda *s: pltpu.VMEM(s, F32)

    def row_sum(mats):
        xb, xq, yb = (n, mats, 32, XW), (n, mats, 16, XW), (n, mats, 16, YW)
        moves = [vm(*xb), vm(*xb), vm(*xb), vm(*xq), vm(n, 4, mats, 16, YW), vm(*yb), vm(*yb), vm(*yb)]
        return [vf(8, 4, mats, 32, XW), vf(8, 2, 4, mats, 16, YW), *moves, *moves]

    dma = pltpu.SemaphoreType.DMA
    vmem = pl.BlockSpec(memory_space=pltpu.VMEM)
    hbm = pl.BlockSpec(memory_space=pl.ANY)
    return pl.pallas_call(
        main_kernel,
        out_shape=(
            jax.ShapeDtypeStruct((128, 512), BF),
            jax.ShapeDtypeStruct((n, 4, 2, 2, 16, 2 * HALF), BF),
            jax.ShapeDtypeStruct((2 * HALF, 1024), BF),
            jax.ShapeDtypeStruct((512, 1024), BF),
            jax.ShapeDtypeStruct((n, 128, 512), BF),
        ),
        in_specs=[vmem, vmem, vmem, vmem, hbm, hbm, hbm],
        out_specs=(vmem, hbm, hbm, hbm, hbm),
        scratch_shapes=[
            vm(n, 4, 2, 3, 16, 2 * HALF), vm(16, 16, 512), vm(n, 128, 1024), vm(n, 128, 1024),
            vm(1024, HALF), vm(1024, HALF), vm(HALF, 1024), vm(2 * HALF, 512),
            vm(8, 128, 256), vm(2, 4, 128, 512), vm(3, 2, 128, 256), vm(4, 128, 256), vm(128, 256), vm(3, 128, 256), vm(128, 256),
            vm(n, 2 * HALF, 128), vm(n, 512, 128),
            vf(n, 16, XW), vf(n, 16, YW),
            vf(n, 128, 512), vf(n, 128, 512), vf(128, 512), vf(128, 512), vm(128, 512), vm(128, 512),
            *row_sum(2), *row_sum(1),
            dma((KINDS,)), dma((10, SLOTS)), dma((19, n)), dma((ONCE,)), dma((ONCE,)), dma((2,)),
            dma((3,)), dma((5,)),
        ],
        compiler_params=pltpu.CompilerParams(
            collective_id=0, has_side_effects=True, vmem_limit_bytes=60 << 20
        ),
        cost_estimate=pl.CostEstimate(flops=10**10, bytes_accessed=30 * 10**6, transcendentals=0),
        name="row_sums",
    )(v, counts, owner, og, gate, up, down)


def grads_kernel(xt_hbm, c_hbm, ht_hbm, o_hbm, y_hbm, gate_hbm, up_hbm, down_hbm, out_hbm, xt, c, ht, o, gate, up, down, lsem, wsem):
    load = pltpu.make_async_copy
    strips = [slice(0, HALF), slice(HALF, 2 * HALF)]
    quarters = [slice(i * HALF // 2, (i + 1) * HALF // 2) for i in range(4)]
    x_in, c_in = load(xt_hbm, xt, lsem.at[0]), load(c_hbm, c, lsem.at[1])
    ht_in = [load(ht_hbm.at[s], ht.at[s], lsem.at[2 + i]) for i, s in enumerate(quarters)]
    o_in = [
        [load(o_hbm.at[:, :, :, m, :, s], o.at[:, :, :, m, :, s], lsem.at[6 + 2 * i + m]) for m in range(2)]
        for i, s in enumerate(strips)
    ]
    c_in.start()
    ht_in[0].start()
    ht_in[1].start()
    x_in.start()
    for copies in (o_in[0], ht_in[2:], o_in[1]):
        for copy in copies:
            copy.start()
    out = []

    def write(src, dst):
        out.append(pltpu.make_async_copy(src, dst, wsem.at[len(out)]))
        out[-1].start()

    write(y_hbm, out_hbm)
    c_in.wait()
    for i, s in enumerate(strips):
        for q in (2 * i, 2 * i + 1):
            ht_in[q].wait()
            down[quarters[q]] = jnp.dot(ht[quarters[q]], c[...].reshape(1024, 512), preferred_element_type=F32)
            write(down.at[quarters[q]], down_hbm.at[quarters[q]])
        if i == 0:
            x_in.wait()
        for m, (grad, hbm) in enumerate(((gate, gate_hbm), (up, up_hbm))):
            o_in[i][m].wait()
            rows = [slice(0, 512)] if i + m < 2 else [slice(0, 256), slice(256, 512)]
            for r in rows:
                grad[r, s] = jnp.dot(xt[r], o[:, :, :, m, :, s].reshape(1024, HALF), preferred_element_type=F32)
                write(grad.at[r, s], hbm.at[r, s])
    for copy in out:
        copy.wait()


def grads_call(xt, c, ht, o, y):
    hbm = pl.BlockSpec(memory_space=pl.ANY)
    up, down = (512, 2 * HALF), (2 * HALF, 512)
    return pl.pallas_call(
        grads_kernel,
        out_shape=(
            *(jax.ShapeDtypeStruct(shape, F32) for shape in (up, up, down)),
            jax.ShapeDtypeStruct(y.shape, y.dtype),
        ),
        in_specs=[hbm] * 5,
        out_specs=(hbm, hbm, hbm, hbm),
        scratch_shapes=[
            *(pltpu.VMEM(a.shape, BF) for a in (xt, c, ht, o)),
            *(pltpu.VMEM(shape, F32) for shape in (up, up, down)),
            pltpu.SemaphoreType.DMA((10,)), pltpu.SemaphoreType.DMA((10,)),
        ],
        compiler_params=pltpu.CompilerParams(vmem_limit_bytes=60 << 20),
        cost_estimate=pl.CostEstimate(flops=8 * 10**9, bytes_accessed=24 * 10**6, transcendentals=0),
        name="weight_grads",
    )(xt, c, ht, o, y)


def local(vision_tokens, image_counts, image_owner, gate_weight, up_weight, down_weight, out_grad):
    y, o, ht, xt, c = main_call(
        vision_tokens, image_counts[None, :], image_owner[None, :], out_grad, gate_weight, up_weight, down_weight
    )
    grad_gate, grad_up, grad_down, layer_out = grads_call(xt, c, ht, o, y)
    return (layer_out, grad_gate, grad_up, grad_down)


def solution(mesh):
    in_specs = (
        P(("row", "col"), None),
        P(),
        P(),
        P("row", "col"),
        P("row", "col"),
        P("col", "row"),
        P("col", "row"),
    )
    out_specs = (P("col", "row"), P("row", "col"), P("row", "col"), P("col", "row"))
    return jax.shard_map(local, mesh=mesh, in_specs=in_specs, out_specs=out_specs, check_vma=False)
```
